512 devices in a mesh: row: 16 (over y, core), col: 32 (over z, x).
Axes of the slice: x: 4, y: 8, z: 8, core: 2. Of those that a mesh axis runs over, the one named last changes fastest.
Arguments:
- root_inverse: float32 [8192, 8192], P('row', 'col'), may hold values from -6 to 6
- boundary_map: int32 [4096], replicated, may hold values from 2 to 8191, as said below
- lower_factor: float32 [4096, 4096], P('row', 'col'), may hold values from -0.09375 to 0.09375
- upper_factor: float32 [4096, 4096], P('row', 'col'), may hold values from -0.09375 to 0.09375
- diagonal_inverse: float32 [4096, 4096], P('row', 'col'), may hold values from -6 to 6
Outputs:
- sigma_bs: float32 [4096, 4096], P('row', 'col')
- sigma_sb: float32 [4096, 4096], P('row', 'col')
- sigma_ss: float32 [4096, 4096], P('row', 'col')
The draws below stay inside these ranges and needn't reach their ends.
Inputs may be any that keep to these rules, and one draw needn't show every extreme that they name: `boundary_map`: root unknowns come four to a lattice site (two spin components, real and imaginary part each), site s holding indices 4 s to 4 s + 3. The child's boundary is the projected half-spinor of every root site: entries 2 q and 2 q + 1 are the real and imaginary unknown of the second spin component of one site, 4 s + 2 and 4 s + 3. Entry p lies in [256 * (p // 128), 256 * (p // 128 + 1)); each root site appears once, in the child's own order of sites within each block of 256 root indices.
All inputs are finite; a program needn't handle non-finite values.
Results may differ from the reference program's by a relative error of at most 0.000084.
Values sent between devices are 32-bit elements; how exact they have to be, the bound alone decides.
No kernel may reach another device: no remote copies, remote signals or barrier semaphores. Data moves between devices by JAX's collectives and lax.ppermute only.
A program may use at most 64 MiB of HBM per device.

```python
import jax
import jax.numpy as jnp
from jax import lax

PANEL = 256
ROOT = 8192
BOUND = 4096
SEP = 4096


def site_order(order_key):
    return jax.random.permutation(order_key, PANEL // 4).astype(jnp.int32)


def draw_boundary_map(key, part):
    key = jax.random.fold_in(key, 11)
    blocks = ROOT // PANEL
    order_keys = jax.random.split(jax.random.fold_in(key, 1), blocks)
    orders = jax.vmap(site_order)(order_keys)
    offsets = (jnp.arange(blocks, dtype=jnp.int32) * (PANEL // 4))[:, None]
    site_ids = orders + offsets
    first = 4 * site_ids + 2
    paired = jnp.stack([first, first + 1], axis=-1)
    return paired.reshape(-1).astype(jnp.int32)


def shard_levels(rng, shape, pieces, smallest, top_value):
    def one(axis_at, shards_of):
        steps = jax.random.uniform(jax.random.fold_in(jax.random.fold_in(rng, 6), axis_at), (shards_of,), jnp.float32, smallest / len(pieces), top_value / len(pieces))
        return jnp.repeat(jnp.exp(steps), shape[axis_at] // shards_of).reshape((-1,) + (1,) * (len(shape) - axis_at - 1))

    level = one(*pieces[0])
    for cut in pieces[1:]:
        level = level * one(*cut)
    return level


def gaussian(own_key, extent, width, most, cuts=(), held_as=jnp.bfloat16):
    level = shard_levels(own_key, extent, cuts, -0.22, 0.18) if cuts else 1.0
    drawn = jax.random.normal(own_key, extent, jnp.float32) * width * level
    return jnp.minimum(jnp.maximum(drawn, -most), most).astype(held_as)


def setup_inputs(seed: int = 0) -> dict:
    arg_keys = jax.random.split(jax.random.key(seed), 6)
    root_inverse = gaussian(arg_keys[0], (ROOT, ROOT), 1.0, 6.0, ((0, 16), (1, 32)), jnp.float32)
    boundary_map = draw_boundary_map(jax.random.fold_in(arg_keys[5], 71), 0)
    lower_factor = gaussian(arg_keys[2], (BOUND, SEP), BOUND ** -0.5, 0.09375, ((0, 16), (1, 32)), jnp.float32)
    upper_factor = gaussian(arg_keys[3], (SEP, BOUND), BOUND ** -0.5, 0.09375, ((0, 16), (1, 32)), jnp.float32)
    diagonal_inverse = gaussian(arg_keys[4], (SEP, SEP), 1.0, 6.0, ((0, 16), (1, 32)), jnp.float32)
    return {"root_inverse": root_inverse, "boundary_map": boundary_map, "lower_factor": lower_factor, "upper_factor": upper_factor, "diagonal_inverse": diagonal_inverse}


def reference(root_inverse, boundary_map, lower_factor, upper_factor, diagonal_inverse):
    picked = jnp.take(root_inverse, boundary_map.astype(jnp.int32), axis=0)
    sigma_bb = jnp.take(picked, boundary_map.astype(jnp.int32), axis=1)
    sigma_bs = -jnp.dot(sigma_bb, lower_factor, preferred_element_type=jnp.float32, precision=lax.Precision.HIGHEST)
    sigma_sb = -jnp.dot(upper_factor, sigma_bb, preferred_element_type=jnp.float32, precision=lax.Precision.HIGHEST)
    sigma_ss = diagonal_inverse - jnp.dot(upper_factor, sigma_bs, preferred_element_type=jnp.float32, precision=lax.Precision.HIGHEST)
    return sigma_bs, sigma_sb, sigma_ss
```

```python
import jax
import jax.numpy as jnp
import numpy as np
from jax import lax
from jax.experimental import pallas as pl
from jax.experimental.pallas import tpu as pltpu
from jax.sharding import Mesh, PartitionSpec as P

F32 = jnp.float32
BF16 = jnp.bfloat16
VMEM = pl.BlockSpec(memory_space=pltpu.VMEM)
PARAMS = pltpu.CompilerParams(vmem_limit_bytes=40 * 1024 * 1024)


def split2(v):
    hi = v.astype(BF16)
    return hi, (v - hi.astype(F32)).astype(BF16)


def dot(a, b):
    return lax.dot_general(a, b, (((1,), (0,)), ((), ())), preferred_element_type=F32)


def pick_kernel(rows_ref, cols_ref, root_ref, lower_ref, upper_ref, su_ref, send_ref):
    iota = lax.broadcasted_iota(jnp.int32, (256, 128), 0)
    col_hot = jnp.where(cols_ref[...] == iota, 1.0, 0.0).astype(BF16)
    for part in range(2):
        row_hot = jnp.where(rows_ref[part : part + 1, :] == iota, 1.0, 0.0).astype(BF16)
        left = root_ref[256 * part : 256 * (part + 1), :]
        picked = None
        for _ in range(3):
            piece = left.astype(BF16)
            left = left - piece.astype(F32)
            across = lax.dot_general(
                row_hot, piece, (((0,), (0,)), ((), ())), preferred_element_type=F32
            )
            value = dot(across.astype(BF16), col_hot)
            picked = value if picked is None else picked + value
        su_ref[128 * part : 128 * (part + 1), :] = picked
        for core in range(2):
            send_ref[core, part, 0] = picked[64 * core : 64 * (core + 1), :]
            start = 128 * part + 64 * core
            send_ref[core, part, 1] = lower_ref[start : start + 64, :]
    su_ref[256:512, :] = upper_ref[...]


def pick(rows, cols, root, lower, upper):
    return pl.pallas_call(
        pick_kernel,
        out_shape=(
            jax.ShapeDtypeStruct((512, 128), F32),
            jax.ShapeDtypeStruct((2, 2, 2, 64, 128), F32),
        ),
        in_specs=[VMEM] * 5,
        out_specs=(VMEM, VMEM),
        compiler_params=PARAMS,
    )(rows, cols, root, lower, upper)


def three_pass(ah, al, bh, bl):
    return dot(ah[...], bh) + (dot(ah[...], bl) + dot(al[...], bh))


def coupling_kernel(core_ref, su_ref, own_ref, other_ref, out_ref, ah, al, bh, bl):
    core = core_ref[0]
    for z in range(8):
        hi, lo = split2(su_ref[z, 256:512, :])
        ah[:, 128 * z : 128 * (z + 1)] = hi
        al[:, 128 * z : 128 * (z + 1)] = lo
        first = pl.multiple_of(128 * z + 64 * core, 64)
        second = pl.multiple_of(128 * z + 64 * (1 - core), 64)
        for x in range(4):
            hi, lo = split2(own_ref[z, x])
            bh[pl.ds(first, 64), 128 * x : 128 * (x + 1)] = hi
            bl[pl.ds(first, 64), 128 * x : 128 * (x + 1)] = lo
            hi, lo = split2(other_ref[z, x])
            bh[pl.ds(second, 64), 128 * x : 128 * (x + 1)] = hi
            bl[pl.ds(second, 64), 128 * x : 128 * (x + 1)] = lo
    for n in range(2):
        cols = slice(256 * n, 256 * (n + 1))
        part = three_pass(ah, al, bh[:, cols], bl[:, cols])
        out_ref[2 * n] = part[:, :128]
        out_ref[2 * n + 1] = part[:, 128:]


def couple(core, gathered, own, other):
    return pl.pallas_call(
        coupling_kernel,
        out_shape=jax.ShapeDtypeStruct((4, 256, 128), F32),
        in_specs=[pl.BlockSpec(memory_space=pltpu.SMEM)] + [VMEM] * 3,
        out_specs=VMEM,
        scratch_shapes=[
            pltpu.VMEM((256, 1024), BF16),
            pltpu.VMEM((256, 1024), BF16),
            pltpu.VMEM((1024, 512), BF16),
            pltpu.VMEM((1024, 512), BF16),
        ],
        compiler_params=PARAMS,
    )(core, gathered, own, other)


def pair_kernel(su_ref, w_ref, lower_ref, out_ref, ah, al, bh, bl):
    for z in range(8):
        cols = slice(128 * z, 128 * (z + 1))
        ah[:256, cols], al[:256, cols] = split2(su_ref[z, :256, :])
        ah[256:, cols], al[256:, cols] = split2(w_ref[z])
        for core in range(2):
            start = 128 * z + 64 * core
            for x in range(4):
                hi, lo = split2(lower_ref[z, core, x])
                bh[start : start + 64, 128 * x : 128 * (x + 1)] = hi
                bl[start : start + 64, 128 * x : 128 * (x + 1)] = lo
    for n in range(2):
        cols = slice(256 * n, 256 * (n + 1))
        part = three_pass(ah, al, bh[:, cols], bl[:, cols])
        for i in range(2):
            for k in range(2):
                out_ref[2 * n + i, k] = part[256 * k : 256 * (k + 1), 128 * i : 128 * (i + 1)]


def pair(gathered, w, lower):
    return pl.pallas_call(
        pair_kernel,
        out_shape=jax.ShapeDtypeStruct((4, 2, 256, 128), F32),
        in_specs=[VMEM] * 3,
        out_specs=VMEM,
        scratch_shapes=[
            pltpu.VMEM((512, 1024), BF16),
            pltpu.VMEM((512, 1024), BF16),
            pltpu.VMEM((1024, 512), BF16),
            pltpu.VMEM((1024, 512), BF16),
        ],
        compiler_params=PARAMS,
    )(gathered, w, lower)


def exchange(v, axis):
    return lax.all_to_all(v, axis, 0, 0, tiled=True)


def spread(v, axis, count):
    return exchange(jnp.broadcast_to(v[None], (count,) + v.shape), axis)


def shards(root_inverse, boundary_map, lower_factor, upper_factor, diagonal_inverse):
    y, c, z, x = (lax.axis_index(name) for name in ("y", "c", "z", "x"))
    blocks = boundary_map.reshape(32, 128)
    row, col = 2 * y + c, 4 * z + x
    rows = lax.dynamic_slice_in_dim(blocks, 2 * row, 2) - 256 * (
        2 * row + jnp.arange(2, dtype=jnp.int32)[:, None]
    )
    cols = lax.dynamic_slice_in_dim(blocks, col, 1) - 256 * col
    su, send = pick(rows, cols, root_inverse, lower_factor, upper_factor)
    gathered = lax.all_gather(su, "z", axis=0, tiled=False)
    moved = exchange(send, "c").reshape(4, 2, 64, 128)
    moved = exchange(moved, "x")
    lower_all = lax.all_gather(moved[:, 1].reshape(256, 128), ("y", "c"), axis=0, tiled=True)
    lower_all = lower_all.reshape(8, 2, 4, 64, 128)
    own = spread(moved[:, 0], "y", 8)
    other = lax.ppermute(own, "c", [(0, 1), (1, 0)])
    part = couple(c.astype(jnp.int32).reshape(1), gathered, own, other)
    w = exchange(part, "x").sum(axis=0)
    w_all = spread(w, "z", 8)
    both = exchange(pair(gathered, w_all, lower_all), "x").sum(axis=0)
    return (-both[0], -w, diagonal_inverse + both[1])


def solution(mesh):
    grid = Mesh(np.asarray(mesh.devices).reshape(8, 2, 8, 4), ("y", "c", "z", "x"))
    block = P(("y", "c"), ("z", "x"))
    return jax.shard_map(
        shards,
        mesh=grid,
        in_specs=(block, P(), block, block, block),
        out_specs=(block, block, block),
        check_vma=False,
    )
```

```python
import jax
import jax.numpy as jnp
import numpy as np
from jax import lax
from jax.experimental import pallas as pl
from jax.experimental.pallas import tpu as pltpu
from jax.sharding import Mesh, PartitionSpec as P

F32 = jnp.float32
BF16 = jnp.bfloat16
VMEM = pl.BlockSpec(memory_space=pltpu.VMEM)
SMEM = pl.BlockSpec(memory_space=pltpu.SMEM)
HBM = pl.BlockSpec(memory_space=pltpu.HBM)
PARAMS = pltpu.CompilerParams(vmem_limit_bytes=32 * 1024 * 1024)
DMA = pltpu.SemaphoreType.DMA


def shape(*dims, dtype=F32):
    return jax.ShapeDtypeStruct(dims, dtype)


def split2(v):
    hi = v.astype(BF16)
    return hi, (v - hi.astype(F32)).astype(BF16)


def dot(a, b):
    return lax.dot_general(a, b, (((1,), (0,)), ((), ())), preferred_element_type=F32)


def three_pass(ah, al, bh, bl):
    return dot(ah, bh) + (dot(ah, bl) + dot(al, bh))


def pick_kernel(
    at_ref, map_hbm, root_hbm, lower_hbm, upper_hbm, su_ref, first_ref, second_ref, picks, root, lower, sems
):
    loads = [
        pltpu.make_async_copy(map_hbm, picks, sems.at[0]),
        pltpu.make_async_copy(root_hbm, root, sems.at[1]),
        pltpu.make_async_copy(lower_hbm, lower, sems.at[2]),
        pltpu.make_async_copy(upper_hbm, su_ref.at[256:512], sems.at[3]),
    ]
    for load in loads:
        load.start()
    row, col, odd = at_ref[0], at_ref[1], at_ref[3]
    iota = lax.broadcasted_iota(jnp.int32, (256, 128), 0)
    loads[0].wait()
    cols = picks[pl.ds(col, 1), :] - 256 * col
    col_hot = jnp.where(cols == iota, 1.0, 0.0).astype(BF16)
    hots = []
    for part in range(2):
        block = 2 * row + part
        rows = picks[pl.ds(block, 1), :] - 256 * block
        hots.append(jnp.where(rows == iota, 1.0, 0.0).astype(BF16))
    loads[1].wait()
    for part in range(2):
        left = root[256 * part : 256 * (part + 1), :]
        picked = None
        for _ in range(3):
            piece = left.astype(BF16)
            left = left - piece.astype(F32)
            across = lax.dot_general(
                hots[part], piece, (((0,), (0,)), ((), ())), preferred_element_type=F32
            )
            value = dot(across.astype(BF16), col_hot)
            picked = value if picked is None else picked + value
        su_ref[128 * part : 128 * (part + 1), :] = picked
    for load in loads[2:]:
        load.wait()
    near = pl.multiple_of(128 * odd, 128)
    far = pl.multiple_of(128 - 128 * odd, 128)
    first_ref[0] = su_ref[pl.ds(near, 128), :]
    first_ref[1] = lower[pl.ds(near, 128), :]
    second_ref[0] = su_ref[pl.ds(far, 128), :]
    second_ref[1] = lower[pl.ds(far, 128), :]


def pick(at, blocks, root, lower, upper):
    return pl.pallas_call(
        pick_kernel,
        out_shape=(shape(512, 128), shape(2, 128, 128), shape(2, 128, 128)),
        in_specs=[SMEM] + [HBM] * 4,
        out_specs=(VMEM, VMEM, VMEM),
        scratch_shapes=[
            pltpu.VMEM((32, 128), jnp.int32),
            pltpu.VMEM((512, 256), F32),
            pltpu.VMEM((256, 128), F32),
            DMA((4,)),
        ],
        compiler_params=pltpu.CompilerParams(vmem_limit_bytes=62 * 1024 * 1024),
    )(at, blocks, root, lower, upper)


def fan_kernel(first_ref, second_ref, copies_ref, lower_ref):
    for t, ref in enumerate((first_ref, second_ref)):
        lower_ref[128 * t : 128 * (t + 1), :] = ref[1]
        value = ref[0]
        for i in range(8):
            copies_ref[i, t] = value


def fan(first, second):
    return pl.pallas_call(
        fan_kernel,
        out_shape=(shape(8, 2, 128, 128), shape(256, 128)),
        in_specs=[VMEM] * 2,
        out_specs=(VMEM, VMEM),
        compiler_params=PARAMS,
    )(first, second)


def couple(at, gathered, columns, before=None):
    def kernel(at_ref, su_hbm, columns_ref, *refs):
        before_ref, (out_ref, upper, ah, al, bh, bl, sem) = (
            (None, refs) if before is None else (refs[0], refs[1:])
        )
        load = pltpu.make_async_copy(su_hbm.at[:, 256:512], upper, sem)
        load.start()
        for z in range(8):
            rows = slice(128 * z, 128 * (z + 1))
            for t in range(2):
                cols = slice(128 * t, 128 * (t + 1))
                bh[rows, cols], bl[rows, cols] = split2(columns_ref[z, t])
        load.wait()
        for z in range(8):
            rows = slice(128 * z, 128 * (z + 1))
            ah[:, rows], al[:, rows] = split2(upper[z])
        part = three_pass(ah[...], al[...], bh[...], bl[...])
        if before is None:
            out_ref[0] = part[:, :128]
            out_ref[1] = part[:, 128:]
        else:
            core, odd = at_ref[2], at_ref[3]
            out_ref[2 * core + odd] = before_ref[0]
            out_ref[2 * core + 1 - odd] = before_ref[1]
            out_ref[2 * (1 - core) + odd] = part[:, :128]
            out_ref[2 * (1 - core) + 1 - odd] = part[:, 128:]

    more = () if before is None else (before,)
    return pl.pallas_call(
        kernel,
        out_shape=shape(2 + 2 * len(more), 256, 128),
        in_specs=[SMEM, HBM, VMEM] + [VMEM] * len(more),
        out_specs=VMEM,
        scratch_shapes=[
            pltpu.VMEM((8, 256, 128), F32),
            pltpu.VMEM((256, 1024), BF16),
            pltpu.VMEM((256, 1024), BF16),
            pltpu.VMEM((1024, 256), BF16),
            pltpu.VMEM((1024, 256), BF16),
            DMA,
        ],
        compiler_params=PARAMS,
        cost_estimate=pl.CostEstimate(flops=3 << 28, bytes_accessed=3 << 20, transcendentals=0),
    )(at, gathered, columns, *more)


def lower_columns(odd, lower, bh, bl):
    for z in range(8):
        rows = slice(128 * z, 128 * (z + 1))
        for core in range(2):
            for t in range(2):
                cols = slice(256 * core + 128 * t, 256 * core + 128 * (t + 1))
                place = 128 * jnp.where(odd == 0, t, 1 - t)
                value = lower[2 * z + core, pl.ds(pl.multiple_of(place, 128), 128), :]
                bh[rows, cols], bl[rows, cols] = split2(value)


def side_kernel(at_ref, su_hbm, lower, s0, s1, s2, s3, sigma, ah, al, bh, bl, out, sem):
    load = pltpu.make_async_copy(su_hbm.at[:, 0:256], sigma, sem)
    load.start()
    lower_columns(at_ref[3], lower, bh, bl)
    load.wait()
    for z in range(8):
        rows = slice(128 * z, 128 * (z + 1))
        ah[:, rows], al[:, rows] = split2(sigma[z])
    for n in range(2):
        cols = slice(256 * n, 256 * (n + 1))
        part = three_pass(ah[...], al[...], bh[:, cols], bl[:, cols])
        out[2 * n] = part[:, :128]
        out[2 * n + 1] = part[:, 128:]
    for k, ref in enumerate((s0, s1, s2, s3)):
        ref[...] = out[(at_ref[4] + k) & 3]


def side(at, gathered, lower):
    return pl.pallas_call(
        side_kernel,
        out_shape=(shape(256, 128),) * 4,
        in_specs=[SMEM, HBM, VMEM],
        out_specs=(VMEM,) * 4,
        scratch_shapes=[
            pltpu.VMEM((8, 256, 128), F32),
            pltpu.VMEM((256, 1024), BF16),
            pltpu.VMEM((256, 1024), BF16),
            pltpu.VMEM((1024, 512), BF16),
            pltpu.VMEM((1024, 512), BF16),
            pltpu.VMEM((4, 256, 128), F32),
            DMA,
        ],
        compiler_params=PARAMS,
        cost_estimate=pl.CostEstimate(flops=6 << 28, bytes_accessed=6 << 20, transcendentals=0),
    )(at, gathered, lower)


def last_kernel(at_ref, w_ref, lower, out_ref, ah, al, bh, bl):
    lower_columns(at_ref[3], lower, bh, bl)
    for z in range(8):
        rows = slice(128 * z, 128 * (z + 1))
        ah[:, rows], al[:, rows] = split2(w_ref[z])
    for n in range(2):
        cols = slice(256 * n, 256 * (n + 1))
        part = three_pass(ah[...], al[...], bh[:, cols], bl[:, cols])
        out_ref[2 * n] = part[:, :128]
        out_ref[2 * n + 1] = part[:, 128:]


def last(at, w, lower):
    return pl.pallas_call(
        last_kernel,
        out_shape=shape(4, 256, 128),
        in_specs=[SMEM, VMEM, VMEM],
        out_specs=VMEM,
        scratch_shapes=[
            pltpu.VMEM((256, 1024), BF16),
            pltpu.VMEM((256, 1024), BF16),
            pltpu.VMEM((1024, 512), BF16),
            pltpu.VMEM((1024, 512), BF16),
        ],
        compiler_params=PARAMS,
    )(at, w, lower)


def exchange(v, axis):
    return lax.all_to_all(v, axis, 0, 0, tiled=True)


def deal(v, t):
    moves = [(4 * c + x, 4 * (x >> 1) + 2 * c + ((x & 1) ^ t)) for c in range(2) for x in range(4)]
    return lax.ppermute(v, ("c", "x"), moves)


def shards(root_inverse, boundary_map, lower_factor, upper_factor, diagonal_inverse):
    y, c, z, x = (lax.axis_index(name) for name in ("y", "c", "z", "x"))
    at = jnp.stack([2 * y + c, 4 * z + x, c, x & 1, x]).astype(jnp.int32)
    su, first, second = pick(
        at, boundary_map.reshape(32, 128), root_inverse, lower_factor, upper_factor
    )
    gathered = lax.all_gather(su, "z", axis=0, tiled=False)
    copies, lower = fan(deal(first, 0), deal(second, 1))
    lower = lax.all_gather(lower, ("y", "c"), axis=0, tiled=False)
    own = exchange(copies, "y")
    other = lax.ppermute(own, "c", [(0, 1), (1, 0)])
    part = couple(at, gathered, other, couple(at, gathered, own))
    w = exchange(part, "x").sum(axis=0)
    w_all = exchange(jnp.broadcast_to(w[None], (8, 256, 128)), "z")
    pieces = side(at, gathered, lower)
    total = pieces[0]
    for k in range(1, 4):
        total = total + lax.ppermute(pieces[k], "x", [(i, (i + k) & 3) for i in range(4)])
    total, w_all = lax.optimization_barrier((-total, w_all))
    product = exchange(last(at, w_all, lower), "x").sum(axis=0)
    return (total, -w, diagonal_inverse + product)


def solution(mesh):
    grid = Mesh(np.asarray(mesh.devices).reshape(8, 2, 8, 4), ("y", "c", "z", "x"))
    block = P(("y", "c"), ("z", "x"))
    return jax.shard_map(
        shards,
        mesh=grid,
        in_specs=(block, P(), block, block, block),
        out_specs=(block, block, block),
        check_vma=False,
    )
```

```python
import jax
import jax.numpy as jnp
import numpy as np
from jax import lax
from jax.experimental import pallas as pl
from jax.experimental.pallas import tpu as pltpu
from jax.sharding import Mesh, PartitionSpec as P

F32 = jnp.float32
BF16 = jnp.bfloat16
VMEM = pl.BlockSpec(memory_space=pltpu.VMEM)
SMEM = pl.BlockSpec(memory_space=pltpu.SMEM)
HBM = pl.BlockSpec(memory_space=pltpu.HBM)
PARAMS = pltpu.CompilerParams(vmem_limit_bytes=32 * 1024 * 1024)
WIDE = pltpu.CompilerParams(vmem_limit_bytes=62 * 1024 * 1024)
MIDDLE = pltpu.CompilerParams(vmem_limit_bytes=52 * 1024 * 1024)
DMA = pltpu.SemaphoreType.DMA


def shape(*dims, dtype=F32):
    return jax.ShapeDtypeStruct(dims, dtype)


def split2(v):
    hi = v.astype(BF16)
    return hi, (v - hi.astype(F32)).astype(BF16)


def dot(a, b):
    return lax.dot_general(a, b, (((1,), (0,)), ((), ())), preferred_element_type=F32)


def three_pass(ah, al, bh, bl):
    return dot(ah, bh) + (dot(ah, bl) + dot(al, bh))


def device(ref):
    number = ref[0]
    return number >> 5, number & 31, (number >> 5) & 1, (number >> 2) & 7, number & 3


def pick_kernel(
    at_ref, map_hbm, root_hbm, lower_hbm, sigma_ref, first_ref, second_ref, picks, root, lower, sems
):
    loads = [
        pltpu.make_async_copy(map_hbm, picks, sems.at[0]),
        pltpu.make_async_copy(root_hbm, root, sems.at[1]),
        pltpu.make_async_copy(lower_hbm, lower, sems.at[2]),
    ]
    for load in loads:
        load.start()
    row, col, _, _, x = device(at_ref)
    odd = x & 1
    iota = lax.broadcasted_iota(jnp.int32, (256, 128), 0)
    loads[0].wait()
    cols = picks[pl.ds(col, 1), :] - 256 * col
    col_hot = jnp.where(cols == iota, 1.0, 0.0).astype(BF16)
    hots = []
    for part in range(2):
        block = 2 * row + part
        rows = picks[pl.ds(block, 1), :] - 256 * block
        hots.append(jnp.where(rows == iota, 1.0, 0.0).astype(BF16))
    loads[1].wait()
    stack = []
    for part in range(2):
        left = root[256 * part : 256 * (part + 1), :]
        pieces = []
        for _ in range(3):
            piece = left.astype(BF16)
            left = left - piece.astype(F32)
            pieces.append(piece)
        across = lax.dot_general(
            hots[part],
            jnp.concatenate(pieces, axis=1),
            (((0,), (0,)), ((), ())),
            preferred_element_type=F32,
        ).astype(BF16)
        stack += [across[:, 256 * i : 256 * (i + 1)] for i in range(3)]
    value = dot(jnp.concatenate(stack, axis=0), col_hot)
    for part in range(2):
        v = [value[128 * (3 * part + i) : 128 * (3 * part + i + 1), :] for i in range(3)]
        sigma_ref[128 * part : 128 * (part + 1), :] = (v[0] + v[1]) + v[2]
    loads[2].wait()
    near = pl.multiple_of(128 * odd, 128)
    far = pl.multiple_of(128 - 128 * odd, 128)
    first_ref[0] = sigma_ref[pl.ds(near, 128), :]
    first_ref[1] = lower[pl.ds(near, 128), :]
    second_ref[0] = sigma_ref[pl.ds(far, 128), :]
    second_ref[1] = lower[pl.ds(far, 128), :]


def pick(at, blocks, root, lower):
    return pl.pallas_call(
        pick_kernel,
        out_shape=(shape(256, 128), shape(2, 128, 128), shape(2, 128, 128)),
        in_specs=[SMEM] + [HBM] * 3,
        out_specs=(VMEM, VMEM, VMEM),
        scratch_shapes=[
            pltpu.VMEM((32, 128), jnp.int32),
            pltpu.VMEM((512, 256), F32),
            pltpu.VMEM((256, 128), F32),
            DMA((3,)),
        ],
        compiler_params=WIDE,
    )(at, blocks, root, lower)


def fan_kernel(first_ref, second_ref, copies_ref, lower_ref):
    for t, ref in enumerate((first_ref, second_ref)):
        lower_ref[128 * t : 128 * (t + 1), :] = ref[1]
        value = ref[0]
        for i in range(8):
            copies_ref[i, t] = value


def fan(first, second):
    return pl.pallas_call(
        fan_kernel,
        out_shape=(shape(8, 2, 128, 128), shape(256, 128)),
        in_specs=[VMEM] * 2,
        out_specs=(VMEM, VMEM),
        compiler_params=PARAMS,
    )(first, second)


def couple(at, upper, columns, before=None):
    def kernel(at_ref, upper_hbm, columns_hbm, *refs):
        before_ref, (out_ref, left, right, ah, al, bh, bl, sems) = (
            (None, refs) if before is None else (refs[0], refs[1:])
        )
        loads = [
            pltpu.make_async_copy(columns_hbm, right, sems.at[0]),
            pltpu.make_async_copy(upper_hbm, left, sems.at[1]),
        ]
        for load in loads:
            load.start()
        loads[0].wait()
        for z in range(8):
            rows = slice(128 * z, 128 * (z + 1))
            for t in range(2):
                cols = slice(128 * t, 128 * (t + 1))
                bh[rows, cols], bl[rows, cols] = split2(right[z, t])
        loads[1].wait()
        for z in range(8):
            rows = slice(128 * z, 128 * (z + 1))
            ah[:, rows], al[:, rows] = split2(left[z])
        part = three_pass(ah[...], al[...], bh[...], bl[...])
        if before is None:
            out_ref[0] = part[:, :128]
            out_ref[1] = part[:, 128:]
        else:
            _, _, core, _, x = device(at_ref)
            odd = x & 1
            out_ref[2 * core + odd] = before_ref[0]
            out_ref[2 * core + 1 - odd] = before_ref[1]
            out_ref[2 * (1 - core) + odd] = part[:, :128]
            out_ref[2 * (1 - core) + 1 - odd] = part[:, 128:]

    more = () if before is None else (before,)
    return pl.pallas_call(
        kernel,
        out_shape=shape(2 + 2 * len(more), 256, 128),
        in_specs=[SMEM, HBM, HBM] + [VMEM] * len(more),
        out_specs=VMEM,
        scratch_shapes=[
            pltpu.VMEM((8, 256, 128), F32),
            pltpu.VMEM((8, 2, 128, 128), F32),
            pltpu.VMEM((256, 1024), BF16),
            pltpu.VMEM((256, 1024), BF16),
            pltpu.VMEM((1024, 256), BF16),
            pltpu.VMEM((1024, 256), BF16),
            DMA((2,)),
        ],
        compiler_params=PARAMS,
        cost_estimate=pl.CostEstimate(flops=3 << 28, bytes_accessed=3 << 20, transcendentals=0),
    )(at, upper, columns, *more)


def side_kernel(at_ref, lower_hbm, *refs):
    blocks, sums, (bh, bl, lower, ah, al, out, sem) = refs[:8], refs[8:12], refs[12:]
    load = pltpu.make_async_copy(lower_hbm, lower, sem)
    load.start()
    _, _, _, z, x = device(at_ref)
    odd = x & 1
    for k, ref in enumerate(blocks):
        cols = pl.ds(pl.multiple_of(128 * ((z - k) & 7), 128), 128)
        ah[:, cols], al[:, cols] = split2(ref[...])
    load.wait()
    for i in range(8):
        rows = slice(128 * i, 128 * (i + 1))
        for core in range(2):
            for t in range(2):
                cols = slice(256 * core + 128 * t, 256 * core + 128 * (t + 1))
                place = 128 * (odd if t == 0 else 1 - odd)
                value = lower[2 * i + core, pl.ds(pl.multiple_of(place, 128), 128), :]
                bh[rows, cols], bl[rows, cols] = split2(value)
    for n in range(2):
        cols = slice(256 * n, 256 * (n + 1))
        part = three_pass(ah[...], al[...], bh[:, cols], bl[:, cols])
        out[2 * n] = part[:, :128]
        out[2 * n + 1] = part[:, 128:]
    for k, ref in enumerate(sums):
        ref[...] = out[(x + k) & 3]


def side(at, lower, blocks):
    return pl.pallas_call(
        side_kernel,
        out_shape=(shape(256, 128),) * 4 + (shape(1024, 512, dtype=BF16),) * 2,
        in_specs=[SMEM, HBM] + [VMEM] * 8,
        out_specs=(VMEM,) * 6,
        scratch_shapes=[
            pltpu.VMEM((16, 256, 128), F32),
            pltpu.VMEM((256, 1024), BF16),
            pltpu.VMEM((256, 1024), BF16),
            pltpu.VMEM((4, 256, 128), F32),
            DMA,
        ],
        compiler_params=WIDE,
        cost_estimate=pl.CostEstimate(flops=6 << 28, bytes_accessed=6 << 20, transcendentals=0),
    )(at, lower, *blocks)


def last_kernel(w_hbm, hi_hbm, lo_hbm, out_ref, w, ah, al, bh, bl, sems):
    loads = [
        pltpu.make_async_copy(w_hbm, w, sems.at[0]),
        pltpu.make_async_copy(hi_hbm, bh, sems.at[1]),
        pltpu.make_async_copy(lo_hbm, bl, sems.at[2]),
    ]
    for load in loads:
        load.start()
    loads[0].wait()
    for z in range(8):
        rows = slice(128 * z, 128 * (z + 1))
        ah[:, rows], al[:, rows] = split2(w[z])
    for load in loads[1:]:
        load.wait()
    for n in range(2):
        cols = slice(256 * n, 256 * (n + 1))
        part = three_pass(ah[...], al[...], bh[:, cols], bl[:, cols])
        out_ref[2 * n] = part[:, :128]
        out_ref[2 * n + 1] = part[:, 128:]


def last(w, hi, lo):
    return pl.pallas_call(
        last_kernel,
        out_shape=shape(4, 256, 128),
        in_specs=[HBM] * 3,
        out_specs=VMEM,
        scratch_shapes=[
            pltpu.VMEM((8, 256, 128), F32),
            pltpu.VMEM((256, 1024), BF16),
            pltpu.VMEM((256, 1024), BF16),
            pltpu.VMEM((1024, 512), BF16),
            pltpu.VMEM((1024, 512), BF16),
            DMA((3,)),
        ],
        compiler_params=MIDDLE,
    )(w, hi, lo)


def exchange(v, axis):
    return lax.all_to_all(v, axis, 0, 0, tiled=True)


def deal(v, t):
    moves = [(4 * c + x, 4 * (x >> 1) + 2 * c + ((x & 1) ^ t)) for c in range(2) for x in range(4)]
    return lax.ppermute(v, ("c", "x"), moves)


def turn(v, axis, size, k):
    return lax.ppermute(v, axis, [(i, (i + k) % size) for i in range(size)])


def shards(root_inverse, boundary_map, lower_factor, upper_factor, diagonal_inverse):
    at = lax.axis_index(("y", "c", "z", "x")).astype(jnp.int32).reshape(1)
    upper = lax.all_gather(upper_factor, "z", axis=0, tiled=False)
    sigma, first, second = pick(at, boundary_map.reshape(32, 128), root_inverse, lower_factor)
    copies, lower = fan(deal(first, 0), deal(second, 1))
    lower = lax.all_gather(lower, ("y", "c"), axis=0, tiled=False)
    own = exchange(copies, "y")
    blocks = [sigma] + [turn(sigma, "z", 8, k) for k in range(1, 8)]
    own, blocks = lax.optimization_barrier((own, blocks))
    other = turn(own, "c", 2, 1)
    part = couple(at, upper, other, couple(at, upper, own))
    w = exchange(part, "x").sum(axis=0)
    w_all = exchange(jnp.broadcast_to(w[None], (8, 256, 128)), "z")
    *sums, hi, lo = side(at, lower, blocks)
    total = sums[0]
    for k in range(1, 4):
        total = total + turn(sums[k], "x", 4, k)
    total, w_all = lax.optimization_barrier((-total, w_all))
    product = exchange(last(w_all, hi, lo), "x").sum(axis=0)
    return (total, -w, diagonal_inverse + product)


def solution(mesh):
    grid = Mesh(np.asarray(mesh.devices).reshape(8, 2, 8, 4), ("y", "c", "z", "x"))
    block = P(("y", "c"), ("z", "x"))
    return jax.shard_map(
        shards,
        mesh=grid,
        in_specs=(block, P(), block, block, block),
        out_specs=(block, block, block),
        check_vma=False,
    )
```

```python
import jax
import jax.numpy as jnp
import numpy as np
from jax import lax
from jax.experimental import pallas as pl
from jax.experimental.pallas import tpu as pltpu
from jax.sharding import Mesh, PartitionSpec as P

F32 = jnp.float32
BF16 = jnp.bfloat16
VMEM = pl.BlockSpec(memory_space=pltpu.VMEM)
SMEM = pl.BlockSpec(memory_space=pltpu.SMEM)
HBM = pl.BlockSpec(memory_space=pltpu.HBM)
PARAMS = pltpu.CompilerParams(vmem_limit_bytes=32 * 1024 * 1024)
WIDE = pltpu.CompilerParams(vmem_limit_bytes=62 * 1024 * 1024)
MIDDLE = pltpu.CompilerParams(vmem_limit_bytes=51 * 1024 * 1024)
DMA = pltpu.SemaphoreType.DMA


def shape(*dims, dtype=F32):
    return jax.ShapeDtypeStruct(dims, dtype)


def split2(v):
    hi = v.astype(BF16)
    return hi, (v - hi.astype(F32)).astype(BF16)


def dot(a, b):
    return lax.dot_general(a, b, (((1,), (0,)), ((), ())), preferred_element_type=F32)


def three_pass(ah, al, bh, bl):
    return dot(ah, bh) + (dot(ah, bl) + dot(al, bh))


def device(ref):
    number = ref[0]
    return number >> 5, number & 31, (number >> 5) & 1, (number >> 2) & 7, number & 3


def pick_kernel(
    at_ref, map_hbm, root_hbm, lower_hbm, upper_hbm, su_ref, first_ref, second_ref, picks, root, lower, sems
):
    loads = [
        pltpu.make_async_copy(map_hbm, picks, sems.at[0]),
        pltpu.make_async_copy(root_hbm, root, sems.at[1]),
        pltpu.make_async_copy(lower_hbm, lower, sems.at[2]),
        pltpu.make_async_copy(upper_hbm, su_ref.at[256:512], sems.at[3]),
    ]
    for load in loads:
        load.start()
    row, col, _, _, x = device(at_ref)
    odd = x & 1
    iota = lax.broadcasted_iota(jnp.int32, (256, 128), 0)
    loads[0].wait()
    cols = picks[pl.ds(col, 1), :] - 256 * col
    col_hot = jnp.where(cols == iota, 1.0, 0.0).astype(BF16)
    hots = []
    for part in range(2):
        block = 2 * row + part
        rows = picks[pl.ds(block, 1), :] - 256 * block
        hots.append(jnp.where(rows == iota, 1.0, 0.0).astype(BF16))
    loads[1].wait()
    stack = []
    for part in range(2):
        left = root[256 * part : 256 * (part + 1), :]
        pieces = []
        for _ in range(3):
            piece = left.astype(BF16)
            left = left - piece.astype(F32)
            pieces.append(piece)
        across = lax.dot_general(
            hots[part],
            jnp.concatenate(pieces, axis=1),
            (((0,), (0,)), ((), ())),
            preferred_element_type=F32,
        ).astype(BF16)
        stack += [across[:, 256 * i : 256 * (i + 1)] for i in range(3)]
    value = dot(jnp.concatenate(stack, axis=0), col_hot)
    for part in range(2):
        v = [value[128 * (3 * part + i) : 128 * (3 * part + i + 1), :] for i in range(3)]
        su_ref[128 * part : 128 * (part + 1), :] = (v[0] + v[1]) + v[2]
    for load in loads[2:]:
        load.wait()
    near = pl.multiple_of(128 * odd, 128)
    far = pl.multiple_of(128 - 128 * odd, 128)
    first_ref[0] = su_ref[pl.ds(near, 128), :]
    first_ref[1] = lower[pl.ds(near, 128), :]
    second_ref[0] = su_ref[pl.ds(far, 128), :]
    second_ref[1] = lower[pl.ds(far, 128), :]


def pick(at, blocks, root, lower, upper):
    return pl.pallas_call(
        pick_kernel,
        out_shape=(shape(512, 128), shape(2, 128, 128), shape(2, 128, 128)),
        in_specs=[SMEM] + [HBM] * 4,
        out_specs=(VMEM, VMEM, VMEM),
        scratch_shapes=[
            pltpu.VMEM((32, 128), jnp.int32),
            pltpu.VMEM((512, 256), F32),
            pltpu.VMEM((256, 128), F32),
            DMA((4,)),
        ],
        compiler_params=WIDE,
    )(at, blocks, root, lower, upper)


def fan_kernel(first_ref, second_ref, copies_ref, lower_ref):
    for t, ref in enumerate((first_ref, second_ref)):
        lower_ref[128 * t : 128 * (t + 1), :] = ref[1]
        value = ref[0]
        for i in range(8):
            copies_ref[i, t] = value


def fan(first, second):
    return pl.pallas_call(
        fan_kernel,
        out_shape=(shape(8, 2, 128, 128), shape(256, 128)),
        in_specs=[VMEM] * 2,
        out_specs=(VMEM, VMEM),
        compiler_params=PARAMS,
    )(first, second)


def couple(at, upper, columns, before=None):
    def kernel(at_ref, upper_hbm, columns_hbm, *refs):
        before_ref, (out_ref, left, right, ah, al, bh, bl, sems) = (
            (None, refs) if before is None else (refs[0], refs[1:])
        )
        loads = [
            pltpu.make_async_copy(columns_hbm, right, sems.at[0]),
            pltpu.make_async_copy(upper_hbm.at[:, 256:512], left, sems.at[1]),
        ]
        for load in loads:
            load.start()
        loads[0].wait()
        for z in range(8):
            rows = slice(128 * z, 128 * (z + 1))
            for t in range(2):
                cols = slice(128 * t, 128 * (t + 1))
                bh[rows, cols], bl[rows, cols] = split2(right[z, t])
        loads[1].wait()
        for z in range(8):
            rows = slice(128 * z, 128 * (z + 1))
            ah[:, rows], al[:, rows] = split2(left[z])
        part = three_pass(ah[...], al[...], bh[...], bl[...])
        if before is None:
            out_ref[0] = part[:, :128]
            out_ref[1] = part[:, 128:]
        else:
            _, _, core, _, x = device(at_ref)
            odd = x & 1
            out_ref[2 * core + odd] = before_ref[0]
            out_ref[2 * core + 1 - odd] = before_ref[1]
            out_ref[2 * (1 - core) + odd] = part[:, :128]
            out_ref[2 * (1 - core) + 1 - odd] = part[:, 128:]

    more = () if before is None else (before,)
    return pl.pallas_call(
        kernel,
        out_shape=shape(2 + 2 * len(more), 256, 128),
        in_specs=[SMEM, HBM, HBM] + [VMEM] * len(more),
        out_specs=VMEM,
        scratch_shapes=[
            pltpu.VMEM((8, 256, 128), F32),
            pltpu.VMEM((8, 2, 128, 128), F32),
            pltpu.VMEM((256, 1024), BF16),
            pltpu.VMEM((256, 1024), BF16),
            pltpu.VMEM((1024, 256), BF16),
            pltpu.VMEM((1024, 256), BF16),
            DMA((2,)),
        ],
        compiler_params=PARAMS,
        cost_estimate=pl.CostEstimate(flops=3 << 28, bytes_accessed=3 << 20, transcendentals=0),
    )(at, upper, columns, *more)


def side_kernel(at_ref, su_hbm, lower_hbm, out_ref, bh, bl, sigma, lower, ah, al, sems):
    loads = [
        pltpu.make_async_copy(su_hbm.at[:, 0:256], sigma, sems.at[0]),
        pltpu.make_async_copy(lower_hbm, lower, sems.at[1]),
    ]
    for load in loads:
        load.start()
    _, _, _, _, x = device(at_ref)
    odd = x & 1
    loads[0].wait()
    for z in range(8):
        rows = slice(128 * z, 128 * (z + 1))
        ah[:, rows], al[:, rows] = split2(sigma[z])
    loads[1].wait()
    for z in range(8):
        rows = slice(128 * z, 128 * (z + 1))
        for core in range(2):
            for t in range(2):
                cols = slice(256 * core + 128 * t, 256 * core + 128 * (t + 1))
                place = 128 * (odd if t == 0 else 1 - odd)
                value = lower[2 * z + core, pl.ds(pl.multiple_of(place, 128), 128), :]
                bh[rows, cols], bl[rows, cols] = split2(value)
    for n in range(2):
        cols = slice(256 * n, 256 * (n + 1))
        part = three_pass(ah[...], al[...], bh[:, cols], bl[:, cols])
        out_ref[2 * n] = part[:, :128]
        out_ref[2 * n + 1] = part[:, 128:]


def side(at, gathered, lower):
    return pl.pallas_call(
        side_kernel,
        out_shape=(shape(4, 256, 128),) + (shape(1024, 512, dtype=BF16),) * 2,
        in_specs=[SMEM, HBM, HBM],
        out_specs=(VMEM,) * 3,
        scratch_shapes=[
            pltpu.VMEM((8, 256, 128), F32),
            pltpu.VMEM((16, 256, 128), F32),
            pltpu.VMEM((256, 1024), BF16),
            pltpu.VMEM((256, 1024), BF16),
            DMA((2,)),
        ],
        compiler_params=WIDE,
        cost_estimate=pl.CostEstimate(flops=6 << 28, bytes_accessed=6 << 20, transcendentals=0),
    )(at, gathered, lower)


def last_kernel(w_hbm, hi_hbm, lo_hbm, side_hbm, out_ref, w, ah, al, bh, bl, sems):
    loads = [
        pltpu.make_async_copy(w_hbm, w, sems.at[0]),
        pltpu.make_async_copy(hi_hbm, bh, sems.at[1]),
        pltpu.make_async_copy(lo_hbm, bl, sems.at[2]),
        pltpu.make_async_copy(side_hbm, out_ref.at[:, 0], sems.at[3]),
    ]
    for load in loads:
        load.start()
    loads[0].wait()
    for z in range(8):
        rows = slice(128 * z, 128 * (z + 1))
        ah[:, rows], al[:, rows] = split2(w[z])
    for load in loads[1:3]:
        load.wait()
    for n in range(2):
        cols = slice(256 * n, 256 * (n + 1))
        part = three_pass(ah[...], al[...], bh[:, cols], bl[:, cols])
        out_ref[2 * n, 1] = part[:, :128]
        out_ref[2 * n + 1, 1] = part[:, 128:]
    loads[3].wait()


def last(w, hi, lo, sides):
    return pl.pallas_call(
        last_kernel,
        out_shape=shape(4, 2, 256, 128),
        in_specs=[HBM] * 4,
        out_specs=VMEM,
        scratch_shapes=[
            pltpu.VMEM((8, 256, 128), F32),
            pltpu.VMEM((256, 1024), BF16),
            pltpu.VMEM((256, 1024), BF16),
            pltpu.VMEM((1024, 512), BF16),
            pltpu.VMEM((1024, 512), BF16),
            DMA((4,)),
        ],
        compiler_params=MIDDLE,
    )(w, hi, lo, sides)


def exchange(v, axis):
    return lax.all_to_all(v, axis, 0, 0, tiled=True)


def deal(v, t):
    moves = [(4 * c + x, 4 * (x >> 1) + 2 * c + ((x & 1) ^ t)) for c in range(2) for x in range(4)]
    return lax.ppermute(v, ("c", "x"), moves)


def turn(v, axis, size, k):
    return lax.ppermute(v, axis, [(i, (i + k) % size) for i in range(size)])


def shards(root_inverse, boundary_map, lower_factor, upper_factor, diagonal_inverse):
    at = lax.axis_index(("y", "c", "z", "x")).astype(jnp.int32).reshape(1)
    su, first, second = pick(
        at, boundary_map.reshape(32, 128), root_inverse, lower_factor, upper_factor
    )
    gathered = lax.all_gather(su, "z", axis=0, tiled=False)
    copies, lower = fan(deal(first, 0), deal(second, 1))
    lower = lax.all_gather(lower, ("y", "c"), axis=0, tiled=False)
    own = exchange(copies, "y")
    other = turn(own, "c", 2, 1)
    part = couple(at, gathered, other, couple(at, gathered, own))
    w = exchange(part, "x").sum(axis=0)
    w_all = exchange(jnp.broadcast_to(w[None], (8, 256, 128)), "z")
    sides, hi, lo = side(at, gathered, lower)
    both = exchange(last(w_all, hi, lo, sides), "x").sum(axis=0)
    return (-both[0], -w, diagonal_inverse + both[1])


def solution(mesh):
    grid = Mesh(np.asarray(mesh.devices).reshape(8, 2, 8, 4), ("y", "c", "z", "x"))
    block = P(("y", "c"), ("z", "x"))
    return jax.shard_map(
        shards,
        mesh=grid,
        in_specs=(block, P(), block, block, block),
        out_specs=(block, block, block),
        check_vma=False,
    )
```

```python
import jax
import jax.numpy as jnp
import numpy as np
from jax import lax
from jax.experimental import pallas as pl
from jax.experimental.pallas import tpu as pltpu
from jax.sharding import Mesh, PartitionSpec as P

F32 = jnp.float32
BF16 = jnp.bfloat16
VMEM = pl.BlockSpec(memory_space=pltpu.VMEM)
SMEM = pl.BlockSpec(memory_space=pltpu.SMEM)
HBM = pl.BlockSpec(memory_space=pltpu.HBM)
PARAMS = pltpu.CompilerParams(vmem_limit_bytes=32 * 1024 * 1024)
WIDE = pltpu.CompilerParams(vmem_limit_bytes=62 * 1024 * 1024)
MIDDLE = pltpu.CompilerParams(vmem_limit_bytes=52 * 1024 * 1024)
DMA = pltpu.SemaphoreType.DMA


def shape(*dims, dtype=F32):
    return jax.ShapeDtypeStruct(dims, dtype)


def split2(v):
    hi = v.astype(BF16)
    return hi, (v - hi.astype(F32)).astype(BF16)


def dot(a, b):
    return lax.dot_general(a, b, (((1,), (0,)), ((), ())), preferred_element_type=F32)


def three_pass(ah, al, bh, bl):
    return dot(ah, bh) + (dot(ah, bl) + dot(al, bh))


def device(ref):
    number = ref[0]
    return number >> 5, number & 31, (number >> 5) & 1, (number >> 2) & 7, number & 3


def pick_kernel(
    at_ref, map_hbm, root_hbm, lower_hbm, upper_hbm, su_ref, first_ref, second_ref, picks, root, lower, sems
):
    loads = [
        pltpu.make_async_copy(map_hbm, picks, sems.at[0]),
        pltpu.make_async_copy(root_hbm, root, sems.at[1]),
        pltpu.make_async_copy(lower_hbm, lower, sems.at[2]),
        pltpu.make_async_copy(upper_hbm, su_ref.at[256:512], sems.at[3]),
    ]
    for load in loads:
        load.start()
    row, col, _, _, x = device(at_ref)
    odd = x & 1
    iota = lax.broadcasted_iota(jnp.int32, (256, 128), 0)
    loads[0].wait()
    cols = picks[pl.ds(col, 1), :] - 256 * col
    col_hot = jnp.where(cols == iota, 1.0, 0.0).astype(BF16)
    hots = []
    for part in range(2):
        block = 2 * row + part
        rows = picks[pl.ds(block, 1), :] - 256 * block
        hots.append(jnp.where(rows == iota, 1.0, 0.0).astype(BF16))
    loads[1].wait()
    stack = []
    for part in range(2):
        left = root[256 * part : 256 * (part + 1), :]
        pieces = []
        for _ in range(3):
            piece = left.astype(BF16)
            left = left - piece.astype(F32)
            pieces.append(piece)
        across = lax.dot_general(
            hots[part],
            jnp.concatenate(pieces, axis=1),
            (((0,), (0,)), ((), ())),
            preferred_element_type=F32,
        ).astype(BF16)
        stack += [across[:, 256 * i : 256 * (i + 1)] for i in range(3)]
    value = dot(jnp.concatenate(stack, axis=0), col_hot)
    for part in range(2):
        v = [value[128 * (3 * part + i) : 128 * (3 * part + i + 1), :] for i in range(3)]
        su_ref[128 * part : 128 * (part + 1), :] = (v[0] + v[1]) + v[2]
    for load in loads[2:]:
        load.wait()
    near = pl.multiple_of(128 * odd, 128)
    far = pl.multiple_of(128 - 128 * odd, 128)
    first_ref[0] = su_ref[pl.ds(near, 128), :]
    first_ref[1] = lower[pl.ds(near, 128), :]
    second_ref[0] = su_ref[pl.ds(far, 128), :]
    second_ref[1] = lower[pl.ds(far, 128), :]


def pick(at, blocks, root, lower, upper):
    return pl.pallas_call(
        pick_kernel,
        out_shape=(shape(512, 128), shape(2, 128, 128), shape(2, 128, 128)),
        in_specs=[SMEM] + [HBM] * 4,
        out_specs=(VMEM, VMEM, VMEM),
        scratch_shapes=[
            pltpu.VMEM((32, 128), jnp.int32),
            pltpu.VMEM((512, 256), F32),
            pltpu.VMEM((256, 128), F32),
            DMA((4,)),
        ],
        compiler_params=WIDE,
    )(at, blocks, root, lower, upper)


def fan_kernel(first_ref, second_ref, copies_ref, lower_ref):
    for t, ref in enumerate((first_ref, second_ref)):
        lower_ref[128 * t : 128 * (t + 1), :] = ref[1]
        value = ref[0]
        for i in range(8):
            copies_ref[i, t] = value


def fan(first, second):
    return pl.pallas_call(
        fan_kernel,
        out_shape=(shape(8, 2, 128, 128), shape(256, 128)),
        in_specs=[VMEM] * 2,
        out_specs=(VMEM, VMEM),
        compiler_params=PARAMS,
    )(first, second)


def couple(at, upper, columns, before=None):
    def kernel(at_ref, upper_hbm, columns_hbm, *refs):
        before_ref, (out_ref, left, right, ah, al, bh, bl, sems) = (
            (None, refs) if before is None else (refs[0], refs[1:])
        )
        loads = [
            pltpu.make_async_copy(columns_hbm, right, sems.at[0]),
            pltpu.make_async_copy(upper_hbm.at[:, 256:512], left, sems.at[1]),
        ]
        for load in loads:
            load.start()
        loads[0].wait()
        for z in range(8):
            rows = slice(128 * z, 128 * (z + 1))
            for t in range(2):
                cols = slice(128 * t, 128 * (t + 1))
                bh[rows, cols], bl[rows, cols] = split2(right[z, t])
        loads[1].wait()
        for z in range(8):
            rows = slice(128 * z, 128 * (z + 1))
            ah[:, rows], al[:, rows] = split2(left[z])
        part = three_pass(ah[...], al[...], bh[...], bl[...])
        if before is None:
            out_ref[0] = part[:, :128]
            out_ref[1] = part[:, 128:]
        else:
            _, _, core, _, x = device(at_ref)
            odd = x & 1
            out_ref[2 * core + odd] = before_ref[0]
            out_ref[2 * core + 1 - odd] = before_ref[1]
            out_ref[2 * (1 - core) + odd] = part[:, :128]
            out_ref[2 * (1 - core) + 1 - odd] = part[:, 128:]

    more = () if before is None else (before,)
    return pl.pallas_call(
        kernel,
        out_shape=shape(2 + 2 * len(more), 256, 128),
        in_specs=[SMEM, HBM, HBM] + [VMEM] * len(more),
        out_specs=VMEM,
        scratch_shapes=[
            pltpu.VMEM((8, 256, 128), F32),
            pltpu.VMEM((8, 2, 128, 128), F32),
            pltpu.VMEM((256, 1024), BF16),
            pltpu.VMEM((256, 1024), BF16),
            pltpu.VMEM((1024, 256), BF16),
            pltpu.VMEM((1024, 256), BF16),
            DMA((2,)),
        ],
        compiler_params=PARAMS,
        cost_estimate=pl.CostEstimate(flops=3 << 28, bytes_accessed=3 << 20, transcendentals=0),
    )(at, upper, columns, *more)


def side_kernel(at_ref, su_hbm, lower_hbm, out_ref, bh, bl, sigma, lower, ah, al, sems):
    loads = [
        pltpu.make_async_copy(su_hbm.at[:, 0:256], sigma, sems.at[0]),
        pltpu.make_async_copy(lower_hbm, lower, sems.at[1]),
    ]
    for load in loads:
        load.start()
    _, _, _, _, x = device(at_ref)
    odd = x & 1
    loads[0].wait()
    for z in range(8):
        rows = slice(128 * z, 128 * (z + 1))
        ah[:, rows], al[:, rows] = split2(sigma[z])
    loads[1].wait()
    for z in range(8):
        rows = slice(128 * z, 128 * (z + 1))
        for core in range(2):
            for t in range(2):
                cols = slice(256 * core + 128 * t, 256 * core + 128 * (t + 1))
                place = 128 * (odd if t == 0 else 1 - odd)
                value = lower[2 * z + core, pl.ds(pl.multiple_of(place, 128), 128), :]
                bh[rows, cols], bl[rows, cols] = split2(value)
    for n in range(2):
        cols = slice(256 * n, 256 * (n + 1))
        part = three_pass(ah[...], al[...], bh[:, cols], bl[:, cols])
        out_ref[2 * n] = part[:, :128]
        out_ref[2 * n + 1] = part[:, 128:]


def side(at, gathered, lower):
    return pl.pallas_call(
        side_kernel,
        out_shape=(shape(4, 256, 128),) + (shape(1024, 512, dtype=BF16),) * 2,
        in_specs=[SMEM, HBM, HBM],
        out_specs=(VMEM,) * 3,
        scratch_shapes=[
            pltpu.VMEM((8, 256, 128), F32),
            pltpu.VMEM((16, 256, 128), F32),
            pltpu.VMEM((256, 1024), BF16),
            pltpu.VMEM((256, 1024), BF16),
            DMA((2,)),
        ],
        compiler_params=WIDE,
        cost_estimate=pl.CostEstimate(flops=6 << 28, bytes_accessed=6 << 20, transcendentals=0),
    )(at, gathered, lower)


def last_kernel(w_hbm, hi_hbm, lo_hbm, out_ref, w, ah, al, bh, bl, sems):
    loads = [
        pltpu.make_async_copy(w_hbm, w, sems.at[0]),
        pltpu.make_async_copy(hi_hbm, bh, sems.at[1]),
        pltpu.make_async_copy(lo_hbm, bl, sems.at[2]),
    ]
    for load in loads:
        load.start()
    loads[0].wait()
    for z in range(8):
        rows = slice(128 * z, 128 * (z + 1))
        ah[:, rows], al[:, rows] = split2(w[z])
    for load in loads[1:]:
        load.wait()
    for n in range(2):
        cols = slice(256 * n, 256 * (n + 1))
        part = three_pass(ah[...], al[...], bh[:, cols], bl[:, cols])
        out_ref[2 * n] = part[:, :128]
        out_ref[2 * n + 1] = part[:, 128:]


def last(w, hi, lo):
    return pl.pallas_call(
        last_kernel,
        out_shape=shape(4, 256, 128),
        in_specs=[HBM] * 3,
        out_specs=VMEM,
        scratch_shapes=[
            pltpu.VMEM((8, 256, 128), F32),
            pltpu.VMEM((256, 1024), BF16),
            pltpu.VMEM((256, 1024), BF16),
            pltpu.VMEM((1024, 512), BF16),
            pltpu.VMEM((1024, 512), BF16),
            DMA((3,)),
        ],
        compiler_params=MIDDLE,
    )(w, hi, lo)


def exchange(v, axis):
    return lax.all_to_all(v, axis, 0, 0, tiled=True)


def deal(v, t):
    moves = [(4 * c + x, 4 * (x >> 1) + 2 * c + ((x & 1) ^ t)) for c in range(2) for x in range(4)]
    return lax.ppermute(v, ("c", "x"), moves)


def turn(v, axis, size, k):
    return lax.ppermute(v, axis, [(i, (i + k) % size) for i in range(size)])


def shards(root_inverse, boundary_map, lower_factor, upper_factor, diagonal_inverse):
    at = lax.axis_index(("y", "c", "z", "x")).astype(jnp.int32).reshape(1)
    su, first, second = pick(
        at, boundary_map.reshape(32, 128), root_inverse, lower_factor, upper_factor
    )
    gathered = lax.all_gather(su, "z", axis=0, tiled=False)
    copies, lower = fan(deal(first, 0), deal(second, 1))
    lower = lax.all_gather(lower, ("y", "c"), axis=0, tiled=False)
    own = exchange(copies, "y")
    other = turn(own, "c", 2, 1)
    part = couple(at, gathered, other, couple(at, gathered, own))
    w = exchange(part, "x").sum(axis=0)
    w_all = exchange(jnp.broadcast_to(w[None], (8, 256, 128)), "z")
    sides, hi, lo = side(at, gathered, lower)
    t = lax.psum_scatter(sides, "x", scatter_dimension=0, tiled=False)
    product = exchange(last(w_all, hi, lo), "x").sum(axis=0)
    return (-t, -w, diagonal_inverse + product)


def solution(mesh):
    grid = Mesh(np.asarray(mesh.devices).reshape(8, 2, 8, 4), ("y", "c", "z", "x"))
    block = P(("y", "c"), ("z", "x"))
    return jax.shard_map(
        shards,
        mesh=grid,
        in_specs=(block, P(), block, block, block),
        out_specs=(block, block, block),
        check_vma=False,
    )
```

```python
import jax
import jax.numpy as jnp
import numpy as np
from jax import lax
from jax.experimental import pallas as pl
from jax.experimental.pallas import tpu as pltpu
from jax.sharding import Mesh, PartitionSpec as P

F32 = jnp.float32
BF16 = jnp.bfloat16
VMEM = pl.BlockSpec(memory_space=pltpu.VMEM)
SMEM = pl.BlockSpec(memory_space=pltpu.SMEM)
HBM = pl.BlockSpec(memory_space=pltpu.HBM)
PARAMS = pltpu.CompilerParams(vmem_limit_bytes=32 * 1024 * 1024)
WIDE = pltpu.CompilerParams(vmem_limit_bytes=62 * 1024 * 1024)
MIDDLE = pltpu.CompilerParams(vmem_limit_bytes=52 * 1024 * 1024)
DMA = pltpu.SemaphoreType.DMA


def shape(*dims, dtype=F32):
    return jax.ShapeDtypeStruct(dims, dtype)


def split2(v):
    hi = v.astype(BF16)
    return hi, (v - hi.astype(F32)).astype(BF16)


def dot(a, b):
    return lax.dot_general(a, b, (((1,), (0,)), ((), ())), preferred_element_type=F32)


def three_pass(ah, al, bh, bl):
    return dot(ah, bh) + (dot(ah, bl) + dot(al, bh))


def device(ref):
    number = ref[0]
    return number >> 5, number & 31, (number >> 5) & 1, (number >> 2) & 7, number & 3


def pick_kernel(
    at_ref, map_hbm, root_hbm, lower_hbm, upper_hbm, su_ref, first_ref, second_ref, picks, root, lower, sems
):
    loads = [
        pltpu.make_async_copy(map_hbm, picks, sems.at[0]),
        pltpu.make_async_copy(root_hbm, root, sems.at[1]),
        pltpu.make_async_copy(lower_hbm, lower, sems.at[2]),
        pltpu.make_async_copy(upper_hbm, su_ref.at[256:512], sems.at[3]),
    ]
    for load in loads:
        load.start()
    row, col, _, _, x = device(at_ref)
    odd = x & 1
    iota = lax.broadcasted_iota(jnp.int32, (256, 128), 0)
    loads[0].wait()
    cols = picks[pl.ds(col, 1), :] - 256 * col
    col_hot = jnp.where(cols == iota, 1.0, 0.0).astype(BF16)
    hots = []
    for part in range(2):
        block = 2 * row + part
        rows = picks[pl.ds(block, 1), :] - 256 * block
        hots.append(jnp.where(rows == iota, 1.0, 0.0).astype(BF16))
    loads[1].wait()
    stack = []
    for part in range(2):
        left = root[256 * part : 256 * (part + 1), :]
        pieces = []
        for _ in range(3):
            piece = left.astype(BF16)
            left = left - piece.astype(F32)
            pieces.append(piece)
        across = lax.dot_general(
            hots[part],
            jnp.concatenate(pieces, axis=1),
            (((0,), (0,)), ((), ())),
            preferred_element_type=F32,
        ).astype(BF16)
        stack += [across[:, 256 * i : 256 * (i + 1)] for i in range(3)]
    value = dot(jnp.concatenate(stack, axis=0), col_hot)
    for part in range(2):
        v = [value[128 * (3 * part + i) : 128 * (3 * part + i + 1), :] for i in range(3)]
        su_ref[128 * part : 128 * (part + 1), :] = (v[0] + v[1]) + v[2]
    for load in loads[2:]:
        load.wait()
    near = pl.multiple_of(128 * odd, 128)
    far = pl.multiple_of(128 - 128 * odd, 128)
    first_ref[0] = su_ref[pl.ds(near, 128), :]
    first_ref[1] = lower[pl.ds(near, 128), :]
    second_ref[0] = su_ref[pl.ds(far, 128), :]
    second_ref[1] = lower[pl.ds(far, 128), :]


def pick(at, blocks, root, lower, upper):
    return pl.pallas_call(
        pick_kernel,
        out_shape=(shape(512, 128), shape(2, 128, 128), shape(2, 128, 128)),
        in_specs=[SMEM] + [HBM] * 4,
        out_specs=(VMEM, VMEM, VMEM),
        scratch_shapes=[
            pltpu.VMEM((32, 128), jnp.int32),
            pltpu.VMEM((512, 256), F32),
            pltpu.VMEM((256, 128), F32),
            DMA((4,)),
        ],
        compiler_params=WIDE,
    )(at, blocks, root, lower, upper)


def fan_kernel(first_ref, second_ref, copies_ref, lower_ref):
    for t, ref in enumerate((first_ref, second_ref)):
        lower_ref[128 * t : 128 * (t + 1), :] = ref[1]
        value = ref[0]
        for i in range(8):
            copies_ref[i, t] = value


def fan(first, second):
    return pl.pallas_call(
        fan_kernel,
        out_shape=(shape(8, 2, 128, 128), shape(256, 128)),
        in_specs=[VMEM] * 2,
        out_specs=(VMEM, VMEM),
        compiler_params=PARAMS,
    )(first, second)


def couple(at, upper, columns, before=None):
    def kernel(at_ref, upper_hbm, columns_hbm, *refs):
        before_ref, (out_ref, left, right, ah, al, bh, bl, sems) = (
            (None, refs) if before is None else (refs[0], refs[1:])
        )
        loads = [
            pltpu.make_async_copy(columns_hbm, right, sems.at[0]),
            pltpu.make_async_copy(upper_hbm.at[:, 256:512], left, sems.at[1]),
        ]
        for load in loads:
            load.start()
        loads[0].wait()
        for z in range(8):
            rows = slice(128 * z, 128 * (z + 1))
            for t in range(2):
                cols = slice(128 * t, 128 * (t + 1))
                bh[rows, cols], bl[rows, cols] = split2(right[z, t])
        loads[1].wait()
        for z in range(8):
            rows = slice(128 * z, 128 * (z + 1))
            ah[:, rows], al[:, rows] = split2(left[z])
        part = three_pass(ah[...], al[...], bh[...], bl[...])
        if before is None:
            out_ref[0] = part[:, :128]
            out_ref[1] = part[:, 128:]
        else:
            _, _, core, _, x = device(at_ref)
            odd = x & 1
            out_ref[2 * core + odd] = before_ref[0]
            out_ref[2 * core + 1 - odd] = before_ref[1]
            out_ref[2 * (1 - core) + odd] = part[:, :128]
            out_ref[2 * (1 - core) + 1 - odd] = part[:, 128:]

    more = () if before is None else (before,)
    return pl.pallas_call(
        kernel,
        out_shape=shape(2 + 2 * len(more), 256, 128),
        in_specs=[SMEM, HBM, HBM] + [VMEM] * len(more),
        out_specs=VMEM,
        scratch_shapes=[
            pltpu.VMEM((8, 256, 128), F32),
            pltpu.VMEM((8, 2, 128, 128), F32),
            pltpu.VMEM((256, 1024), BF16),
            pltpu.VMEM((256, 1024), BF16),
            pltpu.VMEM((1024, 256), BF16),
            pltpu.VMEM((1024, 256), BF16),
            DMA((2,)),
        ],
        compiler_params=PARAMS,
        cost_estimate=pl.CostEstimate(flops=3 << 28, bytes_accessed=3 << 20, transcendentals=0),
    )(at, upper, columns, *more)


def side_kernel(
    at_ref, su_hbm, lower_hbm, out_hbm, hi_hbm, lo_hbm, sigma, lower, ah, al, bh, bl, out, sems
):
    loads = [pltpu.make_async_copy(su_hbm.at[:, 0:256], sigma, sems.at[0])]
    for i in range(2):
        rows = slice(8 * i, 8 * (i + 1))
        loads.append(pltpu.make_async_copy(lower_hbm.at[rows], lower.at[rows], sems.at[1 + i]))
    for load in loads:
        load.start()
    _, _, _, _, x = device(at_ref)
    odd = x & 1
    loads[0].wait()
    for z in range(8):
        rows = slice(128 * z, 128 * (z + 1))
        ah[:, rows], al[:, rows] = split2(sigma[z])
    for z in range(8):
        if z % 4 == 0:
            loads[1 + z // 4].wait()
        rows = slice(128 * z, 128 * (z + 1))
        for core in range(2):
            for t in range(2):
                cols = slice(256 * core + 128 * t, 256 * core + 128 * (t + 1))
                place = 128 * (odd if t == 0 else 1 - odd)
                value = lower[2 * z + core, pl.ds(pl.multiple_of(place, 128), 128), :]
                bh[rows, cols], bl[rows, cols] = split2(value)
    stores = [
        pltpu.make_async_copy(bh, hi_hbm, sems.at[3]),
        pltpu.make_async_copy(bl, lo_hbm, sems.at[4]),
    ]
    for store in stores:
        store.start()
    for n in range(2):
        cols = slice(256 * n, 256 * (n + 1))
        part = -three_pass(ah[...], al[...], bh[:, cols], bl[:, cols])
        out[2 * n] = part[:, :128]
        out[2 * n + 1] = part[:, 128:]
        pair = slice(2 * n, 2 * n + 2)
        stores.append(pltpu.make_async_copy(out.at[pair], out_hbm.at[pair], sems.at[5 + n]))
        stores[-1].start()
    for store in stores:
        store.wait()


def side(at, gathered, lower):
    return pl.pallas_call(
        side_kernel,
        out_shape=(shape(4, 256, 128),) + (shape(1024, 512, dtype=BF16),) * 2,
        in_specs=[SMEM, HBM, HBM],
        out_specs=(HBM,) * 3,
        scratch_shapes=[
            pltpu.VMEM((8, 256, 128), F32),
            pltpu.VMEM((16, 256, 128), F32),
            pltpu.VMEM((256, 1024), BF16),
            pltpu.VMEM((256, 1024), BF16),
            pltpu.VMEM((1024, 512), BF16),
            pltpu.VMEM((1024, 512), BF16),
            pltpu.VMEM((4, 256, 128), F32),
            DMA((7,)),
        ],
        compiler_params=WIDE,
        cost_estimate=pl.CostEstimate(flops=6 << 28, bytes_accessed=6 << 20, transcendentals=0),
    )(at, gathered, lower)


def last_kernel(w_hbm, hi_hbm, lo_hbm, out_ref, w, ah, al, bh, bl, sems):
    loads = [
        pltpu.make_async_copy(w_hbm, w, sems.at[0]),
        pltpu.make_async_copy(hi_hbm, bh, sems.at[1]),
        pltpu.make_async_copy(lo_hbm, bl, sems.at[2]),
    ]
    for load in loads:
        load.start()
    loads[0].wait()
    for z in range(8):
        rows = slice(128 * z, 128 * (z + 1))
        ah[:, rows], al[:, rows] = split2(w[z])
    for load in loads[1:]:
        load.wait()
    for n in range(2):
        cols = slice(256 * n, 256 * (n + 1))
        part = three_pass(ah[...], al[...], bh[:, cols], bl[:, cols])
        out_ref[2 * n] = part[:, :128]
        out_ref[2 * n + 1] = part[:, 128:]


def last(w, hi, lo):
    return pl.pallas_call(
        last_kernel,
        out_shape=shape(4, 256, 128),
        in_specs=[HBM] * 3,
        out_specs=VMEM,
        scratch_shapes=[
            pltpu.VMEM((8, 256, 128), F32),
            pltpu.VMEM((256, 1024), BF16),
            pltpu.VMEM((256, 1024), BF16),
            pltpu.VMEM((1024, 512), BF16),
            pltpu.VMEM((1024, 512), BF16),
            DMA((3,)),
        ],
        compiler_params=MIDDLE,
    )(w, hi, lo)


def exchange(v, axis):
    return lax.all_to_all(v, axis, 0, 0, tiled=True)


def deal(v, t):
    moves = [(4 * c + x, 4 * (x >> 1) + 2 * c + ((x & 1) ^ t)) for c in range(2) for x in range(4)]
    return lax.ppermute(v, ("c", "x"), moves)


def turn(v, axis, size, k):
    return lax.ppermute(v, axis, [(i, (i + k) % size) for i in range(size)])


def shards(root_inverse, boundary_map, lower_factor, upper_factor, diagonal_inverse):
    at = lax.axis_index(("y", "c", "z", "x")).astype(jnp.int32).reshape(1)
    su, first, second = pick(
        at, boundary_map.reshape(32, 128), root_inverse, lower_factor, upper_factor
    )
    gathered = lax.all_gather(su, "z", axis=0, tiled=False)
    copies, lower = fan(deal(first, 0), deal(second, 1))
    lower = lax.all_gather(lower, ("y", "c"), axis=0, tiled=False)
    own = exchange(copies, "y")
    other = turn(own, "c", 2, 1)
    part = couple(at, gathered, other, couple(at, gathered, own))
    w = exchange(part, "x").sum(axis=0)
    w_all = exchange(jnp.broadcast_to(w[None], (8, 256, 128)), "z")
    sides, hi, lo = side(at, gathered, lower)
    t = lax.psum_scatter(sides, "x", scatter_dimension=0, tiled=False)
    product = exchange(last(w_all, hi, lo), "x").sum(axis=0)
    return (t, -w, diagonal_inverse + product)


def solution(mesh):
    grid = Mesh(np.asarray(mesh.devices).reshape(8, 2, 8, 4), ("y", "c", "z", "x"))
    block = P(("y", "c"), ("z", "x"))
    return jax.shard_map(
        shards,
        mesh=grid,
        in_specs=(block, P(), block, block, block),
        out_specs=(block, block, block),
        check_vma=False,
    )
```

```python
import jax
import jax.numpy as jnp
import numpy as np
from jax import lax
from jax.experimental import pallas as pl
from jax.experimental.pallas import tpu as pltpu
from jax.sharding import Mesh, PartitionSpec as P

F32 = jnp.float32
BF16 = jnp.bfloat16
VMEM = pl.BlockSpec(memory_space=pltpu.VMEM)
SMEM = pl.BlockSpec(memory_space=pltpu.SMEM)
HBM = pl.BlockSpec(memory_space=pltpu.HBM)
PARAMS = pltpu.CompilerParams(vmem_limit_bytes=32 * 1024 * 1024)
WIDE = pltpu.CompilerParams(vmem_limit_bytes=62 * 1024 * 1024)
NEAR = pltpu.CompilerParams(vmem_limit_bytes=51 * 1024 * 1024)
MIDDLE = pltpu.CompilerParams(vmem_limit_bytes=52 * 1024 * 1024)
DMA = pltpu.SemaphoreType.DMA


def shape(*dims, dtype=F32):
    return jax.ShapeDtypeStruct(dims, dtype)


def split2(v):
    hi = v.astype(BF16)
    return hi, (v - hi.astype(F32)).astype(BF16)


def dot(a, b):
    return lax.dot_general(a, b, (((1,), (0,)), ((), ())), preferred_element_type=F32)


def three_pass(ah, al, bh, bl):
    return dot(ah, bh) + (dot(ah, bl) + dot(al, bh))


def device(ref):
    number = ref[0]
    return number >> 5, number & 31, (number >> 5) & 1, (number >> 2) & 7, number & 3


def pick_kernel(
    at_ref, map_hbm, root_hbm, upper_hbm, su_ref, first_ref, second_ref, picks, root, sems
):
    loads = [
        pltpu.make_async_copy(map_hbm, picks, sems.at[0]),
        pltpu.make_async_copy(root_hbm, root, sems.at[1]),
        pltpu.make_async_copy(upper_hbm, su_ref.at[256:512], sems.at[2]),
    ]
    for load in loads:
        load.start()
    row, col, _, _, x = device(at_ref)
    odd = x & 1
    iota = lax.broadcasted_iota(jnp.int32, (256, 128), 0)
    loads[0].wait()
    cols = picks[pl.ds(col, 1), :] - 256 * col
    col_hot = jnp.where(cols == iota, 1.0, 0.0).astype(BF16)
    hots = []
    for part in range(2):
        block = 2 * row + part
        rows = picks[pl.ds(block, 1), :] - 256 * block
        hots.append(jnp.where(rows == iota, 1.0, 0.0).astype(BF16))
    loads[1].wait()
    stack = []
    for part in range(2):
        left = root[256 * part : 256 * (part + 1), :]
        pieces = []
        for _ in range(3):
            piece = left.astype(BF16)
            left = left - piece.astype(F32)
            pieces.append(piece)
        across = lax.dot_general(
            hots[part],
            jnp.concatenate(pieces, axis=1),
            (((0,), (0,)), ((), ())),
            preferred_element_type=F32,
        ).astype(BF16)
        stack += [across[:, 256 * i : 256 * (i + 1)] for i in range(3)]
    value = dot(jnp.concatenate(stack, axis=0), col_hot)
    for part in range(2):
        v = [value[128 * (3 * part + i) : 128 * (3 * part + i + 1), :] for i in range(3)]
        su_ref[128 * part : 128 * (part + 1), :] = (v[0] + v[1]) + v[2]
    loads[2].wait()
    near = pl.multiple_of(128 * odd, 128)
    far = pl.multiple_of(128 - 128 * odd, 128)
    first_ref[...] = su_ref[pl.ds(near, 128), :]
    second_ref[...] = su_ref[pl.ds(far, 128), :]


def pick(at, blocks, root, upper):
    return pl.pallas_call(
        pick_kernel,
        out_shape=(shape(512, 128), shape(128, 128), shape(128, 128)),
        in_specs=[SMEM] + [HBM] * 3,
        out_specs=(VMEM, VMEM, VMEM),
        scratch_shapes=[
            pltpu.VMEM((32, 128), jnp.int32),
            pltpu.VMEM((512, 256), F32),
            DMA((3,)),
        ],
        compiler_params=WIDE,
    )(at, blocks, root, upper)


def fan_kernel(first_ref, second_ref, copies_ref):
    for t, ref in enumerate((first_ref, second_ref)):
        value = ref[...]
        for i in range(8):
            copies_ref[i, t] = value


def fan(first, second):
    return pl.pallas_call(
        fan_kernel,
        out_shape=shape(8, 2, 128, 128),
        in_specs=[VMEM] * 2,
        out_specs=VMEM,
        compiler_params=PARAMS,
    )(first, second)


def couple(at, upper, columns, before=None):
    def kernel(at_ref, upper_hbm, columns_hbm, *refs):
        before_ref, (out_ref, left, right, ah, al, bh, bl, sems) = (
            (None, refs) if before is None else (refs[0], refs[1:])
        )
        loads = [
            pltpu.make_async_copy(columns_hbm, right, sems.at[0]),
            pltpu.make_async_copy(upper_hbm.at[:, 256:512], left, sems.at[1]),
        ]
        for load in loads:
            load.start()
        _, _, core, _, x = device(at_ref)
        odd = x & 1
        side = core if before is None else 1 - core
        loads[0].wait()
        for z in range(8):
            rows = slice(128 * z, 128 * (z + 1))
            for t in range(2):
                cols = slice(128 * t, 128 * (t + 1))
                bh[rows, cols], bl[rows, cols] = split2(right[z ^ (4 * side), t])
        loads[1].wait()
        for z in range(8):
            rows = slice(128 * z, 128 * (z + 1))
            ah[:, rows], al[:, rows] = split2(left[z])
        part = three_pass(ah[...], al[...], bh[...], bl[...])
        if before is None:
            out_ref[0] = part[:, :128]
            out_ref[1] = part[:, 128:]
        else:
            out_ref[odd] = before_ref[0]
            out_ref[1 - odd] = before_ref[1]
            out_ref[2 + odd] = part[:, :128]
            out_ref[3 - odd] = part[:, 128:]

    more = () if before is None else (before,)
    return pl.pallas_call(
        kernel,
        out_shape=shape(2 + 2 * len(more), 256, 128),
        in_specs=[SMEM, HBM, HBM] + [VMEM] * len(more),
        out_specs=VMEM,
        scratch_shapes=[
            pltpu.VMEM((8, 256, 128), F32),
            pltpu.VMEM((8, 2, 128, 128), F32),
            pltpu.VMEM((256, 1024), BF16),
            pltpu.VMEM((256, 1024), BF16),
            pltpu.VMEM((1024, 256), BF16),
            pltpu.VMEM((1024, 256), BF16),
            DMA((2,)),
        ],
        compiler_params=NEAR,
        cost_estimate=pl.CostEstimate(flops=3 << 28, bytes_accessed=3 << 20, transcendentals=0),
    )(at, upper, columns, *more)


def side_kernel(
    at_ref, su_hbm, lower_hbm, out_hbm, hi_hbm, lo_hbm, sigma, lower, ah, al, bh, bl, out, sems
):
    loads = [pltpu.make_async_copy(su_hbm.at[:, 0:256], sigma, sems.at[0])]
    for i in range(2):
        rows = slice(8 * i, 8 * (i + 1))
        loads.append(pltpu.make_async_copy(lower_hbm.at[rows], lower.at[rows], sems.at[1 + i]))
    for load in loads:
        load.start()
    _, _, _, _, x = device(at_ref)
    odd = x & 1
    loads[0].wait()
    for z in range(8):
        rows = slice(128 * z, 128 * (z + 1))
        ah[:, rows], al[:, rows] = split2(sigma[z])
    for z in range(8):
        if z % 4 == 0:
            loads[1 + z // 4].wait()
        rows = slice(128 * z, 128 * (z + 1))
        for core in range(2):
            for t in range(2):
                cols = slice(256 * core + 128 * t, 256 * core + 128 * (t + 1))
                place = 128 * (odd if t == 0 else 1 - odd)
                value = lower[2 * z + core, pl.ds(pl.multiple_of(place, 128), 128), :]
                bh[rows, cols], bl[rows, cols] = split2(value)
    stores = [
        pltpu.make_async_copy(bh, hi_hbm, sems.at[3]),
        pltpu.make_async_copy(bl, lo_hbm, sems.at[4]),
    ]
    for store in stores:
        store.start()
    for n in range(2):
        cols = slice(256 * n, 256 * (n + 1))
        part = -three_pass(ah[...], al[...], bh[:, cols], bl[:, cols])
        out[2 * n] = part[:, :128]
        out[2 * n + 1] = part[:, 128:]
        pair = slice(2 * n, 2 * n + 2)
        stores.append(pltpu.make_async_copy(out.at[pair], out_hbm.at[pair], sems.at[5 + n]))
        stores[-1].start()
    for store in stores:
        store.wait()


def side(at, gathered, lower):
    return pl.pallas_call(
        side_kernel,
        out_shape=(shape(4, 256, 128),) + (shape(1024, 512, dtype=BF16),) * 2,
        in_specs=[SMEM, HBM, HBM],
        out_specs=(HBM,) * 3,
        scratch_shapes=[
            pltpu.VMEM((8, 256, 128), F32),
            pltpu.VMEM((16, 256, 128), F32),
            pltpu.VMEM((256, 1024), BF16),
            pltpu.VMEM((256, 1024), BF16),
            pltpu.VMEM((1024, 512), BF16),
            pltpu.VMEM((1024, 512), BF16),
            pltpu.VMEM((4, 256, 128), F32),
            DMA((7,)),
        ],
        compiler_params=WIDE,
        cost_estimate=pl.CostEstimate(flops=6 << 28, bytes_accessed=6 << 20, transcendentals=0),
    )(at, gathered, lower)


def last_kernel(at_ref, w_hbm, hi_hbm, lo_hbm, out_hbm, w, ah, al, bh, bl, out, sems):
    loads = [
        pltpu.make_async_copy(w_hbm, w, sems.at[0]),
        pltpu.make_async_copy(hi_hbm, bh, sems.at[1]),
        pltpu.make_async_copy(lo_hbm, bl, sems.at[2]),
    ]
    for load in loads:
        load.start()
    core = device(at_ref)[2]
    loads[0].wait()
    for z in range(8):
        rows = slice(128 * z, 128 * (z + 1))
        ah[:, rows], al[:, rows] = split2(w[z ^ (4 * core)])
    for load in loads[1:]:
        load.wait()
    stores = []
    for n in range(2):
        cols = slice(256 * n, 256 * (n + 1))
        part = three_pass(ah[...], al[...], bh[:, cols], bl[:, cols])
        out[2 * n] = part[:, :128]
        out[2 * n + 1] = part[:, 128:]
        pair, place = slice(2 * n, 2 * n + 2), pl.ds(2 * (n ^ core), 2)
        stores.append(pltpu.make_async_copy(out.at[pair], out_hbm.at[place], sems.at[3 + n]))
        stores[-1].start()
    for store in stores:
        store.wait()


def last(at, w, hi, lo):
    return pl.pallas_call(
        last_kernel,
        out_shape=shape(4, 256, 128),
        in_specs=[SMEM] + [HBM] * 3,
        out_specs=HBM,
        scratch_shapes=[
            pltpu.VMEM((8, 256, 128), F32),
            pltpu.VMEM((256, 1024), BF16),
            pltpu.VMEM((256, 1024), BF16),
            pltpu.VMEM((1024, 512), BF16),
            pltpu.VMEM((1024, 512), BF16),
            pltpu.VMEM((4, 256, 128), F32),
            DMA((5,)),
        ],
        compiler_params=MIDDLE,
    )(at, w, hi, lo)


def exchange(v, axis, size):
    axes = (axis, "c") if axis == "y" else ("c", axis)
    groups = [
        [2 * p + c if axis == "y" else size * c + p for p in (i ^ (size // 2 * c) for i in range(size))]
        for c in range(2)
    ]
    return lax.all_to_all(v, axes, 0, 0, tiled=True, axis_index_groups=groups)


def deal(v, t):
    moves = [(4 * c + x, 4 * (x >> 1) + 2 * c + ((x & 1) ^ t)) for c in range(2) for x in range(4)]
    return lax.ppermute(v, ("c", "x"), moves)


def turn(v, axis, size, k):
    return lax.ppermute(v, axis, [(i, (i + k) % size) for i in range(size)])


def shards(root_inverse, boundary_map, lower_factor, upper_factor, diagonal_inverse):
    at = lax.axis_index(("y", "c", "z", "x")).astype(jnp.int32).reshape(1)
    su, first, second = pick(at, boundary_map.reshape(32, 128), root_inverse, upper_factor)
    gathered = lax.all_gather(su, "z", axis=0, tiled=False)
    copies = fan(deal(first, 0), deal(second, 1))
    copies, lower = lax.optimization_barrier((copies, lower_factor))
    odd = lax.axis_index("x") & 1
    lower = [
        deal(lax.dynamic_slice_in_dim(lower, 128 * (odd ^ t), 128), t) for t in range(2)
    ]
    lower = jnp.concatenate(lower, axis=0)
    lower = lax.all_gather(lower, ("y", "c"), axis=0, tiled=False)
    own = exchange(copies, "y", 8)
    other = turn(own, "c", 2, 1)
    part = couple(at, gathered, other, couple(at, gathered, own))
    w = exchange(part, "x", 4).sum(axis=0)
    w_all = exchange(jnp.broadcast_to(w[None], (8, 256, 128)), "z", 8)
    sides, hi, lo = side(at, gathered, lower)
    t = lax.psum_scatter(sides, "x", scatter_dimension=0, tiled=False)
    product = exchange(last(at, w_all, hi, lo), "x", 4).sum(axis=0)
    return (t, -w, diagonal_inverse + product)


def solution(mesh):
    grid = Mesh(np.asarray(mesh.devices).reshape(8, 2, 8, 4), ("y", "c", "z", "x"))
    block = P(("y", "c"), ("z", "x"))
    return jax.shard_map(
        shards,
        mesh=grid,
        in_specs=(block, P(), block, block, block),
        out_specs=(block, block, block),
        check_vma=False,
    )
```

```python
import jax
import jax.numpy as jnp
import numpy as np
from jax import lax
from jax.experimental import pallas as pl
from jax.experimental.pallas import tpu as pltpu
from jax.sharding import Mesh, PartitionSpec as P

F32 = jnp.float32
BF16 = jnp.bfloat16
VMEM = pl.BlockSpec(memory_space=pltpu.VMEM)
SMEM = pl.BlockSpec(memory_space=pltpu.SMEM)
HBM = pl.BlockSpec(memory_space=pltpu.HBM)
PARAMS = pltpu.CompilerParams(vmem_limit_bytes=32 * 1024 * 1024)
WIDE = pltpu.CompilerParams(vmem_limit_bytes=62 * 1024 * 1024)
MIDDLE = pltpu.CompilerParams(vmem_limit_bytes=52 * 1024 * 1024)
DMA = pltpu.SemaphoreType.DMA
ORDER = (0, 4, 2, 6, 1, 5, 3, 7)


def shape(*dims, dtype=F32):
    return jax.ShapeDtypeStruct(dims, dtype)


def split2(v):
    hi = v.astype(BF16)
    return hi, (v - hi.astype(F32)).astype(BF16)


def dot(a, b):
    return lax.dot_general(a, b, (((1,), (0,)), ((), ())), preferred_element_type=F32)


def three_pass(ah, al, bh, bl):
    return dot(ah, bh) + (dot(ah, bl) + dot(al, bh))


def device(ref):
    number = ref[0]
    return number >> 5, number & 31, (number >> 5) & 1, (number >> 2) & 7, number & 3


def pick_kernel(
    at_ref, map_hbm, root_hbm, sigma_ref, first_ref, second_ref, picks, root, sems
):
    loads = [
        pltpu.make_async_copy(map_hbm, picks, sems.at[0]),
        pltpu.make_async_copy(root_hbm, root, sems.at[1]),
    ]
    for load in loads:
        load.start()
    row, col, _, _, x = device(at_ref)
    odd = x & 1
    iota = lax.broadcasted_iota(jnp.int32, (256, 128), 0)
    loads[0].wait()
    cols = picks[pl.ds(col, 1), :] - 256 * col
    col_hot = jnp.where(cols == iota, 1.0, 0.0).astype(BF16)
    hots = []
    for part in range(2):
        block = 2 * row + part
        rows = picks[pl.ds(block, 1), :] - 256 * block
        hots.append(jnp.where(rows == iota, 1.0, 0.0).astype(BF16))
    loads[1].wait()
    stack = []
    for part in range(2):
        left = root[256 * part : 256 * (part + 1), :]
        pieces = []
        for _ in range(3):
            piece = left.astype(BF16)
            left = left - piece.astype(F32)
            pieces.append(piece)
        across = lax.dot_general(
            hots[part],
            jnp.concatenate(pieces, axis=1),
            (((0,), (0,)), ((), ())),
            preferred_element_type=F32,
        ).astype(BF16)
        stack += [across[:, 256 * i : 256 * (i + 1)] for i in range(3)]
    value = dot(jnp.concatenate(stack, axis=0), col_hot)
    for part in range(2):
        v = [value[128 * (3 * part + i) : 128 * (3 * part + i + 1), :] for i in range(3)]
        sigma_ref[128 * part : 128 * (part + 1), :] = (v[0] + v[1]) + v[2]
    near = pl.multiple_of(128 * odd, 128)
    far = pl.multiple_of(128 - 128 * odd, 128)
    first_ref[...] = sigma_ref[pl.ds(near, 128), :]
    second_ref[...] = sigma_ref[pl.ds(far, 128), :]


def pick(at, blocks, root):
    return pl.pallas_call(
        pick_kernel,
        out_shape=(shape(256, 128), shape(128, 128), shape(128, 128)),
        in_specs=[SMEM] + [HBM] * 2,
        out_specs=(VMEM, VMEM, VMEM),
        scratch_shapes=[
            pltpu.VMEM((32, 128), jnp.int32),
            pltpu.VMEM((512, 256), F32),
            DMA((2,)),
        ],
        compiler_params=WIDE,
    )(at, blocks, root)


def fan_kernel(first_ref, second_ref, copies_ref):
    for t, ref in enumerate((first_ref, second_ref)):
        value = ref[...]
        for i in range(8):
            copies_ref[i, t] = value


def fan(first, second):
    return pl.pallas_call(
        fan_kernel,
        out_shape=shape(8, 2, 128, 128),
        in_specs=[VMEM] * 2,
        out_specs=VMEM,
        compiler_params=PARAMS,
    )(first, second)


def couple(at, upper, columns, before=None):
    def kernel(at_ref, upper_hbm, columns_hbm, *refs):
        before_ref, (out_ref, left, right, ah, al, bh, bl, sems) = (
            (None, refs) if before is None else (refs[0], refs[1:])
        )
        loads = [
            pltpu.make_async_copy(columns_hbm, right, sems.at[0]),
            pltpu.make_async_copy(upper_hbm, left, sems.at[1]),
        ]
        for load in loads:
            load.start()
        _, _, core, _, x = device(at_ref)
        odd = x & 1
        side = core if before is None else 1 - core
        loads[0].wait()
        for z in range(8):
            rows = slice(128 * z, 128 * (z + 1))
            for t in range(2):
                cols = slice(128 * t, 128 * (t + 1))
                bh[rows, cols], bl[rows, cols] = split2(right[z ^ (4 * side), t])
        loads[1].wait()
        for z in range(8):
            rows = slice(128 * z, 128 * (z + 1))
            ah[:, rows], al[:, rows] = split2(left[z])
        part = three_pass(ah[...], al[...], bh[...], bl[...])
        if before is None:
            out_ref[0] = part[:, :128]
            out_ref[1] = part[:, 128:]
        else:
            out_ref[odd] = before_ref[0]
            out_ref[1 - odd] = before_ref[1]
            out_ref[2 + odd] = part[:, :128]
            out_ref[3 - odd] = part[:, 128:]

    more = () if before is None else (before,)
    return pl.pallas_call(
        kernel,
        out_shape=shape(2 + 2 * len(more), 256, 128),
        in_specs=[SMEM, HBM, HBM] + [VMEM] * len(more),
        out_specs=VMEM,
        scratch_shapes=[
            pltpu.VMEM((8, 256, 128), F32),
            pltpu.VMEM((8, 2, 128, 128), F32),
            pltpu.VMEM((256, 1024), BF16),
            pltpu.VMEM((256, 1024), BF16),
            pltpu.VMEM((1024, 256), BF16),
            pltpu.VMEM((1024, 256), BF16),
            DMA((2,)),
        ],
        compiler_params=PARAMS,
        cost_estimate=pl.CostEstimate(flops=3 << 28, bytes_accessed=3 << 20, transcendentals=0),
    )(at, upper, columns, *more)


def side_kernel(
    at_ref, sigma_hbm, lower_hbm, out_hbm, hi_hbm, lo_hbm, sigma, lower, ah, al, bh, bl, out, sems
):
    loads = [pltpu.make_async_copy(sigma_hbm, sigma, sems.at[0])]
    for i in range(2):
        rows = slice(8 * i, 8 * (i + 1))
        loads.append(pltpu.make_async_copy(lower_hbm.at[rows], lower.at[rows], sems.at[1 + i]))
    for load in loads:
        load.start()
    _, _, _, z_at, x = device(at_ref)
    odd = x & 1
    loads[0].wait()
    for k, flip in enumerate(ORDER):
        cols = pl.ds(pl.multiple_of(128 * (z_at ^ flip), 128), 128)
        ah[:, cols], al[:, cols] = split2(sigma[k])
    for z in range(8):
        if z % 4 == 0:
            loads[1 + z // 4].wait()
        rows = slice(128 * z, 128 * (z + 1))
        for core in range(2):
            for t in range(2):
                cols = slice(256 * core + 128 * t, 256 * core + 128 * (t + 1))
                place = 128 * (odd if t == 0 else 1 - odd)
                value = lower[2 * z + core, pl.ds(pl.multiple_of(place, 128), 128), :]
                bh[rows, cols], bl[rows, cols] = split2(value)
    stores = [
        pltpu.make_async_copy(bh, hi_hbm, sems.at[3]),
        pltpu.make_async_copy(bl, lo_hbm, sems.at[4]),
    ]
    for store in stores:
        store.start()
    for n in range(2):
        cols = slice(256 * n, 256 * (n + 1))
        part = -three_pass(ah[...], al[...], bh[:, cols], bl[:, cols])
        out[2 * n] = part[:, :128]
        out[2 * n + 1] = part[:, 128:]
        pair = slice(2 * n, 2 * n + 2)
        stores.append(pltpu.make_async_copy(out.at[pair], out_hbm.at[pair], sems.at[5 + n]))
        stores[-1].start()
    for store in stores:
        store.wait()


def side(at, sigma, lower):
    return pl.pallas_call(
        side_kernel,
        out_shape=(shape(4, 256, 128),) + (shape(1024, 512, dtype=BF16),) * 2,
        in_specs=[SMEM, HBM, HBM],
        out_specs=(HBM,) * 3,
        scratch_shapes=[
            pltpu.VMEM((8, 256, 128), F32),
            pltpu.VMEM((16, 256, 128), F32),
            pltpu.VMEM((256, 1024), BF16),
            pltpu.VMEM((256, 1024), BF16),
            pltpu.VMEM((1024, 512), BF16),
            pltpu.VMEM((1024, 512), BF16),
            pltpu.VMEM((4, 256, 128), F32),
            DMA((7,)),
        ],
        compiler_params=WIDE,
        cost_estimate=pl.CostEstimate(flops=6 << 28, bytes_accessed=6 << 20, transcendentals=0),
    )(at, sigma, lower)


def last_kernel(at_ref, w_hbm, hi_hbm, lo_hbm, out_hbm, w, ah, al, bh, bl, out, sems):
    loads = [
        pltpu.make_async_copy(w_hbm, w, sems.at[0]),
        pltpu.make_async_copy(hi_hbm, bh, sems.at[1]),
        pltpu.make_async_copy(lo_hbm, bl, sems.at[2]),
    ]
    for load in loads:
        load.start()
    core = device(at_ref)[2]
    loads[0].wait()
    for z in range(8):
        rows = slice(128 * z, 128 * (z + 1))
        ah[:, rows], al[:, rows] = split2(w[z ^ (4 * core)])
    for load in loads[1:]:
        load.wait()
    stores = []
    for n in range(2):
        cols = slice(256 * n, 256 * (n + 1))
        part = three_pass(ah[...], al[...], bh[:, cols], bl[:, cols])
        out[2 * n] = part[:, :128]
        out[2 * n + 1] = part[:, 128:]
        pair, place = slice(2 * n, 2 * n + 2), pl.ds(2 * (n ^ core), 2)
        stores.append(pltpu.make_async_copy(out.at[pair], out_hbm.at[place], sems.at[3 + n]))
        stores[-1].start()
    for store in stores:
        store.wait()


def last(at, w, hi, lo):
    return pl.pallas_call(
        last_kernel,
        out_shape=shape(4, 256, 128),
        in_specs=[SMEM] + [HBM] * 3,
        out_specs=HBM,
        scratch_shapes=[
            pltpu.VMEM((8, 256, 128), F32),
            pltpu.VMEM((256, 1024), BF16),
            pltpu.VMEM((256, 1024), BF16),
            pltpu.VMEM((1024, 512), BF16),
            pltpu.VMEM((1024, 512), BF16),
            pltpu.VMEM((4, 256, 128), F32),
            DMA((5,)),
        ],
        compiler_params=MIDDLE,
    )(at, w, hi, lo)


def exchange(v, axis, size):
    axes = (axis, "c") if axis == "y" else ("c", axis)
    groups = [
        [2 * p + c if axis == "y" else size * c + p for p in (i ^ (size // 2 * c) for i in range(size))]
        for c in range(2)
    ]
    return lax.all_to_all(v, axes, 0, 0, tiled=True, axis_index_groups=groups)


def deal(v, t):
    moves = [(4 * c + x, 4 * (x >> 1) + 2 * c + ((x & 1) ^ t)) for c in range(2) for x in range(4)]
    return lax.ppermute(v, ("c", "x"), moves)


def flip(v, axis, size, k):
    return lax.ppermute(v, axis, [(i, i ^ k) for i in range(size)])


def shards(root_inverse, boundary_map, lower_factor, upper_factor, diagonal_inverse):
    at = lax.axis_index(("y", "c", "z", "x")).astype(jnp.int32).reshape(1)
    upper = lax.all_gather(upper_factor, "z", axis=0, tiled=False)
    sigma, first, second = pick(at, boundary_map.reshape(32, 128), root_inverse)
    copies = fan(deal(first, 0), deal(second, 1))
    copies, lower, sigma = lax.optimization_barrier((copies, lower_factor, sigma))
    odd = lax.axis_index("x") & 1
    lower = [
        deal(lax.dynamic_slice_in_dim(lower, 128 * (odd ^ t), 128), t) for t in range(2)
    ]
    lower = lax.all_gather(jnp.concatenate(lower, axis=0), ("y", "c"), axis=0, tiled=False)
    own = exchange(copies, "y", 8)
    sigma = sigma[None]
    for k in (4, 2):
        sigma = jnp.concatenate([sigma, flip(sigma, "z", 8, k)], axis=0)
    own, sigma = lax.optimization_barrier((own, sigma))
    other = flip(own, "c", 2, 1)
    sigma = jnp.concatenate([sigma, flip(sigma, "z", 8, 1)], axis=0)
    part = exchange(couple(at, upper, other, couple(at, upper, own)), "x", 4)
    part, sigma = lax.optimization_barrier((part, sigma))
    w = part.sum(axis=0)
    w_all = exchange(jnp.broadcast_to(w[None], (8, 256, 128)), "z", 8)
    sides, hi, lo = side(at, sigma, lower)
    t = lax.psum_scatter(sides, "x", scatter_dimension=0, tiled=False)
    product = exchange(last(at, w_all, hi, lo), "x", 4).sum(axis=0)
    return (t, -w, diagonal_inverse + product)


def solution(mesh):
    grid = Mesh(np.asarray(mesh.devices).reshape(8, 2, 8, 4), ("y", "c", "z", "x"))
    block = P(("y", "c"), ("z", "x"))
    return jax.shard_map(
        shards,
        mesh=grid,
        in_specs=(block, P(), block, block, block),
        out_specs=(block, block, block),
        check_vma=False,
    )
```

```python
import jax
import jax.numpy as jnp
import numpy as np
from jax import lax
from jax.experimental import pallas as pl
from jax.experimental.pallas import tpu as pltpu
from jax.sharding import Mesh, PartitionSpec as P

F32 = jnp.float32
BF16 = jnp.bfloat16
VMEM = pl.BlockSpec(memory_space=pltpu.VMEM)
SMEM = pl.BlockSpec(memory_space=pltpu.SMEM)
HBM = pl.BlockSpec(memory_space=pltpu.HBM)
PARAMS = pltpu.CompilerParams(vmem_limit_bytes=32 * 1024 * 1024)
WIDE = pltpu.CompilerParams(vmem_limit_bytes=62 * 1024 * 1024)
NEAR = pltpu.CompilerParams(vmem_limit_bytes=51 * 1024 * 1024)
MIDDLE = pltpu.CompilerParams(vmem_limit_bytes=52 * 1024 * 1024)
DMA = pltpu.SemaphoreType.DMA


def shape(*dims, dtype=F32):
    return jax.ShapeDtypeStruct(dims, dtype)


def split2(v):
    hi = v.astype(BF16)
    return hi, (v - hi.astype(F32)).astype(BF16)


def dot(a, b):
    return lax.dot_general(a, b, (((1,), (0,)), ((), ())), preferred_element_type=F32)


def three_pass(ah, al, bh, bl):
    return dot(ah, bh) + (dot(ah, bl) + dot(al, bh))


def device(ref):
    number = ref[0]
    return number >> 5, number & 31, (number >> 5) & 1, (number >> 2) & 7, number & 3


def pick_kernel(
    at_ref, map_hbm, root_hbm, upper_hbm, su_ref, first_ref, second_ref, picks, root, sems
):
    loads = [
        pltpu.make_async_copy(map_hbm, picks, sems.at[0]),
        pltpu.make_async_copy(root_hbm, root, sems.at[1]),
        pltpu.make_async_copy(upper_hbm, su_ref.at[256:512], sems.at[2]),
    ]
    for load in loads:
        load.start()
    row, col, _, _, x = device(at_ref)
    odd = x & 1
    iota = lax.broadcasted_iota(jnp.int32, (256, 128), 0)
    loads[0].wait()
    cols = picks[pl.ds(col, 1), :] - 256 * col
    col_hot = jnp.where(cols == iota, 1.0, 0.0).astype(BF16)
    hots = []
    for part in range(2):
        block = 2 * row + part
        rows = picks[pl.ds(block, 1), :] - 256 * block
        hots.append(jnp.where(rows == iota, 1.0, 0.0).astype(BF16))
    loads[1].wait()
    stack = []
    for part in range(2):
        left = root[256 * part : 256 * (part + 1), :]
        pieces = []
        for _ in range(3):
            piece = left.astype(BF16)
            left = left - piece.astype(F32)
            pieces.append(piece)
        across = lax.dot_general(
            hots[part],
            jnp.concatenate(pieces, axis=1),
            (((0,), (0,)), ((), ())),
            preferred_element_type=F32,
        ).astype(BF16)
        stack += [across[:, 256 * i : 256 * (i + 1)] for i in range(3)]
    value = dot(jnp.concatenate(stack, axis=0), col_hot)
    for part in range(2):
        v = [value[128 * (3 * part + i) : 128 * (3 * part + i + 1), :] for i in range(3)]
        su_ref[128 * part : 128 * (part + 1), :] = (v[0] + v[1]) + v[2]
    loads[2].wait()
    near = pl.multiple_of(128 * odd, 128)
    far = pl.multiple_of(128 - 128 * odd, 128)
    first_ref[...] = su_ref[pl.ds(near, 128), :]
    second_ref[...] = su_ref[pl.ds(far, 128), :]


def pick(at, blocks, root, upper):
    return pl.pallas_call(
        pick_kernel,
        out_shape=(shape(512, 128), shape(128, 128), shape(128, 128)),
        in_specs=[SMEM] + [HBM] * 3,
        out_specs=(VMEM, VMEM, VMEM),
        scratch_shapes=[
            pltpu.VMEM((32, 128), jnp.int32),
            pltpu.VMEM((512, 256), F32),
            DMA((3,)),
        ],
        compiler_params=WIDE,
    )(at, blocks, root, upper)


def fan_kernel(first_ref, second_ref, copies_ref):
    for t, ref in enumerate((first_ref, second_ref)):
        value = ref[...]
        for i in range(8):
            copies_ref[i, t] = value


def fan(first, second):
    return pl.pallas_call(
        fan_kernel,
        out_shape=shape(8, 2, 128, 128),
        in_specs=[VMEM] * 2,
        out_specs=VMEM,
        compiler_params=PARAMS,
    )(first, second)


def couple_kernel(
    at_ref, gathered_hbm, own_hbm, other_hbm, out_ref, left, own, other, ah, al, bh, bl, sems
):
    loads = [
        pltpu.make_async_copy(own_hbm, own, sems.at[0]),
        pltpu.make_async_copy(other_hbm, other, sems.at[1]),
        pltpu.make_async_copy(gathered_hbm.at[:, 256:512], left, sems.at[2]),
    ]
    for load in loads:
        load.start()
    _, _, core, _, x = device(at_ref)
    odd = x & 1
    for n, right in enumerate((own, other)):
        loads[n].wait()
        side = core if n == 0 else 1 - core
        for z in range(8):
            rows = slice(128 * z, 128 * (z + 1))
            for t in range(2):
                cols = slice(256 * n + 128 * t, 256 * n + 128 * (t + 1))
                bh[rows, cols], bl[rows, cols] = split2(right[z ^ (4 * side), t])
    loads[2].wait()
    for z in range(8):
        rows = slice(128 * z, 128 * (z + 1))
        ah[:, rows], al[:, rows] = split2(left[z ^ (4 * core)])
    for n in range(2):
        cols = slice(256 * n, 256 * (n + 1))
        part = three_pass(ah[...], al[...], bh[:, cols], bl[:, cols])
        out_ref[2 * n + odd] = part[:, :128]
        out_ref[2 * n + 1 - odd] = part[:, 128:]


def couple(at, gathered, own, other):
    return pl.pallas_call(
        couple_kernel,
        out_shape=shape(4, 256, 128),
        in_specs=[SMEM, HBM, HBM, HBM],
        out_specs=VMEM,
        scratch_shapes=[
            pltpu.VMEM((8, 256, 128), F32),
            pltpu.VMEM((8, 2, 128, 128), F32),
            pltpu.VMEM((8, 2, 128, 128), F32),
            pltpu.VMEM((256, 1024), BF16),
            pltpu.VMEM((256, 1024), BF16),
            pltpu.VMEM((1024, 512), BF16),
            pltpu.VMEM((1024, 512), BF16),
            DMA((3,)),
        ],
        compiler_params=NEAR,
        cost_estimate=pl.CostEstimate(flops=6 << 28, bytes_accessed=3 << 20, transcendentals=0),
    )(at, gathered, own, other)


def side_kernel(
    at_ref, su_hbm, lower_hbm, out_hbm, hi_hbm, lo_hbm, sigma, lower, ah, al, bh, bl, out, sems
):
    loads = [pltpu.make_async_copy(su_hbm.at[:, 0:256], sigma, sems.at[0])]
    for i in range(2):
        rows = slice(4 * i, 4 * (i + 1))
        loads.append(
            pltpu.make_async_copy(lower_hbm.at[:, rows], lower.at[:, rows], sems.at[1 + i])
        )
    for load in loads:
        load.start()
    _, _, core_at, _, x = device(at_ref)
    odd = x & 1
    loads[0].wait()
    for z in range(8):
        rows = slice(128 * z, 128 * (z + 1))
        ah[:, rows], al[:, rows] = split2(sigma[z ^ (4 * core_at)])
    for z in range(8):
        if z % 4 == 0:
            loads[1 + z // 4].wait()
        rows = slice(128 * z, 128 * (z + 1))
        for core in range(2):
            for t in range(2):
                cols = slice(256 * core + 128 * t, 256 * core + 128 * (t + 1))
                place = 128 * (odd if t == 0 else 1 - odd)
                value = lower[core, z, pl.ds(pl.multiple_of(place, 128), 128), :]
                bh[rows, cols], bl[rows, cols] = split2(value)
    stores = [
        pltpu.make_async_copy(bh, hi_hbm, sems.at[3]),
        pltpu.make_async_copy(bl, lo_hbm, sems.at[4]),
    ]
    for store in stores:
        store.start()
    for n in range(2):
        cols = slice(256 * n, 256 * (n + 1))
        part = -three_pass(ah[...], al[...], bh[:, cols], bl[:, cols])
        out[2 * n] = part[:, :128]
        out[2 * n + 1] = part[:, 128:]
        pair, place = slice(2 * n, 2 * n + 2), pl.ds(2 * (n ^ core_at), 2)
        stores.append(pltpu.make_async_copy(out.at[pair], out_hbm.at[place], sems.at[5 + n]))
        stores[-1].start()
    for store in stores:
        store.wait()


def side(at, gathered, lower):
    return pl.pallas_call(
        side_kernel,
        out_shape=(shape(4, 256, 128),) + (shape(1024, 512, dtype=BF16),) * 2,
        in_specs=[SMEM, HBM, HBM],
        out_specs=(HBM,) * 3,
        scratch_shapes=[
            pltpu.VMEM((8, 256, 128), F32),
            pltpu.VMEM((2, 8, 256, 128), F32),
            pltpu.VMEM((256, 1024), BF16),
            pltpu.VMEM((256, 1024), BF16),
            pltpu.VMEM((1024, 512), BF16),
            pltpu.VMEM((1024, 512), BF16),
            pltpu.VMEM((4, 256, 128), F32),
            DMA((7,)),
        ],
        compiler_params=WIDE,
        cost_estimate=pl.CostEstimate(flops=6 << 28, bytes_accessed=6 << 20, transcendentals=0),
    )(at, gathered, lower)


def last_kernel(at_ref, w_hbm, hi_hbm, lo_hbm, out_hbm, w, ah, al, bh, bl, out, sems):
    loads = [
        pltpu.make_async_copy(w_hbm, w, sems.at[0]),
        pltpu.make_async_copy(hi_hbm, bh, sems.at[1]),
        pltpu.make_async_copy(lo_hbm, bl, sems.at[2]),
    ]
    for load in loads:
        load.start()
    core = device(at_ref)[2]
    loads[0].wait()
    for z in range(8):
        rows = slice(128 * z, 128 * (z + 1))
        ah[:, rows], al[:, rows] = split2(w[z ^ (4 * core)])
    for load in loads[1:]:
        load.wait()
    stores = []
    for n in range(2):
        cols = slice(256 * n, 256 * (n + 1))
        part = three_pass(ah[...], al[...], bh[:, cols], bl[:, cols])
        out[2 * n] = part[:, :128]
        out[2 * n + 1] = part[:, 128:]
        pair, place = slice(2 * n, 2 * n + 2), pl.ds(2 * (n ^ core), 2)
        stores.append(pltpu.make_async_copy(out.at[pair], out_hbm.at[place], sems.at[3 + n]))
        stores[-1].start()
    for store in stores:
        store.wait()


def last(at, w, hi, lo):
    return pl.pallas_call(
        last_kernel,
        out_shape=shape(4, 256, 128),
        in_specs=[SMEM] + [HBM] * 3,
        out_specs=HBM,
        scratch_shapes=[
            pltpu.VMEM((8, 256, 128), F32),
            pltpu.VMEM((256, 1024), BF16),
            pltpu.VMEM((256, 1024), BF16),
            pltpu.VMEM((1024, 512), BF16),
            pltpu.VMEM((1024, 512), BF16),
            pltpu.VMEM((4, 256, 128), F32),
            DMA((5,)),
        ],
        compiler_params=MIDDLE,
    )(at, w, hi, lo)


def rotated(axis, size):
    axes = (axis, "c") if axis == "y" else ("c", axis)
    groups = [
        [2 * p + c if axis == "y" else size * c + p for p in (i ^ (size // 2 * c) for i in range(size))]
        for c in range(2)
    ]
    return axes, groups


def exchange(v, axis, size):
    axes, groups = rotated(axis, size)
    return lax.all_to_all(v, axes, 0, 0, tiled=True, axis_index_groups=groups)


def deal(v, t):
    moves = [(4 * c + x, 4 * (x >> 1) + 2 * c + ((x & 1) ^ t)) for c in range(2) for x in range(4)]
    return lax.ppermute(v, ("c", "x"), moves)


def turn(v, axis, size, k):
    return lax.ppermute(v, axis, [(i, (i + k) % size) for i in range(size)])


def shards(root_inverse, boundary_map, lower_factor, upper_factor, diagonal_inverse):
    at = lax.axis_index(("y", "c", "z", "x")).astype(jnp.int32).reshape(1)
    su, first, second = pick(at, boundary_map.reshape(32, 128), root_inverse, upper_factor)
    axes, groups = rotated("z", 8)
    gathered = lax.all_gather(su, axes, axis=0, tiled=False, axis_index_groups=groups)
    copies = fan(deal(first, 0), deal(second, 1))
    copies, lower = lax.optimization_barrier((copies, lower_factor))
    odd = lax.axis_index("x") & 1
    lower = [
        deal(lax.dynamic_slice_in_dim(lower, 128 * (odd ^ t), 128), t) for t in range(2)
    ]
    lower = jnp.concatenate(lower, axis=0)
    groups = [[2 * i + core for core in range(2) for i in range(8)]]
    lower = lax.all_gather(lower, ("y", "c"), axis=0, tiled=False, axis_index_groups=groups)
    lower = lower.reshape(2, 8, 256, 128)
    own = exchange(copies, "y", 8)
    other = turn(own, "c", 2, 1)
    part = couple(at, gathered, own, other)
    w = exchange(part, "x", 4).sum(axis=0)
    w_all = exchange(jnp.broadcast_to(w[None], (8, 256, 128)), "z", 8)
    sides, hi, lo = side(at, gathered, lower)
    axes, groups = rotated("x", 4)
    t = lax.psum_scatter(
        sides.reshape(1024, 128), axes, scatter_dimension=0, tiled=True, axis_index_groups=groups
    )
    product = exchange(last(at, w_all, hi, lo), "x", 4).sum(axis=0)
    return (t, -w, diagonal_inverse + product)


def solution(mesh):
    grid = Mesh(np.asarray(mesh.devices).reshape(8, 2, 8, 4), ("y", "c", "z", "x"))
    block = P(("y", "c"), ("z", "x"))
    return jax.shard_map(
        shards,
        mesh=grid,
        in_specs=(block, P(), block, block, block),
        out_specs=(block, block, block),
        check_vma=False,
    )
```

```python
import jax
import jax.numpy as jnp
import numpy as np
from jax import lax
from jax.experimental import pallas as pl
from jax.experimental.pallas import tpu as pltpu
from jax.sharding import Mesh, PartitionSpec as P

F32 = jnp.float32
BF16 = jnp.bfloat16
VMEM = pl.BlockSpec(memory_space=pltpu.VMEM)
SMEM = pl.BlockSpec(memory_space=pltpu.SMEM)
HBM = pl.BlockSpec(memory_space=pltpu.HBM)
PARAMS = pltpu.CompilerParams(vmem_limit_bytes=32 * 1024 * 1024)
WIDE = pltpu.CompilerParams(vmem_limit_bytes=62 * 1024 * 1024)
NEAR = pltpu.CompilerParams(vmem_limit_bytes=51 * 1024 * 1024)
MIDDLE = pltpu.CompilerParams(vmem_limit_bytes=52900 * 1024)
DMA = pltpu.SemaphoreType.DMA


def shape(*dims, dtype=F32):
    return jax.ShapeDtypeStruct(dims, dtype)


def split2(v):
    hi = v.astype(BF16)
    return hi, (v - hi.astype(F32)).astype(BF16)


def dot(a, b):
    return lax.dot_general(a, b, (((1,), (0,)), ((), ())), preferred_element_type=F32)


def three_pass(ah, al, bh, bl):
    return dot(ah, bh) + (dot(ah, bl) + dot(al, bh))


def device(ref):
    number = ref[0]
    return number >> 5, number & 31, (number >> 5) & 1, (number >> 2) & 7, number & 3


def pick_kernel(
    at_ref, map_hbm, root_hbm, upper_hbm, su_ref, first_ref, second_ref, picks, root, sems
):
    loads = [
        pltpu.make_async_copy(map_hbm, picks, sems.at[0]),
        pltpu.make_async_copy(root_hbm, root, sems.at[1]),
        pltpu.make_async_copy(upper_hbm, su_ref.at[256:512], sems.at[2]),
    ]
    for load in loads:
        load.start()
    row, col, _, _, x = device(at_ref)
    odd = x & 1
    iota = lax.broadcasted_iota(jnp.int32, (256, 128), 0)
    loads[0].wait()
    cols = picks[pl.ds(col, 1), :] - 256 * col
    col_hot = jnp.where(cols == iota, 1.0, 0.0).astype(BF16)
    hots = []
    for part in range(2):
        block = 2 * row + part
        rows = picks[pl.ds(block, 1), :] - 256 * block
        hots.append(jnp.where(rows == iota, 1.0, 0.0).astype(BF16))
    loads[1].wait()
    stack = []
    for part in range(2):
        left = root[256 * part : 256 * (part + 1), :]
        pieces = []
        for _ in range(3):
            piece = left.astype(BF16)
            left = left - piece.astype(F32)
            pieces.append(piece)
        across = lax.dot_general(
            hots[part],
            jnp.concatenate(pieces, axis=1),
            (((0,), (0,)), ((), ())),
            preferred_element_type=F32,
        ).astype(BF16)
        stack += [across[:, 256 * i : 256 * (i + 1)] for i in range(3)]
    value = dot(jnp.concatenate(stack, axis=0), col_hot)
    for part in range(2):
        v = [value[128 * (3 * part + i) : 128 * (3 * part + i + 1), :] for i in range(3)]
        su_ref[128 * part : 128 * (part + 1), :] = (v[0] + v[1]) + v[2]
    loads[2].wait()
    near = pl.multiple_of(128 * odd, 128)
    far = pl.multiple_of(128 - 128 * odd, 128)
    first_ref[...] = su_ref[pl.ds(near, 128), :]
    second_ref[...] = su_ref[pl.ds(far, 128), :]


def pick(at, blocks, root, upper):
    return pl.pallas_call(
        pick_kernel,
        out_shape=(shape(512, 128), shape(128, 128), shape(128, 128)),
        in_specs=[SMEM] + [HBM] * 3,
        out_specs=(VMEM, VMEM, VMEM),
        scratch_shapes=[
            pltpu.VMEM((32, 128), jnp.int32),
            pltpu.VMEM((512, 256), F32),
            DMA((3,)),
        ],
        compiler_params=WIDE,
    )(at, blocks, root, upper)


def fan_kernel(first_ref, second_ref, copies_ref):
    for t, ref in enumerate((first_ref, second_ref)):
        value = ref[...]
        for i in range(8):
            copies_ref[i, t] = value


def fan(first, second):
    return pl.pallas_call(
        fan_kernel,
        out_shape=shape(8, 2, 128, 128),
        in_specs=[VMEM] * 2,
        out_specs=VMEM,
        compiler_params=PARAMS,
    )(first, second)


def couple_kernel(
    at_ref, gathered_hbm, own_hbm, other_hbm, out_ref, left, own, other, ah, al, bh, bl, sems
):
    loads = [
        pltpu.make_async_copy(own_hbm, own, sems.at[0]),
        pltpu.make_async_copy(other_hbm, other, sems.at[1]),
        pltpu.make_async_copy(gathered_hbm.at[:, 256:512], left, sems.at[2]),
    ]
    for load in loads:
        load.start()
    _, _, core, _, x = device(at_ref)
    odd = x & 1
    for n, right in enumerate((own, other)):
        loads[n].wait()
        side = core if n == 0 else 1 - core
        for z in range(8):
            rows = slice(128 * z, 128 * (z + 1))
            for t in range(2):
                cols = slice(256 * n + 128 * t, 256 * n + 128 * (t + 1))
                bh[rows, cols], bl[rows, cols] = split2(right[z ^ (4 * side), t])
    loads[2].wait()
    for z in range(8):
        rows = slice(128 * z, 128 * (z + 1))
        ah[:, rows], al[:, rows] = split2(left[z ^ (4 * core)])
    for n in range(2):
        cols = slice(256 * n, 256 * (n + 1))
        part = three_pass(ah[...], al[...], bh[:, cols], bl[:, cols])
        out_ref[2 * n + odd] = part[:, :128]
        out_ref[2 * n + 1 - odd] = part[:, 128:]


def couple(at, gathered, own, other):
    return pl.pallas_call(
        couple_kernel,
        out_shape=shape(4, 256, 128),
        in_specs=[SMEM, HBM, HBM, HBM],
        out_specs=VMEM,
        scratch_shapes=[
            pltpu.VMEM((8, 256, 128), F32),
            pltpu.VMEM((8, 2, 128, 128), F32),
            pltpu.VMEM((8, 2, 128, 128), F32),
            pltpu.VMEM((256, 1024), BF16),
            pltpu.VMEM((256, 1024), BF16),
            pltpu.VMEM((1024, 512), BF16),
            pltpu.VMEM((1024, 512), BF16),
            DMA((3,)),
        ],
        compiler_params=NEAR,
        cost_estimate=pl.CostEstimate(flops=6 << 28, bytes_accessed=3 << 20, transcendentals=0),
    )(at, gathered, own, other)


def side_kernel(
    at_ref, su_hbm, lower_hbm, top_hbm, rest_hbm, hi_hbm, lo_hbm, sigma, lower, ah, al, bh, bl, out, sems
):
    loads = [pltpu.make_async_copy(su_hbm.at[:, 0:256], sigma, sems.at[0])]
    for n in range(2):
        loads.append(pltpu.make_async_copy(lower_hbm.at[n], lower.at[n], sems.at[1 + n]))
    for load in loads:
        load.start()
    _, _, core, _, x = device(at_ref)
    odd = x & 1
    loads[0].wait()
    for z in range(8):
        rows = slice(128 * z, 128 * (z + 1))
        ah[:, rows], al[:, rows] = split2(sigma[z ^ (4 * core)])
    stores = []
    for n in range(2):
        loads[1 + n].wait()
        for z in range(8):
            rows = slice(128 * z, 128 * (z + 1))
            for t in range(2):
                cols = slice(128 * t, 128 * (t + 1))
                place = 128 * (odd if t == 0 else 1 - odd)
                value = lower[n, z, pl.ds(pl.multiple_of(place, 128), 128), :]
                bh[n, rows, cols], bl[n, rows, cols] = split2(value)
        stores.append(pltpu.make_async_copy(bh.at[n], hi_hbm.at[n], sems.at[3 + n]))
        stores.append(pltpu.make_async_copy(bl.at[n], lo_hbm.at[n], sems.at[5 + n]))
        part = -three_pass(ah[...], al[...], bh[n], bl[n])
        out[2 * n] = part[:, :128]
        out[2 * n + 1] = part[:, 128:]
        pair, place = slice(2 * n, 2 * n + 2), pl.ds(2 * (n ^ core), 2)
        stores.append(
            pltpu.make_async_copy(out.at[pair, 0:128], top_hbm.at[place], sems.at[7 + n])
        )
        stores.append(
            pltpu.make_async_copy(out.at[pair, 128:256], rest_hbm.at[place], sems.at[9 + n])
        )
        for store in stores[4 * n :]:
            store.start()
    for store in stores:
        store.wait()


def side(at, gathered, lower):
    return pl.pallas_call(
        side_kernel,
        out_shape=(shape(4, 128, 128),) * 2 + (shape(2, 1024, 256, dtype=BF16),) * 2,
        in_specs=[SMEM, HBM, HBM],
        out_specs=(HBM,) * 4,
        scratch_shapes=[
            pltpu.VMEM((8, 256, 128), F32),
            pltpu.VMEM((2, 8, 256, 128), F32),
            pltpu.VMEM((256, 1024), BF16),
            pltpu.VMEM((256, 1024), BF16),
            pltpu.VMEM((2, 1024, 256), BF16),
            pltpu.VMEM((2, 1024, 256), BF16),
            pltpu.VMEM((4, 256, 128), F32),
            DMA((11,)),
        ],
        compiler_params=WIDE,
        cost_estimate=pl.CostEstimate(flops=6 << 28, bytes_accessed=6 << 20, transcendentals=0),
    )(at, gathered, lower)


def last_kernel(at_ref, w_hbm, hi_hbm, lo_hbm, rest_hbm, out_hbm, w, ah, al, bh, bl, out, sems):
    rest = pltpu.make_async_copy(rest_hbm, out_hbm.at[:, 256:384], sems.at[7])
    loads = [pltpu.make_async_copy(w_hbm, w, sems.at[0])]
    for n in range(2):
        loads.append(pltpu.make_async_copy(hi_hbm.at[n], bh.at[n], sems.at[1 + n]))
        loads.append(pltpu.make_async_copy(lo_hbm.at[n], bl.at[n], sems.at[3 + n]))
    for load in loads + [rest]:
        load.start()
    core = device(at_ref)[2]
    loads[0].wait()
    for z in range(8):
        rows = slice(128 * z, 128 * (z + 1))
        ah[:, rows], al[:, rows] = split2(w[z ^ (4 * core)])
    stores = [rest]
    for n in range(2):
        for load in loads[1 + 2 * n : 3 + 2 * n]:
            load.wait()
        part = three_pass(ah[...], al[...], bh[n], bl[n])
        out[2 * n] = part[:, :128]
        out[2 * n + 1] = part[:, 128:]
        pair, place = slice(2 * n, 2 * n + 2), pl.ds(2 * (n ^ core), 2)
        stores.append(
            pltpu.make_async_copy(out.at[pair], out_hbm.at[place, 0:256], sems.at[5 + n])
        )
        stores[-1].start()
    for store in stores:
        store.wait()


def last(at, w, hi, lo, rest):
    return pl.pallas_call(
        last_kernel,
        out_shape=shape(4, 384, 128),
        in_specs=[SMEM] + [HBM] * 4,
        out_specs=HBM,
        scratch_shapes=[
            pltpu.VMEM((8, 256, 128), F32),
            pltpu.VMEM((256, 1024), BF16),
            pltpu.VMEM((256, 1024), BF16),
            pltpu.VMEM((2, 1024, 256), BF16),
            pltpu.VMEM((2, 1024, 256), BF16),
            pltpu.VMEM((4, 256, 128), F32),
            DMA((8,)),
        ],
        compiler_params=MIDDLE,
    )(at, w, hi, lo, rest)


def rotated(axis, size):
    axes = (axis, "c") if axis == "y" else ("c", axis)
    groups = [
        [2 * p + c if axis == "y" else size * c + p for p in (i ^ (size // 2 * c) for i in range(size))]
        for c in range(2)
    ]
    return axes, groups


def exchange(v, axis, size):
    axes, groups = rotated(axis, size)
    return lax.all_to_all(v, axes, 0, 0, tiled=True, axis_index_groups=groups)


def deal(v, t):
    moves = [(4 * c + x, 4 * (x >> 1) + 2 * c + ((x & 1) ^ t)) for c in range(2) for x in range(4)]
    return lax.ppermute(v, ("c", "x"), moves)


def turn(v, axis, size, k):
    return lax.ppermute(v, axis, [(i, (i + k) % size) for i in range(size)])


def shards(root_inverse, boundary_map, lower_factor, upper_factor, diagonal_inverse):
    at = lax.axis_index(("y", "c", "z", "x")).astype(jnp.int32).reshape(1)
    su, first, second = pick(at, boundary_map.reshape(32, 128), root_inverse, upper_factor)
    axes, groups = rotated("z", 8)
    gathered = lax.all_gather(su, axes, axis=0, tiled=False, axis_index_groups=groups)
    copies = fan(deal(first, 0), deal(second, 1))
    copies, lower = lax.optimization_barrier((copies, lower_factor))
    odd = lax.axis_index("x") & 1
    lower = [
        deal(lax.dynamic_slice_in_dim(lower, 128 * (odd ^ t), 128), t) for t in range(2)
    ]
    lower = jnp.concatenate(lower, axis=0)
    groups = [[2 * i + core for core in range(2) for i in range(8)]]
    lower = lax.all_gather(lower, ("y", "c"), axis=0, tiled=False, axis_index_groups=groups)
    lower = lower.reshape(2, 8, 256, 128)
    own = exchange(copies, "y", 8)
    other = turn(own, "c", 2, 1)
    part = couple(at, gathered, own, other)
    w = exchange(part, "x", 4).sum(axis=0)
    w_all = exchange(jnp.broadcast_to(w[None], (8, 256, 128)), "z", 8)
    top, rest, hi, lo = side(at, gathered, lower)
    axes, groups = rotated("x", 4)
    top = lax.psum_scatter(
        top.reshape(512, 128), axes, scatter_dimension=0, tiled=True, axis_index_groups=groups
    )
    sums = exchange(last(at, w_all, hi, lo, rest), "x", 4).sum(axis=0)
    return (jnp.concatenate([top, sums[256:]], axis=0), -w, diagonal_inverse + sums[:256])


def solution(mesh):
    grid = Mesh(np.asarray(mesh.devices).reshape(8, 2, 8, 4), ("y", "c", "z", "x"))
    block = P(("y", "c"), ("z", "x"))
    return jax.shard_map(
        shards,
        mesh=grid,
        in_specs=(block, P(), block, block, block),
        out_specs=(block, block, block),
        check_vma=False,
    )
```

```python
import jax
import jax.numpy as jnp
import numpy as np
from jax import lax
from jax.experimental import pallas as pl
from jax.experimental.pallas import tpu as pltpu
from jax.sharding import Mesh, PartitionSpec as P

F32 = jnp.float32
BF16 = jnp.bfloat16
VMEM = pl.BlockSpec(memory_space=pltpu.VMEM)
SMEM = pl.BlockSpec(memory_space=pltpu.SMEM)
HBM = pl.BlockSpec(memory_space=pltpu.HBM)
PARAMS = pltpu.CompilerParams(vmem_limit_bytes=32 * 1024 * 1024)
WIDE = pltpu.CompilerParams(vmem_limit_bytes=62 * 1024 * 1024)
NEAR = pltpu.CompilerParams(vmem_limit_bytes=51 * 1024 * 1024)
MIDDLE = pltpu.CompilerParams(vmem_limit_bytes=51 * 1024 * 1024)
DMA = pltpu.SemaphoreType.DMA


def shape(*dims, dtype=F32):
    return jax.ShapeDtypeStruct(dims, dtype)


def split2(v):
    hi = v.astype(BF16)
    return hi, (v - hi.astype(F32)).astype(BF16)


def dot(a, b):
    return lax.dot_general(a, b, (((1,), (0,)), ((), ())), preferred_element_type=F32)


def three_pass(ah, al, bh, bl):
    return dot(ah, bh) + (dot(ah, bl) + dot(al, bh))


def device(ref):
    number = ref[0]
    return number >> 5, number & 31, (number >> 5) & 1, (number >> 2) & 7, number & 3


def pick_kernel(
    at_ref, map_hbm, root_hbm, upper_hbm, su_ref, first_ref, second_ref, picks, root, sems
):
    loads = [
        pltpu.make_async_copy(map_hbm, picks, sems.at[0]),
        pltpu.make_async_copy(root_hbm, root, sems.at[1]),
        pltpu.make_async_copy(upper_hbm, su_ref.at[256:512], sems.at[2]),
    ]
    for load in loads:
        load.start()
    row, col, _, _, x = device(at_ref)
    odd = x & 1
    iota = lax.broadcasted_iota(jnp.int32, (256, 128), 0)
    loads[0].wait()
    cols = picks[pl.ds(col, 1), :] - 256 * col
    col_hot = jnp.where(cols == iota, 1.0, 0.0).astype(BF16)
    hots = []
    for part in range(2):
        block = 2 * row + part
        rows = picks[pl.ds(block, 1), :] - 256 * block
        hots.append(jnp.where(rows == iota, 1.0, 0.0).astype(BF16))
    loads[1].wait()
    stack = []
    for part in range(2):
        left = root[256 * part : 256 * (part + 1), :]
        pieces = []
        for _ in range(3):
            piece = left.astype(BF16)
            left = left - piece.astype(F32)
            pieces.append(piece)
        across = lax.dot_general(
            hots[part],
            jnp.concatenate(pieces, axis=1),
            (((0,), (0,)), ((), ())),
            preferred_element_type=F32,
        ).astype(BF16)
        stack += [across[:, 256 * i : 256 * (i + 1)] for i in range(3)]
    value = dot(jnp.concatenate(stack, axis=0), col_hot)
    for part in range(2):
        v = [value[128 * (3 * part + i) : 128 * (3 * part + i + 1), :] for i in range(3)]
        su_ref[128 * part : 128 * (part + 1), :] = (v[0] + v[1]) + v[2]
    loads[2].wait()
    near = pl.multiple_of(128 * odd, 128)
    far = pl.multiple_of(128 - 128 * odd, 128)
    first_ref[...] = su_ref[pl.ds(near, 128), :]
    second_ref[...] = su_ref[pl.ds(far, 128), :]


def pick(at, blocks, root, upper):
    return pl.pallas_call(
        pick_kernel,
        out_shape=(shape(512, 128), shape(128, 128), shape(128, 128)),
        in_specs=[SMEM] + [HBM] * 3,
        out_specs=(VMEM, VMEM, VMEM),
        scratch_shapes=[
            pltpu.VMEM((32, 128), jnp.int32),
            pltpu.VMEM((512, 256), F32),
            DMA((3,)),
        ],
        compiler_params=WIDE,
    )(at, blocks, root, upper)


def fan_kernel(first_ref, second_ref, copies_ref):
    for t, ref in enumerate((first_ref, second_ref)):
        value = ref[...]
        for i in range(8):
            copies_ref[i, t] = value


def fan(first, second):
    return pl.pallas_call(
        fan_kernel,
        out_shape=shape(8, 2, 128, 128),
        in_specs=[VMEM] * 2,
        out_specs=VMEM,
        compiler_params=PARAMS,
    )(first, second)


def couple_kernel(
    at_ref, gathered_hbm, own_hbm, other_hbm, out_ref, left, own, other, ah, al, bh, bl, sems
):
    loads = [
        pltpu.make_async_copy(own_hbm, own, sems.at[0]),
        pltpu.make_async_copy(other_hbm, other, sems.at[1]),
        pltpu.make_async_copy(gathered_hbm.at[:, 256:512], left, sems.at[2]),
    ]
    for load in loads:
        load.start()
    _, _, core, _, x = device(at_ref)
    odd = x & 1
    for n, right in enumerate((own, other)):
        loads[n].wait()
        side = core if n == 0 else 1 - core
        for z in range(8):
            rows = slice(128 * z, 128 * (z + 1))
            for t in range(2):
                cols = slice(256 * n + 128 * t, 256 * n + 128 * (t + 1))
                bh[rows, cols], bl[rows, cols] = split2(right[z ^ (4 * side), t])
    loads[2].wait()
    for z in range(8):
        rows = slice(128 * z, 128 * (z + 1))
        ah[:, rows], al[:, rows] = split2(left[z ^ (4 * core)])
    for n in range(2):
        cols = slice(256 * n, 256 * (n + 1))
        part = three_pass(ah[...], al[...], bh[:, cols], bl[:, cols])
        out_ref[2 * n + odd] = part[:, :128]
        out_ref[2 * n + 1 - odd] = part[:, 128:]


def couple(at, gathered, own, other):
    return pl.pallas_call(
        couple_kernel,
        out_shape=shape(4, 256, 128),
        in_specs=[SMEM, HBM, HBM, HBM],
        out_specs=VMEM,
        scratch_shapes=[
            pltpu.VMEM((8, 256, 128), F32),
            pltpu.VMEM((8, 2, 128, 128), F32),
            pltpu.VMEM((8, 2, 128, 128), F32),
            pltpu.VMEM((256, 1024), BF16),
            pltpu.VMEM((256, 1024), BF16),
            pltpu.VMEM((1024, 512), BF16),
            pltpu.VMEM((1024, 512), BF16),
            DMA((3,)),
        ],
        compiler_params=NEAR,
        cost_estimate=pl.CostEstimate(flops=6 << 28, bytes_accessed=3 << 20, transcendentals=0),
    )(at, gathered, own, other)


def side_kernel(
    at_ref, su_hbm, lower_hbm, rest_hbm, hi_hbm, lo_hbm, sigma, lower, ah, al, bh, bl, out, sems
):
    loads = [pltpu.make_async_copy(su_hbm.at[:, 0:256], sigma, sems.at[0])]
    for n in range(2):
        loads.append(pltpu.make_async_copy(lower_hbm.at[n], lower.at[n], sems.at[1 + n]))
    for load in loads:
        load.start()
    _, _, core, _, x = device(at_ref)
    odd = x & 1
    loads[0].wait()
    for z in range(8):
        rows = slice(128 * z, 128 * (z + 1))
        ah[:, rows], al[:, rows] = split2(sigma[z ^ (4 * core)])
    stores = []
    for n in range(2):
        loads[1 + n].wait()
        for z in range(8):
            rows = slice(128 * z, 128 * (z + 1))
            for t in range(2):
                cols = slice(128 * t, 128 * (t + 1))
                place = 128 * (odd if t == 0 else 1 - odd)
                value = lower[n, z, pl.ds(pl.multiple_of(place, 128), 128), :]
                bh[n, rows, cols], bl[n, rows, cols] = split2(value)
        stores.append(pltpu.make_async_copy(bh.at[n], hi_hbm.at[n], sems.at[3 + n]))
        stores.append(pltpu.make_async_copy(bl.at[n], lo_hbm.at[n], sems.at[5 + n]))
        part = -three_pass(ah[...], al[...], bh[n], bl[n])
        out[2 * n] = part[:, :128]
        out[2 * n + 1] = part[:, 128:]
        pair, place = slice(2 * n, 2 * n + 2), pl.ds(2 * (n ^ core), 2)
        stores.append(pltpu.make_async_copy(out.at[pair], rest_hbm.at[place], sems.at[7 + n]))
        for store in stores[3 * n :]:
            store.start()
    for store in stores:
        store.wait()


def side(at, gathered, lower):
    return pl.pallas_call(
        side_kernel,
        out_shape=(shape(12, 256, 128),) + (shape(2, 1024, 256, dtype=BF16),) * 2,
        in_specs=[SMEM, HBM, HBM],
        out_specs=(HBM,) * 3,
        scratch_shapes=[
            pltpu.VMEM((8, 256, 128), F32),
            pltpu.VMEM((2, 8, 256, 128), F32),
            pltpu.VMEM((256, 1024), BF16),
            pltpu.VMEM((256, 1024), BF16),
            pltpu.VMEM((2, 1024, 256), BF16),
            pltpu.VMEM((2, 1024, 256), BF16),
            pltpu.VMEM((4, 256, 128), F32),
            DMA((9,)),
        ],
        compiler_params=WIDE,
        cost_estimate=pl.CostEstimate(flops=6 << 28, bytes_accessed=6 << 20, transcendentals=0),
    )(at, gathered, lower)


def last_kernel(at_ref, w_hbm, hi_hbm, lo_hbm, rest_hbm, out_hbm, w, ah, al, bh, bl, out, sems):
    rest = pltpu.make_async_copy(rest_hbm.at[0:4], out_hbm.at[:, 256:512], sems.at[7])
    loads = [pltpu.make_async_copy(w_hbm, w, sems.at[0])]
    for n in range(2):
        loads.append(pltpu.make_async_copy(hi_hbm.at[n], bh.at[n], sems.at[1 + n]))
        loads.append(pltpu.make_async_copy(lo_hbm.at[n], bl.at[n], sems.at[3 + n]))
    for load in loads + [rest]:
        load.start()
    core = device(at_ref)[2]
    loads[0].wait()
    for z in range(8):
        rows = slice(128 * z, 128 * (z + 1))
        ah[:, rows], al[:, rows] = split2(w[z ^ (4 * core)])
    stores = [rest]
    for n in range(2):
        for load in loads[1 + 2 * n : 3 + 2 * n]:
            load.wait()
        part = three_pass(ah[...], al[...], bh[n], bl[n])
        out[2 * n] = part[:, :128]
        out[2 * n + 1] = part[:, 128:]
        pair, place = slice(2 * n, 2 * n + 2), pl.ds(2 * (n ^ core), 2)
        stores.append(
            pltpu.make_async_copy(out.at[pair], out_hbm.at[place, 0:256], sems.at[5 + n])
        )
        stores[-1].start()
    for store in stores:
        store.wait()


def last(at, w, hi, lo, rest):
    return pl.pallas_call(
        last_kernel,
        out_shape=shape(4, 512, 128),
        in_specs=[SMEM] + [HBM] * 4,
        out_specs=HBM,
        scratch_shapes=[
            pltpu.VMEM((8, 256, 128), F32),
            pltpu.VMEM((256, 1024), BF16),
            pltpu.VMEM((256, 1024), BF16),
            pltpu.VMEM((2, 1024, 256), BF16),
            pltpu.VMEM((2, 1024, 256), BF16),
            pltpu.VMEM((4, 256, 128), F32),
            DMA((8,)),
        ],
        compiler_params=MIDDLE,
    )(at, w, hi, lo, rest)


def rotated(axis, size):
    axes = (axis, "c") if axis == "y" else ("c", axis)
    groups = [
        [2 * p + c if axis == "y" else size * c + p for p in (i ^ (size // 2 * c) for i in range(size))]
        for c in range(2)
    ]
    return axes, groups


def exchange(v, axis, size):
    axes, groups = rotated(axis, size)
    return lax.all_to_all(v, axes, 0, 0, tiled=True, axis_index_groups=groups)


def deal(v, t):
    moves = [(4 * c + x, 4 * (x >> 1) + 2 * c + ((x & 1) ^ t)) for c in range(2) for x in range(4)]
    return lax.ppermute(v, ("c", "x"), moves)


def turn(v, axis, size, k):
    return lax.ppermute(v, axis, [(i, (i + k) % size) for i in range(size)])


def shards(root_inverse, boundary_map, lower_factor, upper_factor, diagonal_inverse):
    at = lax.axis_index(("y", "c", "z", "x")).astype(jnp.int32).reshape(1)
    su, first, second = pick(at, boundary_map.reshape(32, 128), root_inverse, upper_factor)
    axes, groups = rotated("z", 8)
    gathered = lax.all_gather(su, axes, axis=0, tiled=False, axis_index_groups=groups)
    copies = fan(deal(first, 0), deal(second, 1))
    copies, lower = lax.optimization_barrier((copies, lower_factor))
    odd = lax.axis_index("x") & 1
    lower = [
        deal(lax.dynamic_slice_in_dim(lower, 128 * (odd ^ t), 128), t) for t in range(2)
    ]
    lower = jnp.concatenate(lower, axis=0)
    groups = [[2 * i + core for core in range(2) for i in range(8)]]
    lower = lax.all_gather(lower, ("y", "c"), axis=0, tiled=False, axis_index_groups=groups)
    lower = lower.reshape(2, 8, 256, 128)
    own = exchange(copies, "y", 8)
    other = turn(own, "c", 2, 1)
    part = couple(at, gathered, own, other)
    w = exchange(part, "x", 4).sum(axis=0)
    w_all = exchange(jnp.broadcast_to(w[None], (8, 256, 128)), "z", 8)
    rest, hi, lo = side(at, gathered, lower)
    sums = exchange(last(at, w_all, hi, lo, rest), "x", 4).sum(axis=0)
    return (sums[256:], -w, diagonal_inverse + sums[:256])


def solution(mesh):
    grid = Mesh(np.asarray(mesh.devices).reshape(8, 2, 8, 4), ("y", "c", "z", "x"))
    block = P(("y", "c"), ("z", "x"))
    return jax.shard_map(
        shards,
        mesh=grid,
        in_specs=(block, P(), block, block, block),
        out_specs=(block, block, block),
        check_vma=False,
    )
```

```python
import jax
import jax.numpy as jnp
import numpy as np
from jax import lax
from jax.experimental import pallas as pl
from jax.experimental.pallas import tpu as pltpu
from jax.sharding import Mesh, PartitionSpec as P

F32 = jnp.float32
BF16 = jnp.bfloat16
VMEM = pl.BlockSpec(memory_space=pltpu.VMEM)
SMEM = pl.BlockSpec(memory_space=pltpu.SMEM)
HBM = pl.BlockSpec(memory_space=pltpu.HBM)
PARAMS = pltpu.CompilerParams(vmem_limit_bytes=32 * 1024 * 1024)
WIDE = pltpu.CompilerParams(vmem_limit_bytes=62 * 1024 * 1024)
NEAR = pltpu.CompilerParams(vmem_limit_bytes=51 * 1024 * 1024)
MIDDLE = pltpu.CompilerParams(vmem_limit_bytes=51 * 1024 * 1024)
DMA = pltpu.SemaphoreType.DMA


def shape(*dims, dtype=F32):
    return jax.ShapeDtypeStruct(dims, dtype)


def split2(v):
    hi = v.astype(BF16)
    return hi, (v - hi.astype(F32)).astype(BF16)


def dot(a, b):
    return lax.dot_general(a, b, (((1,), (0,)), ((), ())), preferred_element_type=F32)


def three_pass(ah, al, bh, bl):
    return dot(ah, bh) + (dot(ah, bl) + dot(al, bh))


def device(ref):
    number = ref[0]
    return number >> 5, number & 31, (number >> 5) & 1, (number >> 2) & 7, number & 3


def pick_kernel(
    at_ref, map_hbm, root_hbm, upper_hbm, su_ref, first_ref, second_ref, picks, root, sems
):
    loads = [
        pltpu.make_async_copy(map_hbm, picks, sems.at[0]),
        pltpu.make_async_copy(root_hbm, root, sems.at[1]),
        pltpu.make_async_copy(upper_hbm, su_ref.at[256:512], sems.at[2]),
    ]
    for load in loads:
        load.start()
    row, col, _, _, x = device(at_ref)
    odd = x & 1
    iota = lax.broadcasted_iota(jnp.int32, (256, 128), 0)
    loads[0].wait()
    cols = picks[pl.ds(col, 1), :] - 256 * col
    col_hot = jnp.where(cols == iota, 1.0, 0.0).astype(BF16)
    hots = []
    for part in range(2):
        block = 2 * row + part
        rows = picks[pl.ds(block, 1), :] - 256 * block
        hots.append(jnp.where(rows == iota, 1.0, 0.0).astype(BF16))
    loads[1].wait()
    stack = []
    for part in range(2):
        left = root[256 * part : 256 * (part + 1), :]
        pieces = []
        for _ in range(3):
            piece = left.astype(BF16)
            left = left - piece.astype(F32)
            pieces.append(piece)
        across = lax.dot_general(
            hots[part],
            jnp.concatenate(pieces, axis=1),
            (((0,), (0,)), ((), ())),
            preferred_element_type=F32,
        ).astype(BF16)
        stack += [across[:, 256 * i : 256 * (i + 1)] for i in range(3)]
    value = dot(jnp.concatenate(stack, axis=0), col_hot)
    for part in range(2):
        v = [value[128 * (3 * part + i) : 128 * (3 * part + i + 1), :] for i in range(3)]
        su_ref[128 * part : 128 * (part + 1), :] = (v[0] + v[1]) + v[2]
    loads[2].wait()
    near = pl.multiple_of(128 * odd, 128)
    far = pl.multiple_of(128 - 128 * odd, 128)
    first_ref[...] = su_ref[pl.ds(near, 128), :]
    second_ref[...] = su_ref[pl.ds(far, 128), :]


def pick(at, blocks, root, upper):
    return pl.pallas_call(
        pick_kernel,
        out_shape=(shape(512, 128), shape(128, 128), shape(128, 128)),
        in_specs=[SMEM] + [HBM] * 3,
        out_specs=(VMEM, VMEM, VMEM),
        scratch_shapes=[
            pltpu.VMEM((32, 128), jnp.int32),
            pltpu.VMEM((512, 256), F32),
            DMA((3,)),
        ],
        compiler_params=WIDE,
    )(at, blocks, root, upper)


def fan_kernel(first_ref, second_ref, copies_ref):
    for t, ref in enumerate((first_ref, second_ref)):
        value = ref[...]
        for i in range(8):
            copies_ref[i, t] = value


def fan(first, second):
    return pl.pallas_call(
        fan_kernel,
        out_shape=shape(8, 2, 128, 128),
        in_specs=[VMEM] * 2,
        out_specs=VMEM,
        compiler_params=PARAMS,
    )(first, second)


def couple_kernel(
    at_ref, gathered_hbm, own_hbm, other_hbm, out_ref, left, own, other, ah, al, bh, bl, sems
):
    loads = [
        pltpu.make_async_copy(own_hbm, own, sems.at[0]),
        pltpu.make_async_copy(other_hbm, other, sems.at[1]),
        pltpu.make_async_copy(gathered_hbm.at[:, 256:512], left, sems.at[2]),
    ]
    for load in loads:
        load.start()
    _, _, core, _, x = device(at_ref)
    odd = x & 1
    for n, right in enumerate((own, other)):
        loads[n].wait()
        side = core if n == 0 else 1 - core
        for z in range(8):
            rows = slice(128 * z, 128 * (z + 1))
            for t in range(2):
                cols = slice(256 * n + 128 * t, 256 * n + 128 * (t + 1))
                bh[rows, cols], bl[rows, cols] = split2(right[z ^ (4 * side), t])
    loads[2].wait()
    for z in range(8):
        rows = slice(128 * z, 128 * (z + 1))
        ah[:, rows], al[:, rows] = split2(left[z ^ (4 * core)])
    for n in range(2):
        cols = slice(256 * n, 256 * (n + 1))
        part = three_pass(ah[...], al[...], bh[:, cols], bl[:, cols])
        out_ref[2 * n + odd] = part[:, :128]
        out_ref[2 * n + 1 - odd] = part[:, 128:]


def couple(at, gathered, own, other):
    return pl.pallas_call(
        couple_kernel,
        out_shape=shape(4, 256, 128),
        in_specs=[SMEM, HBM, HBM, HBM],
        out_specs=VMEM,
        scratch_shapes=[
            pltpu.VMEM((8, 256, 128), F32),
            pltpu.VMEM((8, 2, 128, 128), F32),
            pltpu.VMEM((8, 2, 128, 128), F32),
            pltpu.VMEM((256, 1024), BF16),
            pltpu.VMEM((256, 1024), BF16),
            pltpu.VMEM((1024, 512), BF16),
            pltpu.VMEM((1024, 512), BF16),
            DMA((3,)),
        ],
        compiler_params=NEAR,
        cost_estimate=pl.CostEstimate(flops=6 << 28, bytes_accessed=3 << 20, transcendentals=0),
    )(at, gathered, own, other)


def side_kernel(
    at_ref, su_hbm, lower_hbm, rest_hbm, hi_hbm, lo_hbm, sigma, lower, ah, al, bh, bl, out, sems
):
    loads = [pltpu.make_async_copy(su_hbm.at[:, 0:256], sigma, sems.at[0])]
    for n in range(2):
        loads.append(pltpu.make_async_copy(lower_hbm.at[n], lower.at[n], sems.at[1 + n]))
    for load in loads:
        load.start()
    _, _, core, _, x = device(at_ref)
    odd = x & 1
    loads[0].wait()
    for z in range(8):
        rows = slice(128 * z, 128 * (z + 1))
        ah[:, rows], al[:, rows] = split2(sigma[z ^ (4 * core)])
    stores = []
    for n in range(2):
        loads[1 + n].wait()
        for z in range(8):
            rows = slice(128 * z, 128 * (z + 1))
            for t in range(2):
                cols = slice(128 * t, 128 * (t + 1))
                place = 128 * (odd if t == 0 else 1 - odd)
                value = lower[n, z, pl.ds(pl.multiple_of(place, 128), 128), :]
                bh[n, rows, cols], bl[n, rows, cols] = split2(value)
        stores.append(pltpu.make_async_copy(bh.at[n], hi_hbm.at[n], sems.at[3 + n]))
        stores.append(pltpu.make_async_copy(bl.at[n], lo_hbm.at[n], sems.at[5 + n]))
        for store in stores[-2:]:
            store.start()
        part = -three_pass(ah[...], al[...], bh[n], bl[n])
        out[2 * n] = part[:, :128]
        out[2 * n + 1] = part[:, 128:]
        pair, place = slice(2 * n, 2 * n + 2), pl.ds(2 * (n ^ core), 2)
        stores.append(pltpu.make_async_copy(out.at[pair], rest_hbm.at[place], sems.at[7 + n]))
        stores[-1].start()
    for store in stores:
        store.wait()


def side(at, gathered, lower):
    return pl.pallas_call(
        side_kernel,
        out_shape=(shape(12, 256, 128),) + (shape(2, 1024, 256, dtype=BF16),) * 2,
        in_specs=[SMEM, HBM, HBM],
        out_specs=(HBM,) * 3,
        scratch_shapes=[
            pltpu.VMEM((8, 256, 128), F32),
            pltpu.VMEM((2, 8, 256, 128), F32),
            pltpu.VMEM((256, 1024), BF16),
            pltpu.VMEM((256, 1024), BF16),
            pltpu.VMEM((2, 1024, 256), BF16),
            pltpu.VMEM((2, 1024, 256), BF16),
            pltpu.VMEM((4, 256, 128), F32),
            DMA((9,)),
        ],
        compiler_params=WIDE,
        cost_estimate=pl.CostEstimate(flops=6 << 28, bytes_accessed=6 << 20, transcendentals=0),
    )(at, gathered, lower)


def last_kernel(at_ref, w_hbm, hi_hbm, lo_hbm, rest_hbm, out_hbm, w, ah, al, bh, bl, out, rest, sems):
    loads = [pltpu.make_async_copy(w_hbm, w, sems.at[0])]
    for n in range(2):
        loads.append(pltpu.make_async_copy(hi_hbm.at[n], bh.at[n], sems.at[1 + n]))
        loads.append(pltpu.make_async_copy(lo_hbm.at[n], bl.at[n], sems.at[3 + n]))
    loads.append(pltpu.make_async_copy(rest_hbm.at[0:4], rest, sems.at[7]))
    for load in loads:
        load.start()
    core = device(at_ref)[2]
    loads[0].wait()
    for z in range(8):
        rows = slice(128 * z, 128 * (z + 1))
        ah[:, rows], al[:, rows] = split2(w[z ^ (4 * core)])
    stores = []
    for n in range(2):
        for load in loads[1 + 2 * n : 3 + 2 * n]:
            load.wait()
        part = three_pass(ah[...], al[...], bh[n], bl[n])
        out[2 * n] = part[:, :128]
        out[2 * n + 1] = part[:, 128:]
        if n == 0:
            loads[5].wait()
            stores.append(pltpu.make_async_copy(rest, out_hbm.at[:, 256:512], sems.at[8]))
            stores[-1].start()
        pair, place = slice(2 * n, 2 * n + 2), pl.ds(2 * (n ^ core), 2)
        stores.append(
            pltpu.make_async_copy(out.at[pair], out_hbm.at[place, 0:256], sems.at[5 + n])
        )
        stores[-1].start()
    for store in stores:
        store.wait()


def last(at, w, hi, lo, rest):
    return pl.pallas_call(
        last_kernel,
        out_shape=shape(4, 512, 128),
        in_specs=[SMEM] + [HBM] * 4,
        out_specs=HBM,
        scratch_shapes=[
            pltpu.VMEM((8, 256, 128), F32),
            pltpu.VMEM((256, 1024), BF16),
            pltpu.VMEM((256, 1024), BF16),
            pltpu.VMEM((2, 1024, 256), BF16),
            pltpu.VMEM((2, 1024, 256), BF16),
            pltpu.VMEM((4, 256, 128), F32),
            pltpu.VMEM((4, 256, 128), F32),
            DMA((9,)),
        ],
        compiler_params=MIDDLE,
    )(at, w, hi, lo, rest)


def rotated(axis, size):
    axes = (axis, "c") if axis == "y" else ("c", axis)
    groups = [
        [2 * p + c if axis == "y" else size * c + p for p in (i ^ (size // 2 * c) for i in range(size))]
        for c in range(2)
    ]
    return axes, groups


def exchange(v, axis, size):
    axes, groups = rotated(axis, size)
    return lax.all_to_all(v, axes, 0, 0, tiled=True, axis_index_groups=groups)


def deal(v, t):
    moves = [(4 * c + x, 4 * (x >> 1) + 2 * c + ((x & 1) ^ t)) for c in range(2) for x in range(4)]
    return lax.ppermute(v, ("c", "x"), moves)


def turn(v, axis, size, k):
    return lax.ppermute(v, axis, [(i, (i + k) % size) for i in range(size)])


def shards(root_inverse, boundary_map, lower_factor, upper_factor, diagonal_inverse):
    at = lax.axis_index(("y", "c", "z", "x")).astype(jnp.int32).reshape(1)
    su, first, second = pick(at, boundary_map.reshape(32, 128), root_inverse, upper_factor)
    axes, groups = rotated("z", 8)
    gathered = lax.all_gather(su, axes, axis=0, tiled=False, axis_index_groups=groups)
    copies = fan(deal(first, 0), deal(second, 1))
    copies, lower = lax.optimization_barrier((copies, lower_factor))
    odd = lax.axis_index("x") & 1
    lower = [
        deal(lax.dynamic_slice_in_dim(lower, 128 * (odd ^ t), 128), t) for t in range(2)
    ]
    lower = jnp.concatenate(lower, axis=0)
    groups = [[2 * i + core for core in range(2) for i in range(8)]]
    lower = lax.all_gather(lower, ("y", "c"), axis=0, tiled=False, axis_index_groups=groups)
    lower = lower.reshape(2, 8, 256, 128)
    own = exchange(copies, "y", 8)
    other = turn(own, "c", 2, 1)
    part = couple(at, gathered, own, other)
    w = exchange(part, "x", 4).sum(axis=0)
    w_all = exchange(jnp.broadcast_to(w[None], (8, 256, 128)), "z", 8)
    rest, hi, lo = side(at, gathered, lower)
    sums = exchange(last(at, w_all, hi, lo, rest), "x", 4).sum(axis=0)
    return (sums[256:], -w, diagonal_inverse + sums[:256])


def solution(mesh):
    grid = Mesh(np.asarray(mesh.devices).reshape(8, 2, 8, 4), ("y", "c", "z", "x"))
    block = P(("y", "c"), ("z", "x"))
    return jax.shard_map(
        shards,
        mesh=grid,
        in_specs=(block, P(), block, block, block),
        out_specs=(block, block, block),
        check_vma=False,
    )
```

```python
import jax
import jax.numpy as jnp
import numpy as np
from jax import lax
from jax.experimental import pallas as pl
from jax.experimental.pallas import tpu as pltpu
from jax.sharding import Mesh, PartitionSpec as P

F32 = jnp.float32
BF16 = jnp.bfloat16
VMEM = pl.BlockSpec(memory_space=pltpu.VMEM)
SMEM = pl.BlockSpec(memory_space=pltpu.SMEM)
HBM = pl.BlockSpec(memory_space=pltpu.HBM)
PARAMS = pltpu.CompilerParams(vmem_limit_bytes=32 * 1024 * 1024)
WIDE = pltpu.CompilerParams(vmem_limit_bytes=62 * 1024 * 1024)
NEAR = pltpu.CompilerParams(vmem_limit_bytes=51 * 1024 * 1024)
MIDDLE = pltpu.CompilerParams(vmem_limit_bytes=53248 * 1024)
DMA = pltpu.SemaphoreType.DMA


def shape(*dims, dtype=F32):
    return jax.ShapeDtypeStruct(dims, dtype)


def split2(v):
    hi = v.astype(BF16)
    return hi, (v - hi.astype(F32)).astype(BF16)


def dot(a, b):
    return lax.dot_general(a, b, (((1,), (0,)), ((), ())), preferred_element_type=F32)


def three_pass(ah, al, bh, bl):
    return dot(ah, bh) + (dot(ah, bl) + dot(al, bh))


def device(ref):
    number = ref[0]
    return number >> 5, number & 31, (number >> 5) & 1, (number >> 2) & 7, number & 3


def pick_kernel(
    at_ref, map_hbm, root_hbm, upper_hbm, su_ref, first_ref, second_ref, picks, root, sems
):
    loads = [
        pltpu.make_async_copy(map_hbm, picks, sems.at[0]),
        pltpu.make_async_copy(root_hbm, root, sems.at[1]),
        pltpu.make_async_copy(upper_hbm, su_ref.at[256:512], sems.at[2]),
    ]
    for load in loads:
        load.start()
    row, col, _, _, x = device(at_ref)
    odd = x & 1
    iota = lax.broadcasted_iota(jnp.int32, (256, 128), 0)
    loads[0].wait()
    cols = picks[pl.ds(col, 1), :] - 256 * col
    col_hot = jnp.where(cols == iota, 1.0, 0.0).astype(BF16)
    hots = []
    for part in range(2):
        block = 2 * row + part
        rows = picks[pl.ds(block, 1), :] - 256 * block
        hots.append(jnp.where(rows == iota, 1.0, 0.0).astype(BF16))
    loads[1].wait()
    stack = []
    for part in range(2):
        left = root[256 * part : 256 * (part + 1), :]
        pieces = []
        for _ in range(3):
            piece = left.astype(BF16)
            left = left - piece.astype(F32)
            pieces.append(piece)
        across = lax.dot_general(
            hots[part],
            jnp.concatenate(pieces, axis=1),
            (((0,), (0,)), ((), ())),
            preferred_element_type=F32,
        ).astype(BF16)
        stack += [across[:, 256 * i : 256 * (i + 1)] for i in range(3)]
    value = dot(jnp.concatenate(stack, axis=0), col_hot)
    for part in range(2):
        v = [value[128 * (3 * part + i) : 128 * (3 * part + i + 1), :] for i in range(3)]
        su_ref[128 * part : 128 * (part + 1), :] = (v[0] + v[1]) + v[2]
    loads[2].wait()
    near = pl.multiple_of(128 * odd, 128)
    far = pl.multiple_of(128 - 128 * odd, 128)
    first_ref[...] = su_ref[pl.ds(near, 128), :]
    second_ref[...] = su_ref[pl.ds(far, 128), :]


def pick(at, blocks, root, upper):
    return pl.pallas_call(
        pick_kernel,
        out_shape=(shape(512, 128), shape(128, 128), shape(128, 128)),
        in_specs=[SMEM] + [HBM] * 3,
        out_specs=(VMEM, VMEM, VMEM),
        scratch_shapes=[
            pltpu.VMEM((32, 128), jnp.int32),
            pltpu.VMEM((512, 256), F32),
            DMA((3,)),
        ],
        compiler_params=WIDE,
    )(at, blocks, root, upper)


def fan_kernel(first_ref, second_ref, copies_ref):
    for t, ref in enumerate((first_ref, second_ref)):
        value = ref[...]
        for i in range(8):
            copies_ref[i, t] = value


def fan(first, second):
    return pl.pallas_call(
        fan_kernel,
        out_shape=shape(8, 2, 128, 128),
        in_specs=[VMEM] * 2,
        out_specs=VMEM,
        compiler_params=PARAMS,
    )(first, second)


def couple_kernel(
    at_ref, gathered_hbm, own_hbm, other_hbm, out_ref, left, own, other, ah, al, bh, bl, sems
):
    loads = [
        pltpu.make_async_copy(own_hbm, own, sems.at[0]),
        pltpu.make_async_copy(other_hbm, other, sems.at[1]),
        pltpu.make_async_copy(gathered_hbm.at[:, 256:512], left, sems.at[2]),
    ]
    for load in loads:
        load.start()
    _, _, core, _, x = device(at_ref)
    odd = x & 1
    for n, right in enumerate((own, other)):
        loads[n].wait()
        side = core if n == 0 else 1 - core
        for z in range(8):
            rows = slice(128 * z, 128 * (z + 1))
            for t in range(2):
                cols = slice(256 * n + 128 * t, 256 * n + 128 * (t + 1))
                bh[rows, cols], bl[rows, cols] = split2(right[z ^ (4 * side), t])
    loads[2].wait()
    for z in range(8):
        rows = slice(128 * z, 128 * (z + 1))
        ah[:, rows], al[:, rows] = split2(left[z ^ (4 * core)])
    for n in range(2):
        cols = slice(256 * n, 256 * (n + 1))
        part = three_pass(ah[...], al[...], bh[:, cols], bl[:, cols])
        out_ref[2 * n + odd] = part[:, :128]
        out_ref[2 * n + 1 - odd] = part[:, 128:]


def couple(at, gathered, own, other):
    return pl.pallas_call(
        couple_kernel,
        out_shape=shape(4, 256, 128),
        in_specs=[SMEM, HBM, HBM, HBM],
        out_specs=VMEM,
        scratch_shapes=[
            pltpu.VMEM((8, 256, 128), F32),
            pltpu.VMEM((8, 2, 128, 128), F32),
            pltpu.VMEM((8, 2, 128, 128), F32),
            pltpu.VMEM((256, 1024), BF16),
            pltpu.VMEM((256, 1024), BF16),
            pltpu.VMEM((1024, 512), BF16),
            pltpu.VMEM((1024, 512), BF16),
            DMA((3,)),
        ],
        compiler_params=NEAR,
        cost_estimate=pl.CostEstimate(flops=6 << 28, bytes_accessed=3 << 20, transcendentals=0),
    )(at, gathered, own, other)


def side_kernel(
    at_ref, su_hbm, lower_hbm, top_hbm, rest_hbm, hi_hbm, lo_hbm, sigma, lower, ah, al, bh, bl, out, sems
):
    loads = [pltpu.make_async_copy(su_hbm.at[:, 0:256], sigma, sems.at[0])]
    for n in range(2):
        loads.append(pltpu.make_async_copy(lower_hbm.at[n], lower.at[n], sems.at[1 + n]))
    for load in loads:
        load.start()
    _, _, core, _, x = device(at_ref)
    odd = x & 1
    loads[0].wait()
    for z in range(8):
        rows = slice(128 * z, 128 * (z + 1))
        ah[:, rows], al[:, rows] = split2(sigma[z ^ (4 * core)])
    stores = []
    for n in range(2):
        loads[1 + n].wait()
        for z in range(8):
            rows = slice(128 * z, 128 * (z + 1))
            for t in range(2):
                cols = slice(128 * t, 128 * (t + 1))
                place = 128 * (odd if t == 0 else 1 - odd)
                value = lower[n, z, pl.ds(pl.multiple_of(place, 128), 128), :]
                bh[n, rows, cols], bl[n, rows, cols] = split2(value)
        stores.append(pltpu.make_async_copy(bh.at[n], hi_hbm.at[n], sems.at[3 + n]))
        stores.append(pltpu.make_async_copy(bl.at[n], lo_hbm.at[n], sems.at[5 + n]))
        for store in stores[-2:]:
            store.start()
        part = -three_pass(ah[...], al[...], bh[n], bl[n])
        out[2 * n] = part[:, :128]
        out[2 * n + 1] = part[:, 128:]
        pair, place = slice(2 * n, 2 * n + 2), pl.ds(2 * (n ^ core), 2)
        stores.append(
            pltpu.make_async_copy(out.at[pair, 0:192], top_hbm.at[place], sems.at[7 + n])
        )
        stores.append(
            pltpu.make_async_copy(out.at[pair, 192:256], rest_hbm.at[place], sems.at[9 + n])
        )
        for store in stores[-2:]:
            store.start()
    for store in stores:
        store.wait()


def side(at, gathered, lower):
    return pl.pallas_call(
        side_kernel,
        out_shape=(shape(4, 192, 128), shape(48, 64, 128)) + (shape(2, 1024, 256, dtype=BF16),) * 2,
        in_specs=[SMEM, HBM, HBM],
        out_specs=(HBM,) * 4,
        scratch_shapes=[
            pltpu.VMEM((8, 256, 128), F32),
            pltpu.VMEM((2, 8, 256, 128), F32),
            pltpu.VMEM((256, 1024), BF16),
            pltpu.VMEM((256, 1024), BF16),
            pltpu.VMEM((2, 1024, 256), BF16),
            pltpu.VMEM((2, 1024, 256), BF16),
            pltpu.VMEM((4, 256, 128), F32),
            DMA((11,)),
        ],
        compiler_params=WIDE,
        cost_estimate=pl.CostEstimate(flops=6 << 28, bytes_accessed=6 << 20, transcendentals=0),
    )(at, gathered, lower)


def last_kernel(at_ref, w_hbm, hi_hbm, lo_hbm, rest_hbm, out_hbm, w, ah, al, bh, bl, out, rest, sems):
    loads = [pltpu.make_async_copy(w_hbm, w, sems.at[0])]
    for n in range(2):
        loads.append(pltpu.make_async_copy(hi_hbm.at[n], bh.at[n], sems.at[1 + n]))
        loads.append(pltpu.make_async_copy(lo_hbm.at[n], bl.at[n], sems.at[3 + n]))
    loads.append(pltpu.make_async_copy(rest_hbm.at[0:4], rest, sems.at[7]))
    for load in loads:
        load.start()
    core = device(at_ref)[2]
    loads[0].wait()
    for z in range(8):
        rows = slice(128 * z, 128 * (z + 1))
        ah[:, rows], al[:, rows] = split2(w[z ^ (4 * core)])
    stores = []
    for n in range(2):
        for load in loads[1 + 2 * n : 3 + 2 * n]:
            load.wait()
        part = three_pass(ah[...], al[...], bh[n], bl[n])
        out[2 * n] = part[:, :128]
        out[2 * n + 1] = part[:, 128:]
        if n == 0:
            loads[5].wait()
            stores.append(pltpu.make_async_copy(rest, out_hbm.at[:, 256:320], sems.at[8]))
            stores[-1].start()
        pair, place = slice(2 * n, 2 * n + 2), pl.ds(2 * (n ^ core), 2)
        stores.append(
            pltpu.make_async_copy(out.at[pair], out_hbm.at[place, 0:256], sems.at[5 + n])
        )
        stores[-1].start()
    for store in stores:
        store.wait()


def last(at, w, hi, lo, rest):
    return pl.pallas_call(
        last_kernel,
        out_shape=shape(4, 320, 128),
        in_specs=[SMEM] + [HBM] * 4,
        out_specs=HBM,
        scratch_shapes=[
            pltpu.VMEM((8, 256, 128), F32),
            pltpu.VMEM((256, 1024), BF16),
            pltpu.VMEM((256, 1024), BF16),
            pltpu.VMEM((2, 1024, 256), BF16),
            pltpu.VMEM((2, 1024, 256), BF16),
            pltpu.VMEM((4, 256, 128), F32),
            pltpu.VMEM((4, 64, 128), F32),
            DMA((9,)),
        ],
        compiler_params=MIDDLE,
    )(at, w, hi, lo, rest)


def rotated(axis, size):
    axes = (axis, "c") if axis == "y" else ("c", axis)
    groups = [
        [2 * p + c if axis == "y" else size * c + p for p in (i ^ (size // 2 * c) for i in range(size))]
        for c in range(2)
    ]
    return axes, groups


def exchange(v, axis, size):
    axes, groups = rotated(axis, size)
    return lax.all_to_all(v, axes, 0, 0, tiled=True, axis_index_groups=groups)


def deal(v, t):
    moves = [(4 * c + x, 4 * (x >> 1) + 2 * c + ((x & 1) ^ t)) for c in range(2) for x in range(4)]
    return lax.ppermute(v, ("c", "x"), moves)


def turn(v, axis, size, k):
    return lax.ppermute(v, axis, [(i, (i + k) % size) for i in range(size)])


def shards(root_inverse, boundary_map, lower_factor, upper_factor, diagonal_inverse):
    at = lax.axis_index(("y", "c", "z", "x")).astype(jnp.int32).reshape(1)
    su, first, second = pick(at, boundary_map.reshape(32, 128), root_inverse, upper_factor)
    axes, groups = rotated("z", 8)
    gathered = lax.all_gather(su, axes, axis=0, tiled=False, axis_index_groups=groups)
    copies = fan(deal(first, 0), deal(second, 1))
    copies, lower = lax.optimization_barrier((copies, lower_factor))
    odd = lax.axis_index("x") & 1
    lower = [
        deal(lax.dynamic_slice_in_dim(lower, 128 * (odd ^ t), 128), t) for t in range(2)
    ]
    lower = jnp.concatenate(lower, axis=0)
    groups = [[2 * i + core for core in range(2) for i in range(8)]]
    lower = lax.all_gather(lower, ("y", "c"), axis=0, tiled=False, axis_index_groups=groups)
    lower = lower.reshape(2, 8, 256, 128)
    own = exchange(copies, "y", 8)
    other = turn(own, "c", 2, 1)
    part = couple(at, gathered, own, other)
    w = exchange(part, "x", 4).sum(axis=0)
    w_all = exchange(jnp.broadcast_to(w[None], (8, 256, 128)), "z", 8)
    top, rest, hi, lo = side(at, gathered, lower)
    axes, groups = rotated("x", 4)
    top = lax.psum_scatter(
        top.reshape(768, 128), axes, scatter_dimension=0, tiled=True, axis_index_groups=groups
    )
    sums = exchange(last(at, w_all, hi, lo, rest), "x", 4).sum(axis=0)
    return (jnp.concatenate([top, sums[256:]], axis=0), -w, diagonal_inverse + sums[:256])


def solution(mesh):
    grid = Mesh(np.asarray(mesh.devices).reshape(8, 2, 8, 4), ("y", "c", "z", "x"))
    block = P(("y", "c"), ("z", "x"))
    return jax.shard_map(
        shards,
        mesh=grid,
        in_specs=(block, P(), block, block, block),
        out_specs=(block, block, block),
        check_vma=False,
    )
```

```python
import jax
import jax.numpy as jnp
import numpy as np
from jax import lax
from jax.experimental import pallas as pl
from jax.experimental.pallas import tpu as pltpu
from jax.sharding import Mesh, PartitionSpec as P

F32 = jnp.float32
BF16 = jnp.bfloat16
VMEM = pl.BlockSpec(memory_space=pltpu.VMEM)
SMEM = pl.BlockSpec(memory_space=pltpu.SMEM)
HBM = pl.BlockSpec(memory_space=pltpu.HBM)
PARAMS = pltpu.CompilerParams(vmem_limit_bytes=32 * 1024 * 1024)
WIDE = pltpu.CompilerParams(vmem_limit_bytes=62 * 1024 * 1024)
NEAR = pltpu.CompilerParams(vmem_limit_bytes=51 * 1024 * 1024)
MIDDLE = pltpu.CompilerParams(vmem_limit_bytes=51 * 1024 * 1024)
DMA = pltpu.SemaphoreType.DMA


def shape(*dims, dtype=F32):
    return jax.ShapeDtypeStruct(dims, dtype)


def split2(v):
    hi = v.astype(BF16)
    return hi, (v - hi.astype(F32)).astype(BF16)


def dot(a, b):
    return lax.dot_general(a, b, (((1,), (0,)), ((), ())), preferred_element_type=F32)


def three_pass(ah, al, bh, bl):
    return dot(ah, bh) + (dot(ah, bl) + dot(al, bh))


def device(ref):
    number = ref[0]
    return number >> 5, number & 31, (number >> 5) & 1, (number >> 2) & 7, number & 3


def pick_kernel(
    at_ref, map_hbm, root_hbm, upper_hbm, su_ref, first_ref, second_ref, picks, root, sems
):
    loads = [
        pltpu.make_async_copy(map_hbm, picks, sems.at[0]),
        pltpu.make_async_copy(root_hbm, root, sems.at[1]),
        pltpu.make_async_copy(upper_hbm, su_ref.at[256:512], sems.at[2]),
    ]
    for load in loads:
        load.start()
    row, col, _, _, x = device(at_ref)
    odd = x & 1
    iota = lax.broadcasted_iota(jnp.int32, (256, 128), 0)
    loads[0].wait()
    cols = picks[pl.ds(col, 1), :] - 256 * col
    col_hot = jnp.where(cols == iota, 1.0, 0.0).astype(BF16)
    hots = []
    for part in range(2):
        block = 2 * row + part
        rows = picks[pl.ds(block, 1), :] - 256 * block
        hots.append(jnp.where(rows == iota, 1.0, 0.0).astype(BF16))
    loads[1].wait()
    stack = []
    for part in range(2):
        left = root[256 * part : 256 * (part + 1), :]
        pieces = []
        for _ in range(3):
            piece = left.astype(BF16)
            left = left - piece.astype(F32)
            pieces.append(piece)
        across = lax.dot_general(
            hots[part],
            jnp.concatenate(pieces, axis=1),
            (((0,), (0,)), ((), ())),
            preferred_element_type=F32,
        ).astype(BF16)
        stack += [across[:, 256 * i : 256 * (i + 1)] for i in range(3)]
    value = dot(jnp.concatenate(stack, axis=0), col_hot)
    for part in range(2):
        v = [value[128 * (3 * part + i) : 128 * (3 * part + i + 1), :] for i in range(3)]
        su_ref[128 * part : 128 * (part + 1), :] = (v[0] + v[1]) + v[2]
    loads[2].wait()
    near = pl.multiple_of(128 * odd, 128)
    far = pl.multiple_of(128 - 128 * odd, 128)
    first_ref[...] = su_ref[pl.ds(near, 128), :]
    second_ref[...] = su_ref[pl.ds(far, 128), :]


def pick(at, blocks, root, upper):
    return pl.pallas_call(
        pick_kernel,
        out_shape=(shape(512, 128), shape(128, 128), shape(128, 128)),
        in_specs=[SMEM] + [HBM] * 3,
        out_specs=(VMEM, VMEM, VMEM),
        scratch_shapes=[
            pltpu.VMEM((32, 128), jnp.int32),
            pltpu.VMEM((512, 256), F32),
            DMA((3,)),
        ],
        compiler_params=WIDE,
    )(at, blocks, root, upper)


def fan_kernel(first_ref, second_ref, copies_ref):
    for t, ref in enumerate((first_ref, second_ref)):
        value = ref[...]
        for i in range(8):
            copies_ref[i, t] = value


def fan(first, second):
    return pl.pallas_call(
        fan_kernel,
        out_shape=shape(8, 2, 128, 128),
        in_specs=[VMEM] * 2,
        out_specs=VMEM,
        compiler_params=PARAMS,
    )(first, second)


def couple_kernel(
    at_ref, gathered_hbm, own_hbm, other_hbm, out_ref, left, own, other, ah, al, bh, bl, sems
):
    loads = [
        pltpu.make_async_copy(own_hbm, own, sems.at[0]),
        pltpu.make_async_copy(other_hbm, other, sems.at[1]),
        pltpu.make_async_copy(gathered_hbm.at[:, 256:512], left, sems.at[2]),
    ]
    for load in loads:
        load.start()
    _, _, core, _, x = device(at_ref)
    odd = x & 1
    for n, right in enumerate((own, other)):
        loads[n].wait()
        side = core if n == 0 else 1 - core
        for z in range(8):
            rows = slice(128 * z, 128 * (z + 1))
            for t in range(2):
                cols = slice(256 * n + 128 * t, 256 * n + 128 * (t + 1))
                bh[rows, cols], bl[rows, cols] = split2(right[z ^ (4 * side), t])
    loads[2].wait()
    for z in range(8):
        rows = slice(128 * z, 128 * (z + 1))
        ah[:, rows], al[:, rows] = split2(left[z ^ (4 * core)])
    for n in range(2):
        cols = slice(256 * n, 256 * (n + 1))
        part = three_pass(ah[...], al[...], bh[:, cols], bl[:, cols])
        out_ref[2 * n + odd] = part[:, :128]
        out_ref[2 * n + 1 - odd] = part[:, 128:]


def couple(at, gathered, own, other):
    return pl.pallas_call(
        couple_kernel,
        out_shape=shape(4, 256, 128),
        in_specs=[SMEM, HBM, HBM, HBM],
        out_specs=VMEM,
        scratch_shapes=[
            pltpu.VMEM((8, 256, 128), F32),
            pltpu.VMEM((8, 2, 128, 128), F32),
            pltpu.VMEM((8, 2, 128, 128), F32),
            pltpu.VMEM((256, 1024), BF16),
            pltpu.VMEM((256, 1024), BF16),
            pltpu.VMEM((1024, 512), BF16),
            pltpu.VMEM((1024, 512), BF16),
            DMA((3,)),
        ],
        compiler_params=NEAR,
        cost_estimate=pl.CostEstimate(flops=6 << 28, bytes_accessed=3 << 20, transcendentals=0),
    )(at, gathered, own, other)


def side_kernel(
    at_ref, su_hbm, lower_hbm, out_hbm, hi_hbm, lo_hbm, sigma, lower, ah, al, bh, bl, out, sems
):
    loads = [pltpu.make_async_copy(su_hbm.at[:, 0:256], sigma, sems.at[0])]
    for i in range(2):
        rows = slice(4 * i, 4 * (i + 1))
        loads.append(
            pltpu.make_async_copy(lower_hbm.at[:, rows], lower.at[:, rows], sems.at[1 + i])
        )
    for load in loads:
        load.start()
    _, _, core_at, _, x = device(at_ref)
    odd = x & 1
    loads[0].wait()
    for z in range(8):
        rows = slice(128 * z, 128 * (z + 1))
        ah[:, rows], al[:, rows] = split2(sigma[z ^ (4 * core_at)])
    for z in range(8):
        if z % 4 == 0:
            loads[1 + z // 4].wait()
        rows = slice(128 * z, 128 * (z + 1))
        for core in range(2):
            for t in range(2):
                cols = slice(256 * core + 128 * t, 256 * core + 128 * (t + 1))
                place = 128 * (odd if t == 0 else 1 - odd)
                value = lower[core, z, pl.ds(pl.multiple_of(place, 128), 128), :]
                bh[rows, cols], bl[rows, cols] = split2(value)
    stores = [
        pltpu.make_async_copy(bh, hi_hbm, sems.at[3]),
        pltpu.make_async_copy(bl, lo_hbm, sems.at[4]),
    ]
    for store in stores:
        store.start()
    for n in range(2):
        cols = slice(256 * n, 256 * (n + 1))
        part = -three_pass(ah[...], al[...], bh[:, cols], bl[:, cols])
        out[2 * n] = part[:, :128]
        out[2 * n + 1] = part[:, 128:]
        pair, place = slice(2 * n, 2 * n + 2), pl.ds(2 * (n ^ core_at), 2)
        stores.append(pltpu.make_async_copy(out.at[pair], out_hbm.at[place], sems.at[5 + n]))
        stores[-1].start()
    for store in stores:
        store.wait()


def side(at, gathered, lower):
    return pl.pallas_call(
        side_kernel,
        out_shape=(shape(12, 256, 128),) + (shape(1024, 512, dtype=BF16),) * 2,
        in_specs=[SMEM, HBM, HBM],
        out_specs=(HBM,) * 3,
        scratch_shapes=[
            pltpu.VMEM((8, 256, 128), F32),
            pltpu.VMEM((2, 8, 256, 128), F32),
            pltpu.VMEM((256, 1024), BF16),
            pltpu.VMEM((256, 1024), BF16),
            pltpu.VMEM((1024, 512), BF16),
            pltpu.VMEM((1024, 512), BF16),
            pltpu.VMEM((4, 256, 128), F32),
            DMA((7,)),
        ],
        compiler_params=WIDE,
        cost_estimate=pl.CostEstimate(flops=6 << 28, bytes_accessed=6 << 20, transcendentals=0),
    )(at, gathered, lower)


def last_kernel(
    at_ref, w_hbm, hi_hbm, lo_hbm, rest_hbm, out_hbm, w, ah, al, bh, bl, out, rest, sems
):
    loads = [
        pltpu.make_async_copy(w_hbm, w, sems.at[0]),
        pltpu.make_async_copy(hi_hbm, bh, sems.at[1]),
        pltpu.make_async_copy(lo_hbm, bl, sems.at[2]),
        pltpu.make_async_copy(rest_hbm.at[0:4], rest, sems.at[5]),
    ]
    for load in loads:
        load.start()
    core = device(at_ref)[2]
    loads[0].wait()
    for z in range(8):
        rows = slice(128 * z, 128 * (z + 1))
        ah[:, rows], al[:, rows] = split2(w[z ^ (4 * core)])
    for load in loads[1:]:
        load.wait()
    stores = [pltpu.make_async_copy(rest, out_hbm.at[:, 256:512], sems.at[6])]
    stores[0].start()
    for n in range(2):
        cols = slice(256 * n, 256 * (n + 1))
        part = three_pass(ah[...], al[...], bh[:, cols], bl[:, cols])
        out[2 * n] = part[:, :128]
        out[2 * n + 1] = part[:, 128:]
        pair, place = slice(2 * n, 2 * n + 2), pl.ds(2 * (n ^ core), 2)
        stores.append(pltpu.make_async_copy(out.at[pair], out_hbm.at[place, 0:256], sems.at[3 + n]))
        stores[-1].start()
    for store in stores:
        store.wait()


def last(at, w, hi, lo, rest):
    return pl.pallas_call(
        last_kernel,
        out_shape=shape(4, 512, 128),
        in_specs=[SMEM] + [HBM] * 4,
        out_specs=HBM,
        scratch_shapes=[
            pltpu.VMEM((8, 256, 128), F32),
            pltpu.VMEM((256, 1024), BF16),
            pltpu.VMEM((256, 1024), BF16),
            pltpu.VMEM((1024, 512), BF16),
            pltpu.VMEM((1024, 512), BF16),
            pltpu.VMEM((4, 256, 128), F32),
            pltpu.VMEM((4, 256, 128), F32),
            DMA((7,)),
        ],
        compiler_params=MIDDLE,
    )(at, w, hi, lo, rest)


def rotated(axis, size):
    axes = (axis, "c") if axis == "y" else ("c", axis)
    groups = [
        [2 * p + c if axis == "y" else size * c + p for p in (i ^ (size // 2 * c) for i in range(size))]
        for c in range(2)
    ]
    return axes, groups


def exchange(v, axis, size):
    axes, groups = rotated(axis, size)
    return lax.all_to_all(v, axes, 0, 0, tiled=True, axis_index_groups=groups)


def deal(v, t):
    moves = [(4 * c + x, 4 * (x >> 1) + 2 * c + ((x & 1) ^ t)) for c in range(2) for x in range(4)]
    return lax.ppermute(v, ("c", "x"), moves)


def turn(v, axis, size, k):
    return lax.ppermute(v, axis, [(i, (i + k) % size) for i in range(size)])


def shards(root_inverse, boundary_map, lower_factor, upper_factor, diagonal_inverse):
    at = lax.axis_index(("y", "c", "z", "x")).astype(jnp.int32).reshape(1)
    su, first, second = pick(at, boundary_map.reshape(32, 128), root_inverse, upper_factor)
    axes, groups = rotated("z", 8)
    gathered = lax.all_gather(su, axes, axis=0, tiled=False, axis_index_groups=groups)
    copies = fan(deal(first, 0), deal(second, 1))
    copies, lower = lax.optimization_barrier((copies, lower_factor))
    odd = lax.axis_index("x") & 1
    lower = [
        deal(lax.dynamic_slice_in_dim(lower, 128 * (odd ^ t), 128), t) for t in range(2)
    ]
    lower = jnp.concatenate(lower, axis=0)
    groups = [[2 * i + core for core in range(2) for i in range(8)]]
    lower = lax.all_gather(lower, ("y", "c"), axis=0, tiled=False, axis_index_groups=groups)
    lower = lower.reshape(2, 8, 256, 128)
    own = exchange(copies, "y", 8)
    other = turn(own, "c", 2, 1)
    part = couple(at, gathered, own, other)
    w = exchange(part, "x", 4).sum(axis=0)
    w_all = exchange(jnp.broadcast_to(w[None], (8, 256, 128)), "z", 8)
    rest, hi, lo = side(at, gathered, lower)
    sums = exchange(last(at, w_all, hi, lo, rest), "x", 4).sum(axis=0)
    return (sums[256:], -w, diagonal_inverse + sums[:256])


def solution(mesh):
    grid = Mesh(np.asarray(mesh.devices).reshape(8, 2, 8, 4), ("y", "c", "z", "x"))
    block = P(("y", "c"), ("z", "x"))
    return jax.shard_map(
        shards,
        mesh=grid,
        in_specs=(block, P(), block, block, block),
        out_specs=(block, block, block),
        check_vma=False,
    )
```

```python
import jax
import jax.numpy as jnp
import numpy as np
from jax import lax
from jax.experimental import pallas as pl
from jax.experimental.pallas import tpu as pltpu
from jax.sharding import Mesh, PartitionSpec as P

F32 = jnp.float32
BF16 = jnp.bfloat16
VMEM = pl.BlockSpec(memory_space=pltpu.VMEM)
SMEM = pl.BlockSpec(memory_space=pltpu.SMEM)
HBM = pl.BlockSpec(memory_space=pltpu.HBM)
PARAMS = pltpu.CompilerParams(vmem_limit_bytes=32 * 1024 * 1024)
WIDE = pltpu.CompilerParams(vmem_limit_bytes=62 * 1024 * 1024)
NEAR = pltpu.CompilerParams(vmem_limit_bytes=51 * 1024 * 1024)
MIDDLE = pltpu.CompilerParams(vmem_limit_bytes=51 * 1024 * 1024)
DMA = pltpu.SemaphoreType.DMA


def shape(*dims, dtype=F32):
    return jax.ShapeDtypeStruct(dims, dtype)


def split2(v):
    hi = v.astype(BF16)
    return hi, (v - hi.astype(F32)).astype(BF16)


def dot(a, b):
    return lax.dot_general(a, b, (((1,), (0,)), ((), ())), preferred_element_type=F32)


def three_pass(ah, al, bh, bl):
    return dot(ah, bh) + (dot(ah, bl) + dot(al, bh))


def device(ref):
    number = ref[0]
    return number >> 5, number & 31, (number >> 5) & 1, (number >> 2) & 7, number & 3


def pick_kernel(
    at_ref, map_hbm, root_hbm, upper_hbm, su_ref, first_ref, second_ref, picks, root, sems
):
    loads = [
        pltpu.make_async_copy(map_hbm, picks, sems.at[0]),
        pltpu.make_async_copy(root_hbm, root, sems.at[1]),
        pltpu.make_async_copy(upper_hbm, su_ref.at[256:512], sems.at[2]),
    ]
    for load in loads:
        load.start()
    row, col, _, _, x = device(at_ref)
    odd = x & 1
    iota = lax.broadcasted_iota(jnp.int32, (256, 128), 0)
    loads[0].wait()
    cols = picks[pl.ds(col, 1), :] - 256 * col
    col_hot = jnp.where(cols == iota, 1.0, 0.0).astype(BF16)
    hots = []
    for part in range(2):
        block = 2 * row + part
        rows = picks[pl.ds(block, 1), :] - 256 * block
        hots.append(jnp.where(rows == iota, 1.0, 0.0).astype(BF16))
    loads[1].wait()
    stack = []
    for part in range(2):
        left = root[256 * part : 256 * (part + 1), :]
        pieces = []
        for _ in range(3):
            piece = left.astype(BF16)
            left = left - piece.astype(F32)
            pieces.append(piece)
        across = lax.dot_general(
            hots[part],
            jnp.concatenate(pieces, axis=1),
            (((0,), (0,)), ((), ())),
            preferred_element_type=F32,
        ).astype(BF16)
        stack += [across[:, 256 * i : 256 * (i + 1)] for i in range(3)]
    value = dot(jnp.concatenate(stack, axis=0), col_hot)
    for part in range(2):
        v = [value[128 * (3 * part + i) : 128 * (3 * part + i + 1), :] for i in range(3)]
        su_ref[128 * part : 128 * (part + 1), :] = (v[0] + v[1]) + v[2]
    loads[2].wait()
    near = pl.multiple_of(128 * odd, 128)
    far = pl.multiple_of(128 - 128 * odd, 128)
    first_ref[...] = su_ref[pl.ds(near, 128), :]
    second_ref[...] = su_ref[pl.ds(far, 128), :]


def pick(at, blocks, root, upper):
    return pl.pallas_call(
        pick_kernel,
        out_shape=(shape(512, 128), shape(128, 128), shape(128, 128)),
        in_specs=[SMEM] + [HBM] * 3,
        out_specs=(VMEM, VMEM, VMEM),
        scratch_shapes=[
            pltpu.VMEM((32, 128), jnp.int32),
            pltpu.VMEM((512, 256), F32),
            DMA((3,)),
        ],
        compiler_params=WIDE,
    )(at, blocks, root, upper)


def fan_kernel(first_ref, second_ref, copies_ref):
    for t, ref in enumerate((first_ref, second_ref)):
        value = ref[...]
        for i in range(8):
            copies_ref[i, t] = value


def fan(first, second):
    return pl.pallas_call(
        fan_kernel,
        out_shape=shape(8, 2, 128, 128),
        in_specs=[VMEM] * 2,
        out_specs=VMEM,
        compiler_params=PARAMS,
    )(first, second)


def couple_kernel(
    at_ref, gathered_hbm, own, other, out_ref, left, ah, al, bh, bl, sem
):
    load = pltpu.make_async_copy(gathered_hbm.at[:, 256:512], left, sem)
    load.start()
    _, _, core, _, x = device(at_ref)
    odd = x & 1
    for n, right in enumerate((own, other)):
        side = core if n == 0 else 1 - core
        for z in range(8):
            rows = slice(128 * z, 128 * (z + 1))
            for t in range(2):
                cols = slice(256 * n + 128 * t, 256 * n + 128 * (t + 1))
                bh[rows, cols], bl[rows, cols] = split2(right[z ^ (4 * side), t])
    load.wait()
    for z in range(8):
        rows = slice(128 * z, 128 * (z + 1))
        ah[:, rows], al[:, rows] = split2(left[z ^ (4 * core)])
    for n in range(2):
        cols = slice(256 * n, 256 * (n + 1))
        part = three_pass(ah[...], al[...], bh[:, cols], bl[:, cols])
        out_ref[2 * n + odd] = part[:, :128]
        out_ref[2 * n + 1 - odd] = part[:, 128:]


def couple(at, gathered, own, other):
    return pl.pallas_call(
        couple_kernel,
        out_shape=shape(4, 256, 128),
        in_specs=[SMEM, HBM, VMEM, VMEM],
        out_specs=VMEM,
        scratch_shapes=[
            pltpu.VMEM((8, 256, 128), F32),
            pltpu.VMEM((256, 1024), BF16),
            pltpu.VMEM((256, 1024), BF16),
            pltpu.VMEM((1024, 512), BF16),
            pltpu.VMEM((1024, 512), BF16),
            DMA,
        ],
        compiler_params=NEAR,
        cost_estimate=pl.CostEstimate(flops=6 << 28, bytes_accessed=3 << 20, transcendentals=0),
    )(at, gathered, own, other)


def side_kernel(
    at_ref, su_hbm, lower_hbm, out_hbm, hi_hbm, lo_hbm, sigma, lower, ah, al, bh, bl, out, sems
):
    loads = [pltpu.make_async_copy(su_hbm.at[:, 0:256], sigma, sems.at[0])]
    for i in range(2):
        rows = slice(4 * i, 4 * (i + 1))
        loads.append(
            pltpu.make_async_copy(lower_hbm.at[:, rows], lower.at[:, rows], sems.at[1 + i])
        )
    for load in loads:
        load.start()
    _, _, core_at, _, x = device(at_ref)
    odd = x & 1
    loads[0].wait()
    for z in range(8):
        rows = slice(128 * z, 128 * (z + 1))
        ah[:, rows], al[:, rows] = split2(sigma[z ^ (4 * core_at)])
    for z in range(8):
        if z % 4 == 0:
            loads[1 + z // 4].wait()
        rows = slice(128 * z, 128 * (z + 1))
        for core in range(2):
            for t in range(2):
                cols = slice(256 * core + 128 * t, 256 * core + 128 * (t + 1))
                place = 128 * (odd if t == 0 else 1 - odd)
                value = lower[core, z, pl.ds(pl.multiple_of(place, 128), 128), :]
                bh[rows, cols], bl[rows, cols] = split2(value)
    stores = [
        pltpu.make_async_copy(bh, hi_hbm, sems.at[3]),
        pltpu.make_async_copy(bl, lo_hbm, sems.at[4]),
    ]
    for store in stores:
        store.start()
    for n in range(2):
        cols = slice(256 * n, 256 * (n + 1))
        part = -three_pass(ah[...], al[...], bh[:, cols], bl[:, cols])
        out[2 * n] = part[:, :128]
        out[2 * n + 1] = part[:, 128:]
        pair, place = slice(2 * n, 2 * n + 2), pl.ds(2 * (n ^ core_at), 2)
        stores.append(pltpu.make_async_copy(out.at[pair], out_hbm.at[place], sems.at[5 + n]))
        stores[-1].start()
    for store in stores:
        store.wait()


def side(at, gathered, lower):
    return pl.pallas_call(
        side_kernel,
        out_shape=(shape(12, 256, 128),) + (shape(1024, 512, dtype=BF16),) * 2,
        in_specs=[SMEM, HBM, HBM],
        out_specs=(HBM,) * 3,
        scratch_shapes=[
            pltpu.VMEM((8, 256, 128), F32),
            pltpu.VMEM((2, 8, 256, 128), F32),
            pltpu.VMEM((256, 1024), BF16),
            pltpu.VMEM((256, 1024), BF16),
            pltpu.VMEM((1024, 512), BF16),
            pltpu.VMEM((1024, 512), BF16),
            pltpu.VMEM((4, 256, 128), F32),
            DMA((7,)),
        ],
        compiler_params=WIDE,
        cost_estimate=pl.CostEstimate(flops=6 << 28, bytes_accessed=6 << 20, transcendentals=0),
    )(at, gathered, lower)


def last_kernel(
    at_ref, w, hi_hbm, lo_hbm, rest_hbm, out_hbm, ah, al, bh, bl, out, rest, sems
):
    loads = [
        pltpu.make_async_copy(hi_hbm, bh, sems.at[1]),
        pltpu.make_async_copy(lo_hbm, bl, sems.at[2]),
        pltpu.make_async_copy(rest_hbm.at[0:4], rest, sems.at[0]),
    ]
    for load in loads:
        load.start()
    core = device(at_ref)[2]
    for z in range(8):
        rows = slice(128 * z, 128 * (z + 1))
        ah[:, rows], al[:, rows] = split2(w[z ^ (4 * core)])
    for load in loads:
        load.wait()
    stores = [pltpu.make_async_copy(rest, out_hbm.at[:, 256:512], sems.at[5])]
    stores[0].start()
    for n in range(2):
        cols = slice(256 * n, 256 * (n + 1))
        part = three_pass(ah[...], al[...], bh[:, cols], bl[:, cols])
        out[2 * n] = part[:, :128]
        out[2 * n + 1] = part[:, 128:]
        pair, place = slice(2 * n, 2 * n + 2), pl.ds(2 * (n ^ core), 2)
        stores.append(pltpu.make_async_copy(out.at[pair], out_hbm.at[place, 0:256], sems.at[3 + n]))
        stores[-1].start()
    for store in stores:
        store.wait()


def last(at, w, hi, lo, rest):
    return pl.pallas_call(
        last_kernel,
        out_shape=shape(4, 512, 128),
        in_specs=[SMEM, VMEM] + [HBM] * 3,
        out_specs=HBM,
        scratch_shapes=[
            pltpu.VMEM((256, 1024), BF16),
            pltpu.VMEM((256, 1024), BF16),
            pltpu.VMEM((1024, 512), BF16),
            pltpu.VMEM((1024, 512), BF16),
            pltpu.VMEM((4, 256, 128), F32),
            pltpu.VMEM((4, 256, 128), F32),
            DMA((6,)),
        ],
        compiler_params=MIDDLE,
    )(at, w, hi, lo, rest)


def rotated(axis, size):
    axes = (axis, "c") if axis == "y" else ("c", axis)
    groups = [
        [2 * p + c if axis == "y" else size * c + p for p in (i ^ (size // 2 * c) for i in range(size))]
        for c in range(2)
    ]
    return axes, groups


def exchange(v, axis, size):
    axes, groups = rotated(axis, size)
    return lax.all_to_all(v, axes, 0, 0, tiled=True, axis_index_groups=groups)


def deal(v, t):
    moves = [(4 * c + x, 4 * (x >> 1) + 2 * c + ((x & 1) ^ t)) for c in range(2) for x in range(4)]
    return lax.ppermute(v, ("c", "x"), moves)


def turn(v, axis, size, k):
    return lax.ppermute(v, axis, [(i, (i + k) % size) for i in range(size)])


def shards(root_inverse, boundary_map, lower_factor, upper_factor, diagonal_inverse):
    at = lax.axis_index(("y", "c", "z", "x")).astype(jnp.int32).reshape(1)
    su, first, second = pick(at, boundary_map.reshape(32, 128), root_inverse, upper_factor)
    axes, groups = rotated("z", 8)
    gathered = lax.all_gather(su, axes, axis=0, tiled=False, axis_index_groups=groups)
    copies = fan(deal(first, 0), deal(second, 1))
    copies, lower = lax.optimization_barrier((copies, lower_factor))
    odd = lax.axis_index("x") & 1
    lower = [
        deal(lax.dynamic_slice_in_dim(lower, 128 * (odd ^ t), 128), t) for t in range(2)
    ]
    lower = jnp.concatenate(lower, axis=0)
    groups = [[2 * i + core for core in range(2) for i in range(8)]]
    lower = lax.all_gather(lower, ("y", "c"), axis=0, tiled=False, axis_index_groups=groups)
    lower = lower.reshape(2, 8, 256, 128)
    own = exchange(copies, "y", 8)
    other = turn(own, "c", 2, 1)
    part = couple(at, gathered, own, other)
    w = exchange(part, "x", 4).sum(axis=0)
    w_all = exchange(jnp.broadcast_to(w[None], (8, 256, 128)), "z", 8)
    rest, hi, lo = side(at, gathered, lower)
    sums = exchange(last(at, w_all, hi, lo, rest), "x", 4).sum(axis=0)
    return (sums[256:], -w, diagonal_inverse + sums[:256])


def solution(mesh):
    grid = Mesh(np.asarray(mesh.devices).reshape(8, 2, 8, 4), ("y", "c", "z", "x"))
    block = P(("y", "c"), ("z", "x"))
    return jax.shard_map(
        shards,
        mesh=grid,
        in_specs=(block, P(), block, block, block),
        out_specs=(block, block, block),
        check_vma=False,
    )
```

```python
import jax
import jax.numpy as jnp
import numpy as np
from jax import lax
from jax.experimental import pallas as pl
from jax.experimental.pallas import tpu as pltpu
from jax.sharding import Mesh, PartitionSpec as P

F32 = jnp.float32
BF16 = jnp.bfloat16
VMEM = pl.BlockSpec(memory_space=pltpu.VMEM)
SMEM = pl.BlockSpec(memory_space=pltpu.SMEM)
HBM = pl.BlockSpec(memory_space=pltpu.HBM)
PARAMS = pltpu.CompilerParams(vmem_limit_bytes=32 * 1024 * 1024)
WIDE = pltpu.CompilerParams(vmem_limit_bytes=62 * 1024 * 1024)
NEAR = pltpu.CompilerParams(vmem_limit_bytes=51 * 1024 * 1024)
MIDDLE = pltpu.CompilerParams(vmem_limit_bytes=51 * 1024 * 1024)
DMA = pltpu.SemaphoreType.DMA


def shape(*dims, dtype=F32):
    return jax.ShapeDtypeStruct(dims, dtype)


def split2(v):
    hi = v.astype(BF16)
    return hi, (v - hi.astype(F32)).astype(BF16)


def dot(a, b):
    return lax.dot_general(a, b, (((1,), (0,)), ((), ())), preferred_element_type=F32)


def three_pass(ah, al, bh, bl):
    return dot(ah, bh) + (dot(ah, bl) + dot(al, bh))


def device(ref):
    number = ref[0]
    return number >> 5, number & 31, (number >> 5) & 1, (number >> 2) & 7, number & 3


def pick_kernel(
    at_ref, map_hbm, root_hbm, upper_hbm, su_ref, first_ref, second_ref, picks, root, sems
):
    loads = [
        pltpu.make_async_copy(map_hbm, picks, sems.at[0]),
        pltpu.make_async_copy(root_hbm, root, sems.at[1]),
        pltpu.make_async_copy(upper_hbm, su_ref.at[256:512], sems.at[2]),
    ]
    for load in loads:
        load.start()
    row, col, _, _, x = device(at_ref)
    odd = x & 1
    iota = lax.broadcasted_iota(jnp.int32, (256, 128), 0)
    loads[0].wait()
    cols = picks[pl.ds(col, 1), :] - 256 * col
    col_hot = jnp.where(cols == iota, 1.0, 0.0).astype(BF16)
    hots = []
    for part in range(2):
        block = 2 * row + part
        rows = picks[pl.ds(block, 1), :] - 256 * block
        hots.append(jnp.where(rows == iota, 1.0, 0.0).astype(BF16))
    loads[1].wait()
    stack = []
    for part in range(2):
        left = root[256 * part : 256 * (part + 1), :]
        pieces = []
        for _ in range(3):
            piece = left.astype(BF16)
            left = left - piece.astype(F32)
            pieces.append(piece)
        across = lax.dot_general(
            hots[part],
            jnp.concatenate(pieces, axis=1),
            (((0,), (0,)), ((), ())),
            preferred_element_type=F32,
        ).astype(BF16)
        stack += [across[:, 256 * i : 256 * (i + 1)] for i in range(3)]
    value = dot(jnp.concatenate(stack, axis=0), col_hot)
    for part in range(2):
        v = [value[128 * (3 * part + i) : 128 * (3 * part + i + 1), :] for i in range(3)]
        su_ref[128 * part : 128 * (part + 1), :] = (v[0] + v[1]) + v[2]
    loads[2].wait()
    near = pl.multiple_of(128 * odd, 128)
    far = pl.multiple_of(128 - 128 * odd, 128)
    first_ref[...] = su_ref[pl.ds(near, 128), :]
    second_ref[...] = su_ref[pl.ds(far, 128), :]


def pick(at, blocks, root, upper):
    return pl.pallas_call(
        pick_kernel,
        out_shape=(shape(512, 128), shape(128, 128), shape(128, 128)),
        in_specs=[SMEM] + [HBM] * 3,
        out_specs=(VMEM, VMEM, VMEM),
        scratch_shapes=[
            pltpu.VMEM((32, 128), jnp.int32),
            pltpu.VMEM((512, 256), F32),
            DMA((3,)),
        ],
        compiler_params=WIDE,
    )(at, blocks, root, upper)


def fan_kernel(first_ref, second_ref, copies_ref):
    for t, ref in enumerate((first_ref, second_ref)):
        value = ref[...]
        for i in range(8):
            copies_ref[i, t] = value


def fan(first, second):
    return pl.pallas_call(
        fan_kernel,
        out_shape=shape(8, 2, 128, 128),
        in_specs=[VMEM] * 2,
        out_specs=VMEM,
        compiler_params=PARAMS,
    )(first, second)


def couple_kernel(
    at_ref, gathered_hbm, own, other, out_ref, left, ah, al, bh, bl, sem
):
    load = pltpu.make_async_copy(gathered_hbm.at[:, 256:512], left, sem)
    load.start()
    _, _, core, _, x = device(at_ref)
    odd = x & 1
    for n, right in enumerate((own, other)):
        side = core if n == 0 else 1 - core
        for z in range(8):
            rows = slice(128 * z, 128 * (z + 1))
            for t in range(2):
                cols = slice(256 * n + 128 * t, 256 * n + 128 * (t + 1))
                bh[rows, cols], bl[rows, cols] = split2(right[z ^ (4 * side), t])
    load.wait()
    for z in range(8):
        rows = slice(128 * z, 128 * (z + 1))
        ah[:, rows], al[:, rows] = split2(left[z ^ (4 * core)])
    for n in range(2):
        cols = slice(256 * n, 256 * (n + 1))
        part = three_pass(ah[...], al[...], bh[:, cols], bl[:, cols])
        out_ref[2 * n + odd] = part[:, :128]
        out_ref[2 * n + 1 - odd] = part[:, 128:]


def couple(at, gathered, own, other):
    return pl.pallas_call(
        couple_kernel,
        out_shape=shape(4, 256, 128),
        in_specs=[SMEM, HBM, VMEM, VMEM],
        out_specs=VMEM,
        scratch_shapes=[
            pltpu.VMEM((8, 256, 128), F32),
            pltpu.VMEM((256, 1024), BF16),
            pltpu.VMEM((256, 1024), BF16),
            pltpu.VMEM((1024, 512), BF16),
            pltpu.VMEM((1024, 512), BF16),
            DMA,
        ],
        compiler_params=NEAR,
        cost_estimate=pl.CostEstimate(flops=6 << 28, bytes_accessed=3 << 20, transcendentals=0),
    )(at, gathered, own, other)


def side_kernel(
    at_ref, su_hbm, lower_hbm, out_hbm, hi_hbm, lo_hbm, sigma, lower, ah, al, bh, bl, out, sems
):
    loads = [pltpu.make_async_copy(su_hbm.at[:, 0:256], sigma, sems.at[0])]
    for i in range(2):
        rows = slice(4 * i, 4 * (i + 1))
        loads.append(
            pltpu.make_async_copy(lower_hbm.at[:, rows], lower.at[:, rows], sems.at[1 + i])
        )
    for load in loads:
        load.start()
    _, _, core_at, _, x = device(at_ref)
    odd = x & 1
    loads[0].wait()
    for z in range(8):
        rows = slice(128 * z, 128 * (z + 1))
        ah[:, rows], al[:, rows] = split2(sigma[z ^ (4 * core_at)])
    for z in range(8):
        if z % 4 == 0:
            loads[1 + z // 4].wait()
        rows = slice(128 * z, 128 * (z + 1))
        for core in range(2):
            for t in range(2):
                cols = slice(256 * core + 128 * t, 256 * core + 128 * (t + 1))
                place = 128 * (odd if t == 0 else 1 - odd)
                value = lower[core, z, pl.ds(pl.multiple_of(place, 128), 128), :]
                bh[rows, cols], bl[rows, cols] = split2(value)
    stores = [
        pltpu.make_async_copy(bh, hi_hbm, sems.at[3]),
        pltpu.make_async_copy(bl, lo_hbm, sems.at[4]),
    ]
    for store in stores:
        store.start()
    for n in range(2):
        cols = slice(256 * n, 256 * (n + 1))
        part = -three_pass(ah[...], al[...], bh[:, cols], bl[:, cols])
        out[2 * n] = part[:, :128]
        out[2 * n + 1] = part[:, 128:]
        pair, place = slice(2 * n, 2 * n + 2), pl.ds(2 * (n ^ core_at), 2)
        stores.append(pltpu.make_async_copy(out.at[pair], out_hbm.at[place], sems.at[5 + n]))
        stores[-1].start()
    for store in stores:
        store.wait()


def side(at, gathered, lower):
    return pl.pallas_call(
        side_kernel,
        out_shape=(shape(12, 256, 128),) + (shape(1024, 512, dtype=BF16),) * 2,
        in_specs=[SMEM, HBM, HBM],
        out_specs=(HBM,) * 3,
        scratch_shapes=[
            pltpu.VMEM((8, 256, 128), F32),
            pltpu.VMEM((2, 8, 256, 128), F32),
            pltpu.VMEM((256, 1024), BF16),
            pltpu.VMEM((256, 1024), BF16),
            pltpu.VMEM((1024, 512), BF16),
            pltpu.VMEM((1024, 512), BF16),
            pltpu.VMEM((4, 256, 128), F32),
            DMA((7,)),
        ],
        compiler_params=WIDE,
        cost_estimate=pl.CostEstimate(flops=6 << 28, bytes_accessed=6 << 20, transcendentals=0),
    )(at, gathered, lower)


def last_kernel(
    at_ref, w, hi_hbm, lo_hbm, rest_hbm, out_hbm, ah, al, bh, bl, out, rest, sems
):
    loads = [
        pltpu.make_async_copy(hi_hbm, bh, sems.at[1]),
        pltpu.make_async_copy(lo_hbm, bl, sems.at[2]),
        pltpu.make_async_copy(rest_hbm.at[0:4], rest, sems.at[0]),
    ]
    for load in loads:
        load.start()
    core = device(at_ref)[2]
    for z in range(8):
        rows = slice(128 * z, 128 * (z + 1))
        ah[:, rows], al[:, rows] = split2(w[z ^ (4 * core)])
    for load in loads[:2]:
        load.wait()
    stores = []
    for n in range(2):
        cols = slice(256 * n, 256 * (n + 1))
        part = three_pass(ah[...], al[...], bh[:, cols], bl[:, cols])
        out[2 * n] = part[:, :128]
        out[2 * n + 1] = part[:, 128:]
        pair, place = slice(2 * n, 2 * n + 2), pl.ds(2 * (n ^ core), 2)
        stores.append(pltpu.make_async_copy(out.at[pair], out_hbm.at[place, 0:256], sems.at[3 + n]))
        stores[-1].start()
        if n == 0:
            loads[2].wait()
            stores.append(pltpu.make_async_copy(rest, out_hbm.at[:, 256:512], sems.at[5]))
            stores[-1].start()
    for store in stores:
        store.wait()


def last(at, w, hi, lo, rest):
    return pl.pallas_call(
        last_kernel,
        out_shape=shape(4, 512, 128),
        in_specs=[SMEM, VMEM] + [HBM] * 3,
        out_specs=HBM,
        scratch_shapes=[
            pltpu.VMEM((256, 1024), BF16),
            pltpu.VMEM((256, 1024), BF16),
            pltpu.VMEM((1024, 512), BF16),
            pltpu.VMEM((1024, 512), BF16),
            pltpu.VMEM((4, 256, 128), F32),
            pltpu.VMEM((4, 256, 128), F32),
            DMA((6,)),
        ],
        compiler_params=MIDDLE,
    )(at, w, hi, lo, rest)


def rotated(axis, size):
    axes = (axis, "c") if axis == "y" else ("c", axis)
    groups = [
        [2 * p + c if axis == "y" else size * c + p for p in (i ^ (size // 2 * c) for i in range(size))]
        for c in range(2)
    ]
    return axes, groups


def exchange(v, axis, size):
    axes, groups = rotated(axis, size)
    return lax.all_to_all(v, axes, 0, 0, tiled=True, axis_index_groups=groups)


def deal(v, t):
    moves = [(4 * c + x, 4 * (x >> 1) + 2 * c + ((x & 1) ^ t)) for c in range(2) for x in range(4)]
    return lax.ppermute(v, ("c", "x"), moves)


def turn(v, axis, size, k):
    return lax.ppermute(v, axis, [(i, (i + k) % size) for i in range(size)])


def shards(root_inverse, boundary_map, lower_factor, upper_factor, diagonal_inverse):
    at = lax.axis_index(("y", "c", "z", "x")).astype(jnp.int32).reshape(1)
    su, first, second = pick(at, boundary_map.reshape(32, 128), root_inverse, upper_factor)
    axes, groups = rotated("z", 8)
    gathered = lax.all_gather(su, axes, axis=0, tiled=False, axis_index_groups=groups)
    copies = fan(deal(first, 0), deal(second, 1))
    copies, lower = lax.optimization_barrier((copies, lower_factor))
    odd = lax.axis_index("x") & 1
    lower = [
        deal(lax.dynamic_slice_in_dim(lower, 128 * (odd ^ t), 128), t) for t in range(2)
    ]
    lower = jnp.concatenate(lower, axis=0)
    groups = [[2 * i + core for core in range(2) for i in range(8)]]
    lower = lax.all_gather(lower, ("y", "c"), axis=0, tiled=False, axis_index_groups=groups)
    lower = lower.reshape(2, 8, 256, 128)
    own = exchange(copies, "y", 8)
    other = turn(own, "c", 2, 1)
    part = couple(at, gathered, own, other)
    w = exchange(part, "x", 4).sum(axis=0)
    w_all = exchange(jnp.broadcast_to(w[None], (8, 256, 128)), "z", 8)
    rest, hi, lo = side(at, gathered, lower)
    sums = exchange(last(at, w_all, hi, lo, rest), "x", 4).sum(axis=0)
    return (sums[256:], -w, diagonal_inverse + sums[:256])


def solution(mesh):
    grid = Mesh(np.asarray(mesh.devices).reshape(8, 2, 8, 4), ("y", "c", "z", "x"))
    block = P(("y", "c"), ("z", "x"))
    return jax.shard_map(
        shards,
        mesh=grid,
        in_specs=(block, P(), block, block, block),
        out_specs=(block, block, block),
        check_vma=False,
    )
```
